32 devices in a mesh: tp: 2 (over x), dp: 16 (over z, y, core).
Axes of the slice: x: 2, y: 2, z: 4, core: 2. Of those that a mesh axis runs over, the one named last changes fastest.
Arguments:
- tokens: bfloat16 [8192, 768], P('dp'), may hold values from -6 to 6
- latents: bfloat16 [256, 768], P('dp'), may hold values from -6 to 6
- latent_query: bfloat16 [768, 768], P(None, 'tp'), may hold values from -0.21875 to 0.21875
- latent_key: bfloat16 [768, 768], P(None, 'tp'), may hold values from -0.21875 to 0.21875
- latent_value: bfloat16 [768, 768], P(None, 'tp'), may hold values from -0.21875 to 0.21875
- latent_output: bfloat16 [768, 768], P('tp'), may hold values from -1.75 to 1.75
- query_weight: bfloat16 [768, 768], P(None, 'tp'), may hold values from -0.21875 to 0.21875
- key_weight: bfloat16 [768, 768], P(None, 'tp'), may hold values from -0.21875 to 0.21875
- value_weight: bfloat16 [768, 768], P(None, 'tp'), may hold values from -0.21875 to 0.21875
- output_weight: bfloat16 [768, 768], P('tp'), may hold values from -1.75 to 1.75
- up_weight: bfloat16 [768, 3072], P(None, 'tp'), may hold values from -0.21875 to 0.21875
- up_bias: float32 [3072], P('tp'), may hold values from -3 to 3
- down_weight: bfloat16 [3072, 768], P('tp'), may hold values from -0.109375 to 0.109375
- down_bias: float32 [768], replicated, may hold values from -3 to 3
- latent_gain: float32 [768], replicated, may hold values from 0.1 to 1.9
- attention_gain: float32 [768], replicated, may hold values from 0.1 to 1.9
- feed_gain: float32 [768], replicated, may hold values from 0.1 to 1.9
- group_image: int32 [32], replicated, may hold values from 0 to 10, as said below
- token_cotangent: bfloat16 [8192, 768], P('dp'), may hold values from -6 to 6
- latent_cotangent: bfloat16 [256, 768], P('dp'), may hold values from -6 to 6
Outputs:
- mixed_tokens: bfloat16 [8192, 768], P('dp')
- mixed_latents: bfloat16 [256, 768], P('dp')
- token_grad: float32 [8192, 768], P('dp')
- latent_grad: float32 [256, 768], P('dp')
- latent_query_grad: float32 [768, 768], P('dp', 'tp')
- latent_key_grad: float32 [768, 768], P('dp', 'tp')
- latent_value_grad: float32 [768, 768], P('dp', 'tp')
- latent_output_grad: float32 [768, 768], P('tp', 'dp')
- query_weight_grad: float32 [768, 768], P('dp', 'tp')
- key_weight_grad: float32 [768, 768], P('dp', 'tp')
- value_weight_grad: float32 [768, 768], P('dp', 'tp')
- output_weight_grad: float32 [768, 768], P('tp', 'dp')
- up_weight_grad: float32 [768, 3072], P('dp', 'tp')
- up_bias_grad: float32 [3072], P(('tp', 'dp'))
- down_weight_grad: float32 [3072, 768], P('tp', 'dp')
- down_bias_grad: float32 [768], P('dp')
- latent_gain_grad: float32 [768], P('dp')
- attention_gain_grad: float32 [768], P('dp')
- feed_gain_grad: float32 [768], P('dp')
The draws below stay inside these ranges and needn't reach their ends.
Inputs may be any that keep to these rules, and one draw needn't show every extreme that they name: group_image[g] names the image of group g; each image has at least 1 group.
All inputs are finite; a program needn't handle non-finite values.
Results may differ from the reference program's by a relative error of at most 0.02.
Values may be sent and summed in bfloat16 or wider, within the bound.
No kernel may reach another device: no remote copies, remote signals or barrier semaphores. Data moves between devices by JAX's collectives and lax.ppermute only.
A program may use at most 128 MiB of HBM per device.

```python
from functools import partial
import jax
import jax.numpy as jnp
from jax import lax

D = 768
H = 12
E = 64
F = 3072
S = 256
L = 8
GROUPS = 32
TOKENS = 8192
LATENTS = 256


def draw_group_image(key, part):
    key = jax.random.fold_in(key, 7)
    first, second, third = jax.random.split(key, 3)
    others = jnp.concatenate([jnp.full((GROUPS // 8,), 1, jnp.int32), jnp.full((GROUPS // 8,), 2, jnp.int32), jnp.repeat(jnp.arange(3, 11, dtype=jnp.int32), GROUPS // 32)])
    shuffled = jax.random.permutation(first, others)
    parity = jax.random.randint(second, (), 0, 2)
    position = jnp.arange(GROUPS, dtype=jnp.int32)
    labels = jnp.where(position % 2 == parity, 0, shuffled[position // 2])
    relabel = jax.random.permutation(third, jnp.arange(11, dtype=jnp.int32))
    return relabel[labels].astype(jnp.int32)


def level_of(stream_key, shape, pieces, least, largest):
    level = 1.0
    for dim, parts in pieces:
        heights = jax.random.uniform(jax.random.fold_in(jax.random.fold_in(stream_key, 6), dim), (parts,), jnp.float32, least / len(pieces), largest / len(pieces))
        level = level * jnp.repeat(jnp.exp(heights), shape[dim] // parts).reshape((-1,) + (1,) * (len(shape) - 1 - dim))
    return level


def gaussian(own_key, extent, width, reach, cuts=(), kind=jnp.bfloat16):
    level = level_of(own_key, extent, cuts, -0.22, 0.18) if cuts else 1.0
    entries = jax.random.normal(own_key, extent, jnp.float32) * width * level
    return jnp.minimum(jnp.maximum(entries, -reach), reach).astype(kind)


def setup_inputs(seed: int = 0) -> dict:
    streams_of = jax.random.split(jax.random.key(seed), 21)
    return {
        "tokens": gaussian(streams_of[0], (TOKENS, D), 1.0, 6.0, ((0, 16),)),
        "latents": gaussian(streams_of[1], (LATENTS, D), 1.0, 6.0, ((0, 16),)),
        "latent_query": gaussian(streams_of[2], (D, D), D ** -0.5, 0.21875, ((1, 2),)),
        "latent_key": gaussian(streams_of[3], (D, D), D ** -0.5, 0.21875, ((1, 2),)),
        "latent_value": gaussian(streams_of[4], (D, D), D ** -0.5, 0.21875, ((1, 2),)),
        "latent_output": gaussian(streams_of[5], (D, D), (D // 64) ** -0.5, 1.75, ((0, 2),)),
        "query_weight": gaussian(streams_of[6], (D, D), D ** -0.5, 0.21875, ((1, 2),)),
        "key_weight": gaussian(streams_of[7], (D, D), D ** -0.5, 0.21875, ((1, 2),)),
        "value_weight": gaussian(streams_of[8], (D, D), D ** -0.5, 0.21875, ((1, 2),)),
        "output_weight": gaussian(streams_of[9], (D, D), (D // 64) ** -0.5, 1.75, ((0, 2),)),
        "up_weight": gaussian(streams_of[10], (D, F), D ** -0.5, 0.21875, ((1, 2),)),
        "up_bias": gaussian(streams_of[11], (F,), 0.5, 3.0, ((0, 2),), jnp.float32),
        "down_weight": gaussian(streams_of[12], (F, D), F ** -0.5, 0.109375, ((0, 2),)),
        "down_bias": gaussian(streams_of[13], (D,), 0.5, 3.0, (), jnp.float32),
        "latent_gain": jnp.clip(1.0 + 0.18 * jax.random.normal(streams_of[14], (D,), jnp.float32), 0.1, 1.9),
        "attention_gain": jnp.clip(1.0 + 0.18 * jax.random.normal(streams_of[15], (D,), jnp.float32), 0.1, 1.9),
        "feed_gain": jnp.clip(1.0 + 0.18 * jax.random.normal(streams_of[16], (D,), jnp.float32), 0.1, 1.9),
        "group_image": draw_group_image(jax.random.fold_in(streams_of[20], 71), 0),
        "token_cotangent": gaussian(streams_of[18], (TOKENS, D), 1.0, 6.0, ((0, 16),)),
        "latent_cotangent": gaussian(streams_of[19], (LATENTS, D), 1.0, 6.0, ((0, 16),)),
    }


@jax.custom_vjp
def low(v):
    return lax.optimization_barrier(v.astype(jnp.bfloat16)).astype(jnp.float32)

@jax.custom_vjp
def low_back(v):
    return v

def low_keep(v):
    return (low(v), None)

def low_pass(kept, grad):
    return (grad,)

def back_keep(v):
    return (v, None)

def back_low(kept, grad):
    return (low(grad),)
low.defvjp(low_keep, low_pass)
low_back.defvjp(back_keep, back_low)
EPSILON = 1e-05
NEGATIVE = -1000000000.0

def layer_norm(values, gain):
    average = lax.optimization_barrier(jnp.mean(values, axis=-1, keepdims=True))
    centred = values - average
    spread = lax.optimization_barrier(jnp.mean(centred * centred, axis=-1, keepdims=True))
    return centred * lax.rsqrt(spread + EPSILON) * gain

def gelu_tanh(values):
    return 0.5 * values * (1.0 + jnp.tanh(0.7978845608028654 * (values + 0.044715 * values * values * values)))

def matmul(left, right):
    return jnp.dot(left, right, precision=lax.Precision.HIGHEST)

def latent_attention(latents, gain, wquery, wkey, wvalue, woutput, member):
    normed = low(layer_norm(latents, gain))
    queries = low(low_back(matmul(normed, wquery))).reshape(-1, H, E)
    keyset = low(low_back(matmul(normed, wkey))).reshape(-1, H, E)
    valueset = low(low_back(matmul(normed, wvalue))).reshape(-1, H, E)
    scores = low_back(jnp.einsum('qhe,khe->hqk', queries, keyset, precision=lax.Precision.HIGHEST) * E ** (-0.5))
    scores = jnp.where(member[None], scores, NEGATIVE)
    probs = low(jax.nn.softmax(scores, axis=-1))
    mixed = jnp.einsum('hqk,khe->qhe', probs, valueset, precision=lax.Precision.HIGHEST).reshape(-1, H * E)
    mixed = low(low_back(mixed))
    return latents + low_back(matmul(mixed, woutput))

def group_attention(weights, pair):
    wquery, wkey, wvalue = weights
    normed_tokens, normed_latents = pair
    queries = low(low_back(matmul(normed_tokens, wquery))).reshape(S, H, E)
    sources = jnp.concatenate([normed_tokens, normed_latents], axis=0)
    keyset = low(low_back(matmul(sources, wkey))).reshape(S + L, H, E)
    valueset = low(low_back(matmul(sources, wvalue))).reshape(S + L, H, E)
    scores = low_back(jnp.einsum('qhe,khe->hqk', queries, keyset, precision=lax.Precision.HIGHEST) * E ** (-0.5))
    probs = low(jax.nn.softmax(scores, axis=-1))
    mixed = jnp.einsum('hqk,khe->qhe', probs, valueset, precision=lax.Precision.HIGHEST).reshape(S, H * E)
    return low(low_back(mixed))

def forward(member, tokens, latents, lquery, lkey, lvalue, loutput, wquery, wkey, wvalue, woutput, wup, bup, wdown, bdown, glatent, gattention, gfeed):
    latents_mid = latent_attention(latents, glatent, lquery, lkey, lvalue, loutput, member)
    normed_tokens = low(layer_norm(tokens, gattention)).reshape(GROUPS, S, D)
    normed_latents = low(layer_norm(latents_mid, gattention)).reshape(GROUPS, L, D)
    mixed = lax.map(jax.checkpoint(partial(group_attention, (wquery, wkey, wvalue))), (normed_tokens, normed_latents))
    middle = tokens + low_back(matmul(mixed.reshape(TOKENS, D), woutput))
    normed = low(layer_norm(middle, gfeed))
    hidden = low_back(matmul(normed, wup) + bup)
    active = low(gelu_tanh(hidden))
    result = middle + low_back(matmul(active, wdown)) + bdown
    return (result, latents_mid)

def reference(tokens, latents, latent_query, latent_key, latent_value, latent_output, query_weight, key_weight, value_weight, output_weight, up_weight, up_bias, down_weight, down_bias, latent_gain, attention_gain, feed_gain, group_image, token_cotangent, latent_cotangent):
    images = jnp.repeat(group_image, L)
    member = images[:, None] == images[None, :]
    floats = [element.astype(jnp.float32) for element in (tokens, latents, latent_query, latent_key, latent_value, latent_output, query_weight, key_weight, value_weight, output_weight, up_weight, up_bias, down_weight, down_bias, latent_gain, attention_gain, feed_gain)]
    outputs, pullback = jax.vjp(partial(forward, member), *floats)
    grads = pullback((token_cotangent.astype(jnp.float32), latent_cotangent.astype(jnp.float32)))
    return (outputs[0].astype(jnp.bfloat16), outputs[1].astype(jnp.bfloat16), grads[0], grads[1], grads[2], grads[3], grads[4], grads[5], grads[6], grads[7], grads[8], grads[9], grads[10], grads[11], grads[12], grads[13], grads[14], grads[15], grads[16])
```

```python
from functools import partial

import jax
import jax.numpy as jnp
from jax import lax
from jax.sharding import PartitionSpec as P

E = 64
S = 256
L = 8


EPSILON = 1e-05
NEGATIVE = -1000000000.0


def product(left, right):
    return jnp.dot(left, right, preferred_element_type=jnp.float32)


def inner_left(left, right):
    return lax.dot_general(
        left, right, (((0,), (0,)), ((), ())), preferred_element_type=jnp.float32
    )


def inner_right(left, right):
    return lax.dot_general(
        left, right, (((1,), (1,)), ((), ())), preferred_element_type=jnp.float32
    )


def norm_parts(values):
    average = jnp.mean(values, axis=-1, keepdims=True)
    centred = values - average
    spread = jnp.mean(centred * centred, axis=-1, keepdims=True)
    rate = lax.rsqrt(spread + EPSILON)
    return centred * rate, rate


def norm_back(grad, unit, rate, gain):
    scaled = grad * gain
    first = jnp.mean(scaled, axis=-1, keepdims=True)
    second = jnp.mean(scaled * unit, axis=-1, keepdims=True)
    return rate * (scaled - first - unit * second)


def gelu_both(values):
    inner = 0.7978845608028654 * (values + 0.044715 * values * values * values)
    wave = jnp.tanh(inner)
    slope = 0.7978845608028654 * (1.0 + 0.134145 * values * values)
    return (
        0.5 * values * (1.0 + wave),
        0.5 * (1.0 + wave) + 0.5 * values * (1.0 - wave * wave) * slope,
    )


def swap_tp(values):
    return lax.ppermute(values, "tp", [(0, 1), (1, 0)])


def flip(values, bits):
    size = lax.axis_size("dp")
    return lax.ppermute(values, "dp", [(i, i ^ bits) for i in range(size)])


def tp_sum(part):
    low = part.astype(jnp.bfloat16)
    return low.astype(jnp.float32) + swap_tp(low).astype(jnp.float32)


def gather_relative(own):
    size = lax.axis_size("dp")
    held, width = own, 1
    while width * 4 < size:
        held = jnp.concatenate([held, flip(held, width)], axis=0)
        width *= 2
    parts = [held] + [flip(held, width * k) for k in range(1, size // width)]
    return jnp.concatenate(parts, axis=0)


def scatter_sum(grads):
    size = lax.axis_size("dp")
    me = lax.axis_index("dp")
    width = 1
    while width * 4 < size:
        bit = (me // width) % 2
        pairs = grads.reshape((grads.shape[0] // 2, 2) + grads.shape[1:])
        send = lax.dynamic_index_in_dim(pairs, 1 - bit, 1, keepdims=False)
        keep = lax.dynamic_index_in_dim(pairs, bit, 1, keepdims=False)
        got = flip(send.astype(jnp.bfloat16), width)
        grads = keep + got.astype(jnp.float32)
        width *= 2
    place = me // width
    total = lax.dynamic_index_in_dim(grads, place, 0, keepdims=False)
    for k in range(1, size // width):
        send = lax.dynamic_index_in_dim(grads, place ^ k, 0, keepdims=False)
        total = total + flip(send.astype(jnp.bfloat16), width * k).astype(jnp.float32)
    return total


def heads_product(pattern, left, right):
    return jnp.einsum(pattern, left, right, preferred_element_type=jnp.float32)


def latent_probs_of(queries, keys, member, factor):
    scores = heads_product("qhe,khe->hqk", queries, keys) * factor
    scores = jnp.where(member[None], scores, NEGATIVE)
    return jax.nn.softmax(scores, axis=-1)


def local(
    tokens,
    latents,
    latent_query,
    latent_key,
    latent_value,
    latent_output,
    query_weight,
    key_weight,
    value_weight,
    output_weight,
    up_weight,
    up_bias,
    down_weight,
    down_bias,
    latent_gain,
    attention_gain,
    feed_gain,
    group_image,
    token_cotangent,
    latent_cotangent,
):
    f32, b16 = jnp.float32, jnp.bfloat16
    factor = E ** (-0.5)
    size = lax.axis_size("dp")
    me = lax.axis_index("dp")
    width = latent_query.shape[1]
    heads = width // E
    model = tokens.shape[1]
    rows = tokens.shape[0]
    groups = rows // S
    own = latents.shape[0]
    everyone = own * size
    latents_all = gather_relative(latents)
    order = jnp.bitwise_xor(jnp.arange(size, dtype=jnp.int32), me)
    images = jnp.repeat(group_image.reshape(size, groups)[order].reshape(-1), L)
    latent_unit, latent_rate = norm_parts(latents_all.astype(f32))
    latent_low = (latent_unit * latent_gain).astype(b16)
    lat_q = product(latent_low, latent_query).astype(b16).reshape(everyone, heads, E)
    lat_k = product(latent_low, latent_key).astype(b16).reshape(everyone, heads, E)
    lat_v = product(latent_low, latent_value).astype(b16).reshape(everyone, heads, E)
    own_probs = latent_probs_of(lat_q[:own], lat_k, images[:own, None] == images[None, :], factor)
    own_mixed = (
        heads_product("hqk,khe->qhe", own_probs.astype(b16), lat_v).reshape(own, width).astype(b16)
    )
    latents_mid = latents.astype(f32) + tp_sum(product(own_mixed, latent_output))
    token_unit, token_rate = norm_parts(tokens.astype(f32))
    token_low = (token_unit * attention_gain).astype(b16)
    side_unit, side_rate = norm_parts(latents_mid)
    side_low = (side_unit * attention_gain).astype(b16)
    queries = product(token_low, query_weight).astype(b16).reshape(groups, S, heads, E)
    token_keys = product(token_low, key_weight).astype(b16).reshape(groups, S, heads, E)
    token_values = product(token_low, value_weight).astype(b16).reshape(groups, S, heads, E)
    side_keys = product(side_low, key_weight).astype(b16).reshape(groups, L, heads, E)
    side_values = product(side_low, value_weight).astype(b16).reshape(groups, L, heads, E)
    keyset = jnp.concatenate([token_keys, side_keys], axis=1)
    valueset = jnp.concatenate([token_values, side_values], axis=1)
    scores = heads_product("gqhe,gkhe->ghqk", queries, keyset) * factor
    probs = jax.nn.softmax(scores, axis=-1)
    probs_low = probs.astype(b16)
    mixed = heads_product("ghqk,gkhe->gqhe", probs_low, valueset).reshape(rows, width).astype(b16)
    middle = tokens.astype(f32) + tp_sum(product(mixed, output_weight))
    feed_unit, feed_rate = norm_parts(middle)
    feed_low = (feed_unit * feed_gain).astype(b16)
    hidden = product(feed_low, up_weight) + up_bias
    active, slope = gelu_both(hidden)
    active_low = active.astype(b16)
    active_grad = inner_right(token_cotangent, down_weight)
    hidden_grad = (slope * active_grad).astype(b16)
    feed_input_grad = tp_sum(inner_right(hidden_grad, up_weight))
    result = middle + tp_sum(product(active_low, down_weight)) + down_bias
    mixed_tokens = result.astype(b16)
    outer_grad = token_cotangent.astype(f32)
    up_grad = inner_left(feed_low, hidden_grad)
    down_grad = inner_left(token_cotangent, active_low)
    middle_grad = outer_grad + norm_back(feed_input_grad, feed_unit, feed_rate, feed_gain)
    feed_gain_grad = jnp.sum(feed_input_grad * feed_unit, axis=0)
    middle_low = middle_grad.astype(b16)
    output_grad = inner_left(middle_low, mixed)
    mixed_grad = (
        inner_right(middle_low, output_weight).astype(b16).reshape(groups, S, heads, E)
    )
    prob_grad = heads_product("gqhe,gkhe->ghqk", mixed_grad, valueset)
    value_grad = heads_product("ghqk,gqhe->gkhe", probs_low, mixed_grad).astype(b16)
    delta = jnp.sum(prob_grad * probs, axis=-1, keepdims=True)
    score_grad = (probs * (prob_grad - delta)).astype(b16)
    query_grad = (heads_product("ghqk,gkhe->gqhe", score_grad, keyset) * factor).astype(b16)
    query_grad = query_grad.reshape(rows, width)
    key_grad = (heads_product("ghqk,gqhe->gkhe", score_grad, queries) * factor).astype(b16)
    token_key_grad = key_grad[:, :S].reshape(rows, width)
    side_key_grad = key_grad[:, S:].reshape(groups * L, width)
    token_value_grad = value_grad[:, :S].reshape(rows, width)
    side_value_grad = value_grad[:, S:].reshape(groups * L, width)
    side_part = tp_sum(
        inner_right(side_key_grad, key_weight) + inner_right(side_value_grad, value_weight)
    )
    middle_latent_grad = latent_cotangent.astype(f32) + norm_back(
        side_part, side_unit, side_rate, attention_gain
    )
    mid_low = gather_relative(middle_latent_grad.astype(b16))
    latent_mixed_grad = inner_right(mid_low, latent_output).astype(b16)
    latent_mixed_grad = latent_mixed_grad.reshape(everyone, heads, E)
    block = min(everyone, 256)
    member = images[:, None] == images[None, :]

    def latent_rows(start):
        cut = partial(lax.dynamic_slice_in_dim, start_index=start, slice_size=block, axis=0)
        part_queries, part_grad = cut(lat_q), cut(latent_mixed_grad)
        part_probs = latent_probs_of(part_queries, lat_k, cut(member), factor)
        part_low = part_probs.astype(b16)
        part_mixed = heads_product("hqk,khe->qhe", part_low, lat_v)
        prob_grad = heads_product("qhe,khe->hqk", part_grad, lat_v)
        delta = jnp.sum(prob_grad * part_probs, axis=-1, keepdims=True)
        score_grad = (part_probs * (prob_grad - delta)).astype(b16)
        part_query_grad = heads_product("hqk,khe->qhe", score_grad, lat_k) * factor
        part_key_grad = heads_product("hqk,qhe->khe", score_grad, part_queries) * factor
        part_value_grad = heads_product("hqk,qhe->khe", part_low, part_grad)
        return part_mixed, part_query_grad, part_key_grad, part_value_grad

    if block == everyone:
        lat_mixed, lat_q_grad, lat_k_grad, lat_v_grad = latent_rows(0)
    else:

        def step(held, start):
            part_mixed, part_query_grad, part_key_grad, part_value_grad = latent_rows(start)
            held = (held[0] + part_key_grad, held[1] + part_value_grad)
            return held, (part_mixed, part_query_grad)

        zero = jnp.zeros((everyone, heads, E), f32)
        (lat_k_grad, lat_v_grad), (lat_mixed, lat_q_grad) = lax.scan(
            step, (zero, zero), jnp.arange(0, everyone, block)
        )
    lat_mixed = lat_mixed.reshape(everyone, width).astype(b16)
    lat_q_grad = lat_q_grad.reshape(everyone, width).astype(b16)
    lat_k_grad = lat_k_grad.reshape(everyone, width).astype(b16)
    lat_v_grad = lat_v_grad.reshape(everyone, width).astype(b16)
    latent_part = (
        inner_right(lat_q_grad, latent_query)
        + inner_right(lat_k_grad, latent_key)
        + inner_right(lat_v_grad, latent_value)
    )
    latent_gain_part = jnp.sum(latent_part * latent_unit, axis=0, keepdims=True)
    latent_sums = tp_sum(jnp.concatenate([latent_part[:own], latent_gain_part], axis=0))
    latent_grad = middle_latent_grad + norm_back(
        latent_sums[:own], latent_unit[:own], latent_rate[:own], latent_gain
    )
    share = model // size
    latent_gain_done = lax.dynamic_slice_in_dim(latent_sums[own], me * share, share)
    columns = lax.dynamic_slice_in_dim(latent_low, me * share, share, axis=1)
    mid_columns = lax.dynamic_slice_in_dim(mid_low, me * share, share, axis=1)
    latent_query_done = inner_left(columns, lat_q_grad)
    latent_key_done = inner_left(columns, lat_k_grad)
    latent_value_done = inner_left(columns, lat_v_grad)
    latent_output_done = inner_left(lat_mixed, mid_columns)
    token_part = (
        inner_right(query_grad, query_weight)
        + inner_right(token_key_grad, key_weight)
        + inner_right(token_value_grad, value_weight)
    )
    token_part = tp_sum(token_part)
    token_grad = middle_grad + norm_back(token_part, token_unit, token_rate, attention_gain)
    attention_gain_grad = jnp.sum(token_part * token_unit, axis=0) + jnp.sum(
        side_part * side_unit, axis=0
    )
    query_grad_sum = inner_left(token_low, query_grad)
    key_grad_sum = inner_left(token_low, token_key_grad) + inner_left(side_low, side_key_grad)
    value_grad_sum = inner_left(token_low, token_value_grad) + inner_left(
        side_low, side_value_grad
    )
    up_grad = up_grad.reshape(size, share, -1)
    down_grad = down_grad.reshape(size, share, -1)
    output_grad = output_grad.reshape(size, share, -1)
    first = jnp.concatenate([up_grad, down_grad, output_grad], axis=2)
    hidden_units = up_weight.shape[1]
    first = scatter_sum(first)
    up_done = first[:, :hidden_units]
    down_done = first[:, hidden_units : 2 * hidden_units].T
    output_done = first[:, 2 * hidden_units :].T
    second = jnp.concatenate(
        [
            query_grad_sum.reshape(size, share, -1),
            key_grad_sum.reshape(size, share, -1),
            value_grad_sum.reshape(size, share, -1),
        ],
        axis=2,
    )
    second = scatter_sum(second)
    vectors = jnp.concatenate(
        [
            jnp.sum(outer_grad, axis=0).reshape(size, 1, share),
            attention_gain_grad.reshape(size, 1, share),
            feed_gain_grad.reshape(size, 1, share),
            jnp.sum(hidden_grad.astype(f32), axis=0).reshape(size, -1, share),
        ],
        axis=1,
    )
    vectors = scatter_sum(vectors)
    return (
        mixed_tokens,
        latents_mid.astype(b16),
        token_grad,
        latent_grad,
        latent_query_done,
        latent_key_done,
        latent_value_done,
        latent_output_done,
        second[:, :width],
        second[:, width : 2 * width],
        second[:, 2 * width :],
        output_done,
        up_done,
        vectors[3:].reshape(-1),
        down_done,
        vectors[0],
        latent_gain_done,
        vectors[1],
        vectors[2],
    )


def solution(mesh):
    placed = (
        P("dp", None),
        P("dp", None),
        P(None, "tp"),
        P(None, "tp"),
        P(None, "tp"),
        P("tp", None),
        P(None, "tp"),
        P(None, "tp"),
        P(None, "tp"),
        P("tp", None),
        P(None, "tp"),
        P("tp"),
        P("tp", None),
        P(),
        P(),
        P(),
        P(),
        P(),
        P("dp", None),
        P("dp", None),
    )
    return jax.shard_map(
        local,
        mesh=mesh,
        in_specs=placed,
        out_specs=(
            P("dp", None),
            P("dp", None),
            P("dp", None),
            P("dp", None),
            P("dp", "tp"),
            P("dp", "tp"),
            P("dp", "tp"),
            P("tp", "dp"),
            P("dp", "tp"),
            P("dp", "tp"),
            P("dp", "tp"),
            P("tp", "dp"),
            P("dp", "tp"),
            P(("tp", "dp")),
            P("tp", "dp"),
            P("dp"),
            P("dp"),
            P("dp"),
            P("dp"),
        ),
        check_vma=False,
    )
```

```python
from functools import partial

import jax
import jax.numpy as jnp
from jax import lax
from jax.experimental import pallas as pl
from jax.experimental.pallas import tpu as pltpu
from jax.sharding import PartitionSpec as P

E = 64
S = 256
L = 8
EPSILON = 1e-05
NEGATIVE = -1000000000.0
FACTOR = E ** (-0.5)
LOG2E = 1.4426950408889634
F32 = jnp.float32
B16 = jnp.bfloat16


def nn(left, right):
    return lax.dot_general(left, right, (((1,), (0,)), ((), ())), preferred_element_type=F32)


def nt(left, right):
    return lax.dot_general(left, right, (((1,), (1,)), ((), ())), preferred_element_type=F32)


def tn(left, right):
    return lax.dot_general(left, right, (((0,), (0,)), ((), ())), preferred_element_type=F32)


def norm_parts(values):
    average = jnp.mean(values, axis=-1, keepdims=True)
    centred = values - average
    spread = jnp.mean(centred * centred, axis=-1, keepdims=True)
    rate = lax.rsqrt(spread + EPSILON)
    return centred * rate, rate


def norm_back(grad, unit, rate, gain):
    scaled = grad * gain
    first = jnp.mean(scaled, axis=-1, keepdims=True)
    second = jnp.mean(scaled * unit, axis=-1, keepdims=True)
    return rate * (scaled - first - unit * second)


def gelu_both(values):
    square = values * values
    wave = jnp.tanh(0.7978845608028654 * values * (1.0 + 0.044715 * square))
    slope = 0.7978845608028654 * (1.0 + 0.134145 * square)
    half = 0.5 * (1.0 + wave)
    return values * half, half + 0.5 * values * (1.0 - wave * wave) * slope


def head_mask(heads, rows, width):
    row = lax.broadcasted_iota(jnp.int32, (heads * rows, width), 0)
    column = lax.broadcasted_iota(jnp.int32, (heads * rows, width), 1)
    return (row // rows) == (column // E)


def spread_heads(values, heads):
    rows, width = values.shape
    stacked = jnp.concatenate([values] * heads, axis=0)
    return jnp.where(head_mask(heads, rows, width), stacked, jnp.zeros_like(stacked))


def fold_heads(values, heads):
    rows, width = values.shape[0] // heads, values.shape[1]
    kept = jnp.where(head_mask(heads, rows, width), values, jnp.zeros_like(values))
    total = kept[:rows]
    for h in range(1, heads):
        total = total + kept[h * rows : (h + 1) * rows]
    return total


def half_mask(width):
    return lax.broadcasted_iota(jnp.int32, (1, width), 1) < E


def head_only(values, second):
    mask = half_mask(values.shape[1])
    zero = jnp.zeros_like(values)
    return jnp.where(mask, zero, values) if second else jnp.where(mask, values, zero)


def enter_kernel(tokens, gain, wq, wk, wv, q_out, k_out, v_out, saved_out):
    unit, _ = norm_parts(tokens[...].astype(F32))
    low = (unit * gain[...]).astype(B16)
    q = nn(low, wq[...]).astype(B16)
    k = nn(low, wk[...]).astype(B16)
    v = nn(low, wv[...]).astype(B16)
    q_out[...] = q
    k_out[...] = k
    v_out[...] = v
    width = q.shape[1]
    saved_out[:, :width] = q
    saved_out[:, width : 2 * width] = k
    saved_out[:, 2 * width : 3 * width] = v
    saved_out[:, 3 * width :] = low


def latent_kernel(
    heads, own, one, two, gain, own_images, images, wq, wk, wv, wo, latents_out, q_out, k_out, v_out, part_out
):
    latents = jnp.concatenate([one[...], two[...]], axis=0)
    latents_out[...] = latents
    unit, _ = norm_parts(latents.astype(F32))
    low = (unit * gain[...]).astype(B16)
    q = nn(low, wq[...]).astype(B16)
    k = nn(low, wk[...]).astype(B16)
    v = nn(low, wv[...]).astype(B16)
    q_out[...] = q
    k_out[...] = k
    v_out[...] = v
    scores = nt(spread_heads(q[:own], heads), k) * FACTOR
    member = jnp.concatenate([own_images[...]] * heads, axis=0) == images[...]
    scores = jnp.where(member, scores, NEGATIVE)
    weights = jnp.exp(scores - jnp.max(scores, axis=-1, keepdims=True))
    probs = weights / jnp.sum(weights, axis=-1, keepdims=True)
    mixed = fold_heads(nn(probs.astype(B16), v), heads).astype(B16)
    part_out[...] = nn(mixed, wo[...]).astype(B16)


def attend_kernel(
    g, heads, q, k, v, latents, part_one, part_two, gain, wk, wv, wo,
    part_out, o_out, probs_out, side_out, mid_out, mid_low_out,
):
    mid = latents[...].astype(F32) + (part_one[...].astype(F32) + part_two[...].astype(F32))
    mid_out[...] = mid
    mid_low_out[...] = mid.astype(B16)
    unit, _ = norm_parts(mid[g * L : (g + 1) * L])
    side_low = (unit * gain[...]).astype(B16)
    side_k = nn(side_low, wk[...]).astype(B16).astype(F32)
    side_v = nn(side_low, wv[...]).astype(B16).astype(F32)
    width = side_k.shape[1]
    side_out[:, :width] = side_k
    side_out[:, width : 2 * width] = side_v
    side_out[:, 2 * width :] = side_low.astype(F32)
    side_v = spread_heads(side_v, heads).astype(B16)
    side_scores = nt(spread_heads(side_k, heads).astype(B16), q[...])
    scale = FACTOR * LOG2E
    outs, side_probs, lses = [], [], []
    for pair in range(heads // 2):
        cut = slice(pair * 2 * E, (pair + 1) * 2 * E)
        q_pair, k_pair, v_pair = q[:, cut], k[:, cut], v[:, cut]
        for second in (0, 1):
            h = 2 * pair + second
            scores = nt(head_only(k_pair, second), q_pair)
            side = side_scores[h * L : (h + 1) * L]
            top = jnp.maximum(
                jnp.max(scores, axis=0, keepdims=True), jnp.max(side, axis=0, keepdims=True)
            )
            weights = jnp.exp2((scores - top) * scale)
            side = jnp.exp2((side - top) * scale)
            total = jnp.sum(weights, axis=0, keepdims=True) + jnp.sum(side, axis=0, keepdims=True)
            inverse = 1.0 / total
            side_probs.append(side * inverse)
            lses.append(top * scale + jnp.log2(total))
            outs.append(tn((weights * inverse).astype(B16), v_pair))
    side_probs = jnp.concatenate(side_probs, axis=0)
    probs_out[: heads * L, :] = side_probs
    probs_out[heads * L :, :] = jnp.concatenate(
        lses + [jnp.zeros_like(lses[0])] * (8 - heads), axis=0
    )
    side_o = tn(side_probs.astype(B16), side_v)
    first = half_mask(2 * E)
    token_o = jnp.concatenate(
        [jnp.where(first, outs[2 * i], outs[2 * i + 1]) for i in range(heads // 2)], axis=1
    )
    o = (token_o + side_o).astype(B16)
    o_out[...] = o
    part_out[...] = nn(o, wo[...]).astype(B16)


def feed_kernel(
    tokens, part_one, part_two, cotangent, gain, up, up_bias, down,
    part_out, active_out, hidden_grad_out, low_out, middle_out, down_part_out, up_bias_out, down_bias_out,
    part_sum, down_sum,
):
    step = pl.program_id(0)

    @pl.when(step == 0)
    def _():
        middle = tokens[...].astype(F32) + (part_one[...].astype(F32) + part_two[...].astype(F32))
        middle_out[...] = middle
        unit, _ = norm_parts(middle)
        low_out[...] = (unit * gain[...]).astype(B16)
        down_bias_out[...] = jnp.sum(cotangent[...].astype(F32), axis=0, keepdims=True)
        part_sum[...] = jnp.zeros_like(part_sum)
        down_sum[...] = jnp.zeros_like(down_sum)

    hidden = nn(low_out[...], up[...]) + up_bias[...]
    active, slope = gelu_both(hidden)
    active = active.astype(B16)
    active_out[...] = active
    grad = (slope * nt(cotangent[...], down[...])).astype(B16)
    hidden_grad_out[...] = grad
    up_bias_out[...] = jnp.sum(grad.astype(F32), axis=0, keepdims=True)
    part_sum[...] += nt(grad, up[...])
    down_sum[...] += nn(active, down[...])

    @pl.when(step == pl.num_programs(0) - 1)
    def _():
        part_out[...] = part_sum[...].astype(B16)
        down_part_out[...] = down_sum[...].astype(B16)


def turn_kernel(
    g, heads, cotangent, middle, part_one, part_two, gain, wo, wk, wv, o, q, probs, side, mid, *rest
):
    earlier, outs = rest[:g], rest[g:]
    o_grad_out, delta_out, side_score_grad_out, part_out, grads_out, gain_out = outs[:6]
    middle_grad_out, middle_low_out = outs[6:]
    unit, rate = norm_parts(middle[...])
    grad = part_one[...].astype(F32) + part_two[...].astype(F32)
    gain_out[0:1, :] = jnp.sum(grad * unit, axis=0, keepdims=True)
    middle_grad = cotangent[...].astype(F32) + norm_back(grad, unit, rate, gain[...])
    middle_grad_out[...] = middle_grad
    middle_low = middle_grad.astype(B16)
    middle_low_out[...] = middle_low
    o_grad = nt(middle_low, wo[...]).astype(B16)
    o_grad_out[...] = o_grad
    width = o_grad.shape[1]
    rows8 = lax.broadcasted_iota(jnp.int32, (8, width), 0)
    columns8 = lax.broadcasted_iota(jnp.int32, (8, width), 1) // E
    pick = (rows8 == columns8).astype(B16)
    weighted = o_grad.astype(F32) * o[...].astype(F32)
    high = weighted.astype(B16)
    low = (weighted - high.astype(F32)).astype(B16)
    delta = nt(pick, high) + nt(pick, low)
    delta_out[...] = delta
    side_v = spread_heads(side[:, width : 2 * width], heads).astype(B16)
    side_prob_grad = nt(side_v, o_grad)
    side_probs = probs[: heads * L, :]
    wide = jnp.concatenate(
        [jnp.broadcast_to(delta[h : h + 1], (L, delta.shape[1])) for h in range(heads)], axis=0
    )
    score_grad = (side_probs * (side_prob_grad - wide)).astype(B16)
    side_score_grad_out[...] = score_grad
    k_grad = (fold_heads(nn(score_grad, q[...]), heads) * FACTOR).astype(B16)
    v_grad = fold_heads(nn(side_probs.astype(B16), o_grad), heads).astype(B16)
    grads_out[:, :width] = k_grad.astype(F32)
    grads_out[:, width:] = v_grad.astype(F32)
    part = nt(k_grad, wk[...]) + nt(v_grad, wv[...])
    side_unit, _ = norm_parts(mid[g * L : (g + 1) * L, :])
    gain_out[1:2, :] = jnp.sum(part * side_unit, axis=0, keepdims=True)
    gain_out[2:, :] = jnp.zeros_like(gain_out[2:, :])
    part = jnp.concatenate([r[...] for r in earlier] + [part], axis=0)
    part_out[...] = part.astype(part_out.dtype)


def side_kernel(part_one, part_two, mid, cotangent, gain, low_out, grad_out):
    unit, rate = norm_parts(mid[...])
    part = part_one[...].astype(F32) + part_two[...].astype(F32)
    grad = cotangent[...].astype(F32) + norm_back(part, unit, rate, gain[...])
    grad_out[...] = grad
    low_out[...] = grad.astype(B16)


def attend_back_kernel(
    heads, tokens, q, k, v, o_grad, probs, delta, side_score_grad, side, wq, wk, wv, earlier_gain, *rest
):
    side_gains, (part_out, grads_out, gain_out) = rest[:-3], rest[-3:]
    scale = FACTOR * LOG2E
    first = half_mask(2 * E)
    width = q.shape[1]
    side_k = spread_heads(side[:, :width], heads).astype(B16)
    side_q_grad = tn(side_score_grad[...], side_k)
    at = heads * L
    for pair in range(heads // 2):
        start = pair * 2 * E
        cut = slice(start, start + 2 * E)
        q_pair, k_pair, v_pair, grad_pair = q[:, cut], k[:, cut], v[:, cut], o_grad[:, cut]
        q_grads, k_grads, v_grads = [], [], []
        for second in (0, 1):
            h = 2 * pair + second
            scores = nt(head_only(k_pair, second), q_pair)
            weights = jnp.exp2(scores * scale - probs[at + h : at + h + 1, :])
            prob_grad = nt(head_only(v_pair, second), grad_pair)
            score_grad = (weights * (prob_grad - delta[h : h + 1, :])).astype(B16)
            v_grads.append(nn(weights.astype(B16), grad_pair))
            k_grads.append(nn(score_grad, q_pair))
            q_grads.append(tn(score_grad, k_pair))
        q_pair_grad = jnp.where(first, q_grads[0], q_grads[1]) + side_q_grad[:, cut]
        k_pair_grad = jnp.where(first, k_grads[0], k_grads[1])
        v_pair_grad = jnp.where(first, v_grads[0], v_grads[1])
        grads_out[:, start : start + 2 * E] = (q_pair_grad * FACTOR).astype(B16)
        grads_out[:, width + start : width + start + 2 * E] = (k_pair_grad * FACTOR).astype(B16)
        grads_out[:, 2 * width + start : 2 * width + start + 2 * E] = v_pair_grad.astype(B16)
    part = nt(grads_out[:, :width], wq[...]) + nt(grads_out[:, width : 2 * width], wk[...])
    part = part + nt(grads_out[:, 2 * width :], wv[...])
    part_out[...] = part.astype(B16)
    unit, _ = norm_parts(tokens[...].astype(F32))
    total = earlier_gain[...] + jnp.sum(part * unit, axis=0, keepdims=True)
    for r in side_gains:
        total = total + r[1:2, :]
    gain_out[...] = total


def leave_kernel(groups, tokens, gain, *refs):
    grad_out = refs[-1]
    for g in range(groups):
        part_one, part_two, middle_grad = refs[3 * g : 3 * g + 3]
        rows = slice(g * S, (g + 1) * S)
        unit, rate = norm_parts(tokens[rows, :].astype(F32))
        grad = part_one[...].astype(F32) + part_two[...].astype(F32)
        grad_out[rows, :] = middle_grad[...] + norm_back(grad, unit, rate, gain[...])


def result_kernel(groups, bias, *refs):
    out = refs[-1]
    for g in range(groups):
        middle, part_one, part_two = refs[3 * g : 3 * g + 3]
        rows = slice(g * S, (g + 1) * S)
        total = part_one[...].astype(F32) + part_two[...].astype(F32)
        out[rows, :] = (middle[...] + total + bias[...]).astype(B16)


def latent_leave_kernel(latents, part_one, part_two, gain, mid_grad, grad_out, gain_out):
    own = latents.shape[0]
    unit, rate = norm_parts(latents[...].astype(F32))
    total = part_one[...].astype(F32) + part_two[...].astype(F32)
    grad_out[...] = mid_grad[...] + norm_back(total[:own], unit, rate, gain[...])
    gain_out[...] = total[own : own + 8]


def split_pairs(values, bit, share, send_out, keep_out, cut):
    blocks = values.reshape(values.shape[0] // (2 * share), 2, share, values.shape[1])
    even, odd = blocks[:, 0], blocks[:, 1]
    send_out[:, :, cut] = jnp.where(bit == 0, odd, even).astype(B16)
    keep_out[:, :, cut] = jnp.where(bit == 0, even, odd).astype(B16)


def weight_grad_kernel(groups, share, chunk, me, *refs):
    lefts, rights = refs[:groups], refs[groups : 2 * groups]
    send_out, keep_out = refs[2 * groups :]
    flat = [left[...].T for left in lefts]
    for start in range(0, rights[0].shape[1], chunk):
        cut = slice(start, start + chunk)
        total = nn(flat[0], rights[0][:, cut])
        for g in range(1, groups):
            total = total + nn(flat[g], rights[g][:, cut])
        split_pairs(total, me[0] % 2, share, send_out, keep_out, cut)


def attention_grad_kernel(groups, share, me, gain_one, gain_two, *refs):
    saved, grads, middle_low, o, side, side_grads, up_bias, down_bias, gains = (
        refs[i * groups : (i + 1) * groups] for i in range(9)
    )
    send_out, keep_out = refs[9 * groups :]
    bit = me[0] % 2
    width = o[0].shape[1]
    model = middle_low[0].shape[1]
    stack = [jnp.concatenate([r[...] for r in rs], axis=0) for rs in (side, side_grads)]
    side_low = stack[0][:, 2 * width :].astype(B16)
    side_k, side_v = stack[1][:, :width].astype(B16), stack[1][:, width:].astype(B16)
    flat = [r[:, 3 * width :].T for r in saved]
    low_flat = [r[...].T for r in middle_low]

    def total_of(lefts, rights, cut):
        total = nn(lefts[0], rights[0][:, cut])
        for g in range(1, groups):
            total = total + nn(lefts[g], rights[g][:, cut])
        return total

    def cut_of(i):
        return slice(i * width, (i + 1) * width)

    split_pairs(total_of(flat, grads, cut_of(0)), bit, share, send_out, keep_out, cut_of(0))
    total = total_of(flat, grads, cut_of(1)) + tn(side_low, side_k)
    split_pairs(total, bit, share, send_out, keep_out, cut_of(1))
    total = total_of(flat, grads, cut_of(2)) + tn(side_low, side_v)
    split_pairs(total, bit, share, send_out, keep_out, cut_of(2))
    total = total_of(low_flat, o, cut_of(0))
    split_pairs(total, bit, share, send_out, keep_out, cut_of(3))

    def column(rows):
        return jnp.broadcast_to(rows, (8, rows.shape[1])).T

    def sum_of(parts):
        total = parts[0]
        for part in parts[1:]:
            total = total + part
        return total

    columns = [
        column(sum_of([r[...] for r in down_bias])),
        column(sum_of([r[0:1, :] for r in gains])),
        column(gain_one[...] + gain_two[...]),
    ]
    bias = column(sum_of([r[...] for r in up_bias]))
    times = bias.shape[0] // model
    bias = bias.reshape(model // share, times, share, 8)
    columns += [bias[:, i].reshape(model, 8) for i in range(times)]
    lane = lax.broadcasted_iota(jnp.int32, (model, 128), 1)
    block = jnp.zeros((model, 128), F32)
    for i, one in enumerate(columns):
        block = jnp.where(lane == i, one[:, 0:1], block)
    split_pairs(block, bit, share, send_out, keep_out, slice(4 * width, 4 * width + 128))


def halve_kernel(shift, me, keep, got, send_out, keep_out):
    bit = (me[0] // shift) % 2
    for i in range(keep.shape[0]):
        there = keep[i, pl.ds(1 - bit, 1)].astype(F32) + got[i, pl.ds(1 - bit, 1)].astype(F32)
        here = keep[i, pl.ds(bit, 1)].astype(F32) + got[i, pl.ds(bit, 1)].astype(F32)
        send_out[pl.ds(i, 1)] = there.astype(B16)
        keep_out[pl.ds(i, 1)] = here.astype(B16)


def spread_kernel(shift, me, keep, got, own_out, *outs):
    place = me[0] // shift
    for k in range(keep.shape[0]):
        at = pl.ds(place ^ k, 1)
        total = (keep[at].astype(F32) + got[at].astype(F32))[0]
        if k == 0:
            own_out[...] = total
        else:
            outs[k - 1][...] = total.astype(B16)


def finish_kernel(cuts, own, *refs):
    gots, outs = refs[: len(refs) - len(cuts)], refs[len(refs) - len(cuts) :]
    total = own[...]
    for got in gots:
        total = total + got[...].astype(F32)
    for out, (start, end, flat) in zip(outs, cuts):
        part = total[:, start:end]
        out[...] = part.T if flat else part


def latent_back_kernel(
    heads, own, block, me, latents, q, k, v, mid_one, mid_two, images_column, images_row, gain, wq, wk, wv, wo,
    part_out, wq_out, wk_out, wv_out, wo_out, mixed, q_grad, k_grad, v_grad,
):
    mid_low = jnp.concatenate([mid_one[...], mid_two[...]], axis=0)
    o_grad = nt(mid_low, wo[...]).astype(B16)
    unit, _ = norm_parts(latents[...].astype(F32))
    low = (unit * gain[...]).astype(B16)
    everyone = low.shape[0]

    def rows_of(start, ref_q, ref_grad, ref_images):
        wide_q = spread_heads(ref_q, heads)
        wide_grad = spread_heads(ref_grad, heads)
        scores = nt(wide_q, k[...]) * FACTOR
        member = jnp.concatenate([ref_images] * heads, axis=0) == images_row[...]
        scores = jnp.where(member, scores, NEGATIVE)
        weights = jnp.exp(scores - jnp.max(scores, axis=-1, keepdims=True))
        probs = weights / jnp.sum(weights, axis=-1, keepdims=True)
        probs_low = probs.astype(B16)
        prob_grad = nt(wide_grad, v[...])
        delta = jnp.sum(prob_grad * probs, axis=-1, keepdims=True)
        score_grad = (probs * (prob_grad - delta)).astype(B16)
        mixed[pl.ds(start, block), :] = fold_heads(nn(probs_low, v[...]), heads).astype(B16)
        q_grad[pl.ds(start, block), :] = (
            fold_heads(nn(score_grad, k[...]), heads) * FACTOR
        ).astype(B16)
        return tn(score_grad, wide_q), tn(probs_low, wide_grad)

    if block == everyone:
        k_sum, v_sum = rows_of(0, q[...], o_grad, images_column[...])
        k_sum, v_sum = k_sum * FACTOR, v_sum
    else:
        v_grad[...] = o_grad

        def step(i, held):
            start = pl.multiple_of(i * block, block)
            here = pl.ds(start, block)
            one, two = rows_of(start, q[here, :], v_grad[here, :], images_column[here, :])
            return held[0] + one, held[1] + two

        zero = jnp.zeros(k.shape, F32)
        k_sum, v_sum = lax.fori_loop(0, everyone // block, step, (zero, zero))
        k_sum = k_sum * FACTOR
    k_grad[...] = k_sum.astype(B16)
    v_grad[...] = v_sum.astype(B16)
    part = nt(q_grad[...], wq[...]) + nt(k_grad[...], wk[...]) + nt(v_grad[...], wv[...])
    gain_part = jnp.sum(part * unit, axis=0, keepdims=True)
    part_out[...] = jnp.concatenate(
        [part[:own], jnp.broadcast_to(gain_part, (16, part.shape[1]))], axis=0
    ).astype(B16)
    share = wq_out.shape[0]
    model = low.shape[1]
    row = lax.broadcasted_iota(jnp.int32, (share, model), 0)
    column = lax.broadcasted_iota(jnp.int32, (share, model), 1)
    pick = (column == row + me[0] * share).astype(B16)
    columns = nt(pick, low).astype(B16)
    wq_out[...] = nn(columns, q_grad[...])
    wk_out[...] = nn(columns, k_grad[...])
    wv_out[...] = nn(columns, v_grad[...])
    wo_out[...] = nn(nt(pick, mid_low).astype(B16), mixed[...])


MIB = 1024 * 1024
KEPT = "kept"


class Order:
    def __init__(self):
        self.last = None

    def call(self, kernel, name, outs, ins, grid=(1,), scratch=(), limit=24):
        def spec(shape, block):
            if block is None:
                return pl.BlockSpec(tuple(shape), lambda *_: (0,) * len(shape))
            if block == "smem":
                return pl.BlockSpec(memory_space=pltpu.SMEM)
            extent, where = block
            if isinstance(extent, int):
                return pl.BlockSpec((extent, shape[1]), lambda *_: (where, 0))
            return pl.BlockSpec(extent, where)

        arrays = [entry[0] for entry in ins]
        if self.last is not None:
            least = min(range(len(arrays)), key=lambda i: arrays[i].size)
            arrays[least] = after(arrays[least], self.last)
        arrays = [
            pltpu.with_memory_space_constraint(a, pltpu.HBM) if KEPT in entry[2:] else a
            for a, entry in zip(arrays, ins)
        ]
        results = pl.pallas_call(
            kernel,
            out_shape=[
                pltpu.HBM(entry[0], entry[1])
                if KEPT in entry[3:]
                else jax.ShapeDtypeStruct(entry[0], entry[1])
                for entry in outs
            ],
            grid=grid,
            in_specs=[spec(entry[0].shape, entry[1]) for entry in ins],
            out_specs=[spec(entry[0], entry[2]) for entry in outs],
            scratch_shapes=list(scratch),
            compiler_params=pltpu.CompilerParams(vmem_limit_bytes=limit * MIB),
            cost_estimate=pl.CostEstimate(flops=0, bytes_accessed=0, transcendentals=0),
            name=name,
        )(*arrays)
        self.last = min(results, key=lambda a: a.size)
        return results


def after(value, *earlier):
    return lax.optimization_barrier((value, earlier))[0]


def swap_tp(values):
    return lax.ppermute(values, "tp", [(0, 1), (1, 0)])


def flip(values, bits):
    size = lax.axis_size("dp")
    return lax.ppermute(values, "dp", [(i, i ^ bits) for i in range(size)])


def gather_steps(size):
    width, steps = 2, []
    while width * 4 < size:
        steps.append([width])
        width *= 2
    if width < size:
        steps.append([width * k for k in range(1, size // width)])
    steps.reverse()
    return steps + [[1]]


def gather_order(size):
    order = [0]
    for step in gather_steps(size):
        order = order + [i ^ bits for bits in [0] + step for i in order][len(order) :]
    return order


def gather_relative(own):
    held = own
    for step in gather_steps(lax.axis_size("dp"))[:-1]:
        held = jnp.concatenate([held] + [flip(held, bits) for bits in step], axis=0)
    return held, flip(held, 1)


def scatter_sum(grads):
    size = lax.axis_size("dp")
    me = lax.axis_index("dp")
    width = 1
    while width * 4 < size:
        bit = (me // width) % 2
        pairs = grads.reshape((grads.shape[0] // 2, 2) + grads.shape[1:])
        send = lax.dynamic_index_in_dim(pairs, 1 - bit, 1, keepdims=False)
        keep = lax.dynamic_index_in_dim(pairs, bit, 1, keepdims=False)
        got = flip(send.astype(B16), width)
        grads = keep.astype(F32) + got.astype(F32)
        width *= 2
    place = me // width
    total = lax.dynamic_index_in_dim(grads, place, 0, keepdims=False)
    for k in range(1, size // width):
        send = lax.dynamic_index_in_dim(grads, place ^ k, 0, keepdims=False)
        total = total + flip(send.astype(B16), width * k).astype(F32)
    return total


class Scatter:
    def __init__(self, order, share, me):
        self.order, self.share, self.me = order, share, me

    def begin(self, send, keep):
        self.keep, self.got, self.width = keep, flip(send, 1), 2

    def halve(self):
        n, share, columns = self.keep.shape
        four = (n // 2, 2, share, columns)
        half = (n // 2, share, columns)
        send, keep = self.order.call(
            partial(halve_kernel, self.width),
            "halve",
            [(half, B16, None), (half, B16, None, KEPT)],
            [
                (self.me, "smem"),
                (self.keep.reshape(four), None, KEPT),
                (self.got.reshape(four), None),
            ],
        )
        self.keep, self.got = keep, flip(send, self.width)
        self.width *= 2

    def spread(self):
        n, share, columns = self.keep.shape
        flat = (share, columns)
        own, *sends = self.order.call(
            partial(spread_kernel, self.width),
            "spread",
            [(flat, F32, None, KEPT)] + [(flat, B16, None)] * (n - 1),
            [(self.me, "smem"), (self.keep, None, KEPT), (self.got, None)],
        )
        self.own = own
        self.gots = [flip(s, self.width * (k + 1)) for k, s in enumerate(sends)]

    def finish(self, cuts):
        share = self.own.shape[0]
        shapes = [(e - s, share) if flat else (share, e - s) for s, e, flat in cuts]
        return self.order.call(
            partial(finish_kernel, cuts),
            "finish",
            [(shape, F32, None) for shape in shapes],
            [(self.own, None, KEPT)] + [(got, None) for got in self.gots],
        )


def local(
    tokens,
    latents,
    latent_query,
    latent_key,
    latent_value,
    latent_output,
    query_weight,
    key_weight,
    value_weight,
    output_weight,
    up_weight,
    up_bias,
    down_weight,
    down_bias,
    latent_gain,
    attention_gain,
    feed_gain,
    group_image,
    token_cotangent,
    latent_cotangent,
):
    size = lax.axis_size("dp")
    me = lax.axis_index("dp")
    me_row = me.reshape(1)
    width = latent_query.shape[1]
    heads = width // E
    rows, model = tokens.shape
    hidden_units = up_weight.shape[1]
    groups = rows // S
    own = latents.shape[0]
    everyone = own * size
    share = model // size
    aligned = share % 16 == 0 and size >= 8
    each = range(groups)
    latent_gain_row = latent_gain.reshape(1, model)
    attention_gain_row = attention_gain.reshape(1, model)
    feed_gain_row = feed_gain.reshape(1, model)
    up_bias_row = up_bias.reshape(1, hidden_units)
    down_bias_row = down_bias.reshape(1, model)
    chain = Order()
    call = chain.call

    latents_one, latents_two = gather_relative(latents)
    turns = jnp.bitwise_xor(jnp.array(gather_order(size), jnp.int32), me)
    images = jnp.repeat(group_image.reshape(size, groups)[turns].reshape(-1), L)
    q, k, v, saved = zip(
        *(
            call(
                enter_kernel,
                "enter",
                [((S, width), B16, None)] * 3 + [((S, 3 * width + model), B16, None, KEPT)],
                [
                    (tokens, (S, g), KEPT),
                    (attention_gain_row, None),
                    (query_weight, None, KEPT),
                    (key_weight, None, KEPT),
                    (value_weight, None, KEPT),
                ],
            )
            for g in each
        )
    )
    latents_all, lat_q, lat_k, lat_v, latent_part = call(
        partial(latent_kernel, heads, own),
        "latent",
        [((everyone, model), B16, None, KEPT)]
        + [((everyone, width), B16, None, KEPT)] * 3
        + [((own, model), B16, None)],
        [
            (latents_one, None),
            (latents_two, None),
            (latent_gain_row, None),
            (images[:own].reshape(own, 1), None),
            (images.reshape(1, everyone), None),
            (latent_query, None),
            (latent_key, None),
            (latent_value, None),
            (latent_output, None),
        ],
        limit=24 if everyone <= 512 else 56,
    )
    latent_part_two = swap_tp(latent_part)
    part, o, probs, side, mids, mid_lows = zip(
        *(
            call(
                partial(attend_kernel, g, heads),
                "attend",
                [
                    ((S, model), B16, None),
                    ((S, width), B16, None, KEPT),
                    ((heads * L + 8, S), F32, None, KEPT),
                    ((L, 2 * width + model), F32, None, KEPT),
                    ((own, model), F32, None, KEPT),
                    ((own, model), B16, None, KEPT),
                ],
                [
                    (q[g], None),
                    (k[g], None),
                    (v[g], None),
                    (latents, None),
                    (latent_part, None),
                    (latent_part_two, None),
                    (attention_gain_row, None),
                    (key_weight, None),
                    (value_weight, None),
                    (output_weight, None),
                ],
            )
            for g in each
        )
    )
    mid, mixed_latents = mids[0], mid_lows[0]
    part_two = [swap_tp(p) for p in part]
    chunk = hidden_units // 3
    step = (S, chunk), lambda i: (0, i)
    (
        feed_part,
        active,
        hidden_grad,
        feed_low,
        middle,
        down_part,
        up_bias_sum,
        down_bias_sum,
    ) = zip(
        *(
            call(
                feed_kernel,
                "feed",
                [
                    ((S, model), B16, None),
                    ((S, hidden_units), B16, step),
                    ((S, hidden_units), B16, step),
                    ((S, model), B16, None),
                    ((S, model), F32, None, KEPT),
                    ((S, model), B16, None, KEPT),
                    ((1, hidden_units), F32, ((1, chunk), lambda i: (0, i)), KEPT),
                    ((1, model), F32, None, KEPT),
                ],
                [
                    (tokens, (S, g)),
                    (part[g], None),
                    (part_two[g], None),
                    (token_cotangent, (S, g)),
                    (feed_gain_row, None),
                    (up_weight, ((model, chunk), lambda i: (0, i))),
                    (up_bias_row, ((1, chunk), lambda i: (0, i))),
                    (down_weight, ((chunk, model), lambda i: (i, 0))),
                ],
                grid=(hidden_units // chunk,),
                scratch=[pltpu.VMEM((S, model), F32)] * 2,
            )
            for g in each
        )
    )
    feed_part_two = [swap_tp(p) for p in feed_part]

    def weight_grad(lefts, rights, blocks):
        columns = rights[0].shape[1]
        half = (size // 2, share, columns)
        return call(
            partial(weight_grad_kernel, groups, share, columns // 3),
            "weight_grad",
            [(half, B16, None), (half, B16, None, KEPT)],
            [(me_row, "smem")] + list(zip(lefts, blocks)) + [(a, None) for a in rights],
        )

    def turn(g, earlier):
        last = g == groups - 1
        return call(
            partial(turn_kernel, g, heads),
            "turn",
            [
                ((S, width), B16, None),
                ((8, S), F32, None),
                ((heads * L, S), B16, None),
                ((own if last else L, model), B16 if last else F32, None),
                ((L, 2 * width), F32, None, KEPT),
                ((8, model), F32, None, KEPT),
                ((S, model), F32, None, KEPT),
                ((S, model), B16, None, KEPT),
            ],
            [
                (token_cotangent, (S, g)),
                (middle[g], None, KEPT),
                (feed_part[g], None),
                (feed_part_two[g], None),
                (feed_gain_row, None),
                (output_weight, None),
                (key_weight, None),
                (value_weight, None),
                (o[g], None, KEPT),
                (saved[g], ((S, width), lambda *_: (0, 0)), KEPT),
                (probs[g], None, KEPT),
                (side[g], None, KEPT),
                (mid, None, KEPT),
            ]
            + [(a, None) for a in earlier],
        )

    down_sum, up_sum, rest_sum = (Scatter(chain, share, me_row) for _ in range(3))
    if aligned:
        blocks = [(S, g) for g in each]
        down_sum.begin(*weight_grad([token_cotangent] * groups, active, blocks))
    turned = []
    for g in each:
        turned.append(turn(g, [t[3] for t in turned]))
        if aligned and g == 0:
            down_sum.halve()
            up_sum.begin(*weight_grad(feed_low, hidden_grad, [None] * groups))
    (
        o_grad,
        delta,
        side_score_grad,
        side_parts,
        side_grads,
        gains,
        middle_grad,
        middle_low,
    ) = zip(*turned)
    side_part = side_parts[-1]
    side_part_two = swap_tp(side_part)
    if aligned:
        up_sum.halve()
    back = []
    gain_sum = jnp.zeros((1, model), F32)
    for g in each:
        last = g == groups - 1
        back.append(
            call(
                partial(attend_back_kernel, heads),
                "attend_back",
                [
                    ((S, model), B16, None),
                    ((S, 3 * width), B16, None),
                    ((1, model), F32, None),
                ],
                [(tokens, (S, g), KEPT)]
                + [
                    (saved[g], ((S, width), lambda *_, i=i: (0, i)), KEPT) for i in range(3)
                ]
                + [
                    (o_grad[g], None),
                    (probs[g], None, KEPT),
                    (delta[g], None),
                    (side_score_grad[g], None),
                    (side[g], None, KEPT),
                    (query_weight, None),
                    (key_weight, None),
                    (value_weight, None),
                    (gain_sum, None),
                ]
                + [(a, None, KEPT) for a in gains if last],
            )
        )
        gain_sum = back[-1][2]
        if g == 0:
            mid_low, middle_latent_grad = call(
                side_kernel,
                "side",
                [((own, model), B16, None), ((own, model), F32, None, KEPT)],
                [
                    (side_part, None),
                    (side_part_two, None),
                    (mid, None, KEPT),
                    (latent_cotangent, None),
                    (attention_gain_row, None),
                ],
            )
    mid_low_one, mid_low_two = gather_relative(mid_low)
    token_part, grads, _ = zip(*back)
    gain_two = swap_tp(gain_sum)
    token_part_two = [swap_tp(p) for p in token_part]
    if aligned:
        columns = 4 * width + 128
        half = (size // 2, share, columns)
        arrays = (saved, grads, middle_low, o, side, side_grads, up_bias_sum, down_bias_sum, gains)
        kept = [a for of_groups in arrays for a in of_groups]
        down_sum.spread()
        rest_sum.begin(
            *call(
                partial(attention_grad_kernel, groups, share),
                "attention_grad",
                [(half, B16, None), (half, B16, None, KEPT)],
                [(me_row, "smem"), (gain_sum, None), (gain_two, None)]
                + [(a, None) if any(a is b for b in grads) else (a, None, KEPT) for a in kept],
            )
        )
        up_sum.spread()
        rest_sum.halve()
    else:

        def flat(arrays, start, end):
            return jnp.concatenate([a[:, start:end] for a in arrays], axis=0).astype(B16)

        token_low = flat(saved, 3 * width, 3 * width + model)
        side_low = flat(side, 2 * width, 2 * width + model)
        products = (
            tn(token_cotangent, flat(active, 0, hidden_units)),
            tn(flat(feed_low, 0, model), flat(hidden_grad, 0, hidden_units)),
            tn(token_low, flat(grads, 0, width)),
            tn(token_low, flat(grads, width, 2 * width)) + tn(side_low, flat(side_grads, 0, width)),
            tn(token_low, flat(grads, 2 * width, 3 * width))
            + tn(side_low, flat(side_grads, width, 2 * width)),
            tn(flat(middle_low, 0, model), flat(o, 0, width)),
        )
        vectors = [sum(down_bias_sum), sum(gains)[:1], gain_sum + gain_two]
        vectors.append(sum(up_bias_sum).reshape(size, -1, share).swapaxes(0, 1).reshape(-1, model))
        vectors = jnp.concatenate(vectors, axis=0)
        total = jnp.concatenate([a.astype(B16) for a in products + (vectors.T,)], axis=1)
        total = scatter_sum(total.reshape(size, share, -1))
    block = min(everyone, max(16, 65536 // everyone))
    latent_sum, latent_query_done, latent_key_done, latent_value_done, latent_output_done = call(
        partial(latent_back_kernel, heads, own, block),
        "latent_back",
        [((own + 16, model), B16, None)] + [((share, width), F32, None)] * 4,
        [
            (me_row, "smem"),
            (latents_all, None, KEPT),
            (lat_q, None, KEPT),
            (lat_k, None, KEPT),
            (lat_v, None, KEPT),
            (mid_low_one, None),
            (mid_low_two, None),
            (images.reshape(everyone, 1), None),
            (images.reshape(1, everyone), None),
            (latent_gain_row, None),
            (latent_query, None),
            (latent_key, None),
            (latent_value, None),
            (latent_output, None),
        ],
        scratch=[pltpu.VMEM((everyone, width), B16)] * 4,
        limit=24 if everyone <= 512 else 56,
    )
    latent_sum_two = swap_tp(latent_sum)
    (token_grad,) = call(
        partial(leave_kernel, groups),
        "leave",
        [((rows, model), F32, None)],
        [(tokens, None, KEPT), (attention_gain_row, None)]
        + [
            entry
            for g in each
            for entry in (
                (token_part[g], None),
                (token_part_two[g], None),
                (middle_grad[g], None, KEPT),
            )
        ],
    )
    down_part_two = [swap_tp(after(p, *token_part_two)) for p in down_part]
    latent_grad, latent_gain_sum = call(
        latent_leave_kernel,
        "latent_leave",
        [((own, model), F32, None), ((8, model), F32, None)],
        [
            (latents, None),
            (latent_sum, None),
            (latent_sum_two, None),
            (latent_gain_row, None),
            (middle_latent_grad, None, KEPT),
        ],
    )
    latent_gain_done = lax.dynamic_slice_in_dim(latent_gain_sum[0], me * share, share)
    cuts = [(i * width, (i + 1) * width, i == 3) for i in range(4)]
    if aligned:
        rest_sum.spread()
        (down_done,) = down_sum.finish([(0, hidden_units, True)])
        (up_done,) = up_sum.finish([(0, hidden_units, False)])
    (mixed_tokens,) = call(
        partial(result_kernel, groups),
        "result",
        [((rows, model), B16, None)],
        [(down_bias_row, None)]
        + [
            entry
            for g in each
            for entry in (
                (middle[g], None, KEPT),
                (down_part[g], None),
                (down_part_two[g], None),
            )
        ],
    )
    if aligned:
        cuts.append((4 * width, 4 * width + 128, True))
        query_done, key_done, value_done, output_done, vectors = rest_sum.finish(cuts)
    else:
        ends = [hidden_units, 2 * hidden_units] + [2 * hidden_units + i * width for i in range(1, 5)]
        down_done, up_done, query_done, key_done, value_done, output_done, vectors = jnp.split(
            total, ends, axis=1
        )
        down_done, output_done, vectors = down_done.T, output_done.T, vectors.T
    return (
        mixed_tokens,
        mixed_latents,
        token_grad,
        latent_grad,
        latent_query_done,
        latent_key_done,
        latent_value_done,
        latent_output_done.T,
        query_done,
        key_done,
        value_done,
        output_done,
        up_done,
        vectors[3 : 3 + hidden_units // model].reshape(-1),
        down_done,
        vectors[0],
        latent_gain_done,
        vectors[2],
        vectors[1],
    )


def solution(mesh):
    placed = (
        P("dp", None),
        P("dp", None),
        P(None, "tp"),
        P(None, "tp"),
        P(None, "tp"),
        P("tp", None),
        P(None, "tp"),
        P(None, "tp"),
        P(None, "tp"),
        P("tp", None),
        P(None, "tp"),
        P("tp"),
        P("tp", None),
        P(),
        P(),
        P(),
        P(),
        P(),
        P("dp", None),
        P("dp", None),
    )
    return jax.shard_map(
        local,
        mesh=mesh,
        in_specs=placed,
        out_specs=(
            P("dp", None),
            P("dp", None),
            P("dp", None),
            P("dp", None),
            P("dp", "tp"),
            P("dp", "tp"),
            P("dp", "tp"),
            P("tp", "dp"),
            P("dp", "tp"),
            P("dp", "tp"),
            P("dp", "tp"),
            P("tp", "dp"),
            P("dp", "tp"),
            P(("tp", "dp")),
            P("tp", "dp"),
            P("dp"),
            P("dp"),
            P("dp"),
            P("dp"),
        ),
        check_vma=False,
    )
```

```python
from functools import partial

import jax
import jax.numpy as jnp
from jax import lax
from jax.experimental import pallas as pl
from jax.experimental.pallas import tpu as pltpu
from jax.sharding import PartitionSpec as P

E = 64
S = 256
L = 8
EPSILON = 1e-05
NEGATIVE = -1000000000.0
FACTOR = E ** (-0.5)
LOG2E = 1.4426950408889634
F32 = jnp.float32
B16 = jnp.bfloat16


def nn(left, right):
    return lax.dot_general(left, right, (((1,), (0,)), ((), ())), preferred_element_type=F32)


def nt(left, right):
    return lax.dot_general(left, right, (((1,), (1,)), ((), ())), preferred_element_type=F32)


def tn(left, right):
    return lax.dot_general(left, right, (((0,), (0,)), ((), ())), preferred_element_type=F32)


def norm_parts(values):
    average = jnp.mean(values, axis=-1, keepdims=True)
    centred = values - average
    spread = jnp.mean(centred * centred, axis=-1, keepdims=True)
    rate = lax.rsqrt(spread + EPSILON)
    return centred * rate, rate


def norm_back(grad, unit, rate, gain):
    scaled = grad * gain
    first = jnp.mean(scaled, axis=-1, keepdims=True)
    second = jnp.mean(scaled * unit, axis=-1, keepdims=True)
    return rate * (scaled - first - unit * second)


def gelu_both(values):
    square = values * values
    wave = jnp.tanh(0.7978845608028654 * values * (1.0 + 0.044715 * square))
    slope = 0.7978845608028654 * (1.0 + 0.134145 * square)
    half = 0.5 * (1.0 + wave)
    return values * half, half + 0.5 * values * (1.0 - wave * wave) * slope


def head_mask(heads, rows, width):
    row = lax.broadcasted_iota(jnp.int32, (heads * rows, width), 0)
    column = lax.broadcasted_iota(jnp.int32, (heads * rows, width), 1)
    return (row // rows) == (column // E)


def spread_heads(values, heads):
    rows, width = values.shape
    stacked = jnp.concatenate([values] * heads, axis=0)
    return jnp.where(head_mask(heads, rows, width), stacked, jnp.zeros_like(stacked))


def fold_heads(values, heads):
    rows, width = values.shape[0] // heads, values.shape[1]
    kept = jnp.where(head_mask(heads, rows, width), values, jnp.zeros_like(values))
    total = kept[:rows]
    for h in range(1, heads):
        total = total + kept[h * rows : (h + 1) * rows]
    return total


def half_mask(width):
    return lax.broadcasted_iota(jnp.int32, (1, width), 1) < E


def head_only(values, second):
    mask = half_mask(values.shape[1])
    zero = jnp.zeros_like(values)
    return jnp.where(mask, zero, values) if second else jnp.where(mask, values, zero)


def load_kernel(*refs):
    count = (len(refs) - 1) // 2
    ready = refs[-1]
    copies = [
        pltpu.make_async_copy(refs[i], refs[count + i], ready.at[i]) for i in range(count)
    ]
    for copy in copies:
        copy.start()
    for copy in copies:
        copy.wait()


def join_kernel(*refs):
    at = 0
    for r in refs[:-1]:
        refs[-1][at : at + r.shape[0], :] = r[...]
        at += r.shape[0]


def enter_kernel(g, tokens, gain, wq, wk, wv, saved_out):
    unit, _ = norm_parts(tokens[g * S : (g + 1) * S, :].astype(F32))
    low = (unit * gain[...]).astype(B16)
    width = wq.shape[1]
    saved_out[:, :width] = nn(low, wq[...]).astype(B16)
    saved_out[:, width : 2 * width] = nn(low, wk[...]).astype(B16)
    saved_out[:, 2 * width : 3 * width] = nn(low, wv[...]).astype(B16)
    saved_out[:, 3 * width :] = low


def image_rows(order, groups, me, group_image):
    count = len(order) * groups * L
    lane = lax.broadcasted_iota(jnp.int32, (8, count), 1) // L
    images = jnp.zeros((8, count), F32)
    for j, bits in enumerate(order):
        for g in range(groups):
            image = group_image[(me ^ bits) * groups + g].astype(F32)
            images = jnp.where(lane == j * groups + g, image, images)
    return images[:1], images.T[:, :1]


def latent_kernel(
    heads, own, order, me, group_image, one, two, gain, wq, wk, wv, wo, latents_out, q_out, k_out, v_out, part_out
):
    latents = jnp.concatenate([one[...], two[...]], axis=0)
    latents_out[...] = latents
    unit, _ = norm_parts(latents.astype(F32))
    low = (unit * gain[...]).astype(B16)
    q = nn(low, wq[...]).astype(B16)
    k = nn(low, wk[...]).astype(B16)
    v = nn(low, wv[...]).astype(B16)
    q_out[...] = q
    k_out[...] = k
    v_out[...] = v
    scores = nt(spread_heads(q[:own], heads), k) * FACTOR
    images, column = image_rows(order, own // L, me[0], group_image)
    member = jnp.concatenate([column[:own]] * heads, axis=0) == images
    scores = jnp.where(member, scores, NEGATIVE)
    weights = jnp.exp(scores - jnp.max(scores, axis=-1, keepdims=True))
    probs = weights / jnp.sum(weights, axis=-1, keepdims=True)
    mixed = fold_heads(nn(probs.astype(B16), v), heads).astype(B16)
    part_out[...] = nn(mixed, wo[...]).astype(B16)


def pair_of(saved, pair, width):
    start = pair * 2 * E
    return [saved[:, i * width + start : i * width + start + 2 * E] for i in range(3)]


def attend_kernel(
    g, heads, saved, latents, part_one, part_two, gain, wk, wv,
    o_out, probs_out, side_out, mid_out, mid_low_out,
):
    mid = latents[...].astype(F32) + (part_one[...].astype(F32) + part_two[...].astype(F32))
    mid_out[...] = mid
    mid_low_out[...] = mid.astype(B16)
    unit, _ = norm_parts(mid[g * L : (g + 1) * L])
    side_low = (unit * gain[...]).astype(B16)
    side_k = nn(side_low, wk[...]).astype(B16).astype(F32)
    side_v = nn(side_low, wv[...]).astype(B16).astype(F32)
    width = side_k.shape[1]
    side_out[:, :width] = side_k
    side_out[:, width : 2 * width] = side_v
    side_out[:, 2 * width :] = side_low.astype(F32)
    side_v = spread_heads(side_v, heads).astype(B16)
    side_scores = nt(spread_heads(side_k, heads).astype(B16), saved[:, :width])
    scale = FACTOR * LOG2E
    outs, side_probs, lses = [], [], []
    for pair in range(heads // 2):
        q_pair, k_pair, v_pair = pair_of(saved, pair, width)
        for second in (0, 1):
            h = 2 * pair + second
            scores = nt(head_only(k_pair, second), q_pair)
            side = side_scores[h * L : (h + 1) * L]
            top = jnp.maximum(
                jnp.max(scores, axis=0, keepdims=True), jnp.max(side, axis=0, keepdims=True)
            )
            weights = jnp.exp2((scores - top) * scale)
            side = jnp.exp2((side - top) * scale)
            total = jnp.sum(weights, axis=0, keepdims=True) + jnp.sum(side, axis=0, keepdims=True)
            inverse = 1.0 / total
            side_probs.append(side * inverse)
            lses.append(top * scale + jnp.log2(total))
            outs.append(tn((weights * inverse).astype(B16), v_pair))
    side_probs = jnp.concatenate(side_probs, axis=0)
    probs_out[: heads * L, :] = side_probs
    probs_out[heads * L :, :] = jnp.concatenate(
        lses + [jnp.zeros_like(lses[0])] * (8 - heads), axis=0
    )
    side_o = tn(side_probs.astype(B16), side_v)
    first = half_mask(2 * E)
    token_o = jnp.concatenate(
        [jnp.where(first, outs[2 * i], outs[2 * i + 1]) for i in range(heads // 2)], axis=1
    )
    o_out[...] = (token_o + side_o).astype(B16)


def feed_kernel(
    g, chunk, extra, place, tokens, o, o_two, wo, wo_two, cotangent, gain, up, up_bias, down, *rest
):
    earlier, outs = rest[:extra], rest[extra:]
    part_outs, outs = outs[:-7], outs[-7:]
    active_out, hidden_grad_out, low_out, middle_out, down_part_out, up_bias_out, down_bias_out = outs
    rows = slice(g * S, (g + 1) * S)
    first = place[0] == 0
    o_first = jnp.where(first, o[...], o_two[...])
    o_second = jnp.where(first, o_two[...], o[...])
    wo_first = jnp.where(first, wo[...], wo_two[...])
    wo_second = jnp.where(first, wo_two[...], wo[...])
    middle = tokens[rows, :].astype(F32) + (nn(o_first, wo_first) + nn(o_second, wo_second))
    middle_out[...] = middle
    unit, _ = norm_parts(middle)
    low = (unit * gain[...]).astype(B16)
    low_out[...] = low
    outer = cotangent[rows, :]
    down_bias_out[...] = jnp.sum(outer.astype(F32), axis=0, keepdims=True)
    part, down_part = None, None
    for start in range(0, up.shape[1], chunk):
        cut = slice(start, start + chunk)
        hidden = nn(low, up[:, cut]) + up_bias[:, cut]
        active, slope = gelu_both(hidden)
        active = active.astype(B16)
        active_out[:, cut] = active
        grad = (slope * nt(outer, down[cut, :])).astype(B16)
        hidden_grad_out[:, cut] = grad
        up_bias_out[:, cut] = jnp.sum(grad.astype(F32), axis=0, keepdims=True)
        one = nt(grad, up[:, cut])
        two = nn(active, down[cut, :])
        part = one if part is None else part + one
        down_part = two if down_part is None else down_part + two
    at = 0
    for out in part_outs:
        out[...] = part[at : at + out.shape[0]].astype(B16)
        at += out.shape[0]
    for i, r in enumerate(earlier):
        down_part_out[i * S : (i + 1) * S, :] = r[...]
    down_part_out[len(earlier) * S :, :] = down_part.astype(B16)


def turn_kernel(
    g, heads, cuts, cotangent, middle, gain, wo, wk, wv, o, saved, probs, side, mid, *rest
):
    parts, rest = rest[: 2 * cuts], rest[2 * cuts :]
    earlier, outs = rest[:g], rest[g:]
    o_grad_out, delta_out, side_score_grad_out, part_out, grads_out, gain_out = outs[:6]
    middle_grad_out, middle_low_out = outs[6:]
    unit, rate = norm_parts(middle[...])
    sides = [jnp.concatenate([r[...] for r in rs], axis=0) for rs in (parts[:cuts], parts[cuts:])]
    grad = sides[0].astype(F32) + sides[1].astype(F32)
    gain_out[0:1, :] = jnp.sum(grad * unit, axis=0, keepdims=True)
    outer = cotangent[g * S : (g + 1) * S, :].astype(F32)
    middle_grad = outer + norm_back(grad, unit, rate, gain[...])
    middle_grad_out[...] = middle_grad
    middle_low = middle_grad.astype(B16)
    middle_low_out[...] = middle_low
    o_grad = nt(middle_low, wo[...]).astype(B16)
    o_grad_out[...] = o_grad
    width = o_grad.shape[1]
    rows8 = lax.broadcasted_iota(jnp.int32, (8, width), 0)
    columns8 = lax.broadcasted_iota(jnp.int32, (8, width), 1) // E
    pick = (rows8 == columns8).astype(B16)
    weighted = o_grad.astype(F32) * o[...].astype(F32)
    high = weighted.astype(B16)
    low = (weighted - high.astype(F32)).astype(B16)
    delta = nt(pick, high) + nt(pick, low)
    delta_out[...] = delta
    side_v = spread_heads(side[:, width : 2 * width], heads).astype(B16)
    side_prob_grad = nt(side_v, o_grad)
    side_probs = probs[: heads * L, :]
    wide = jnp.concatenate(
        [jnp.broadcast_to(delta[h : h + 1], (L, delta.shape[1])) for h in range(heads)], axis=0
    )
    score_grad = (side_probs * (side_prob_grad - wide)).astype(B16)
    side_score_grad_out[...] = score_grad
    k_grad = (fold_heads(nn(score_grad, saved[:, :width]), heads) * FACTOR).astype(B16)
    v_grad = fold_heads(nn(side_probs.astype(B16), o_grad), heads).astype(B16)
    grads_out[:, :width] = k_grad.astype(F32)
    grads_out[:, width:] = v_grad.astype(F32)
    part = nt(k_grad, wk[...]) + nt(v_grad, wv[...])
    side_unit, _ = norm_parts(mid[g * L : (g + 1) * L, :])
    gain_out[1:2, :] = jnp.sum(part * side_unit, axis=0, keepdims=True)
    gain_out[2:, :] = jnp.zeros_like(gain_out[2:, :])
    part = jnp.concatenate([r[...] for r in earlier] + [part], axis=0)
    part_out[...] = part.astype(part_out.dtype)


def side_kernel(part_one, part_two, mid, cotangent, gain, low_out, grad_out):
    unit, rate = norm_parts(mid[...])
    part = part_one[...].astype(F32) + part_two[...].astype(F32)
    grad = cotangent[...].astype(F32) + norm_back(part, unit, rate, gain[...])
    grad_out[...] = grad
    low_out[...] = grad.astype(B16)


def attend_back_kernel(
    g, heads, tokens, saved, o_grad, probs, delta, side_score_grad, side, wq, wk, wv, *rest
):
    part_out, grads_out, gain_out = rest[-3:]
    gains, earlier = rest[: min(g, 1) + 1], rest[min(g, 1) + 1 : -3]
    scale = FACTOR * LOG2E
    first = half_mask(2 * E)
    width = o_grad.shape[1]
    side_k = spread_heads(side[:, :width], heads).astype(B16)
    side_q_grad = tn(side_score_grad[...], side_k)
    at = heads * L
    for pair in range(heads // 2):
        start = pair * 2 * E
        cut = slice(start, start + 2 * E)
        q_pair, k_pair, v_pair = pair_of(saved, pair, width)
        grad_pair = o_grad[:, cut]
        q_grads, k_grads, v_grads = [], [], []
        for second in (0, 1):
            h = 2 * pair + second
            scores = nt(head_only(k_pair, second), q_pair)
            weights = jnp.exp2(scores * scale - probs[at + h : at + h + 1, :])
            prob_grad = nt(head_only(v_pair, second), grad_pair)
            score_grad = (weights * (prob_grad - delta[h : h + 1, :])).astype(B16)
            v_grads.append(nn(weights.astype(B16), grad_pair))
            k_grads.append(nn(score_grad, q_pair))
            q_grads.append(tn(score_grad, k_pair))
        q_pair_grad = jnp.where(first, q_grads[0], q_grads[1]) + side_q_grad[:, cut]
        k_pair_grad = jnp.where(first, k_grads[0], k_grads[1])
        v_pair_grad = jnp.where(first, v_grads[0], v_grads[1])
        grads_out[:, start : start + 2 * E] = (q_pair_grad * FACTOR).astype(B16)
        grads_out[:, width + start : width + start + 2 * E] = (k_pair_grad * FACTOR).astype(B16)
        grads_out[:, 2 * width + start : 2 * width + start + 2 * E] = v_pair_grad.astype(B16)
    part = nt(grads_out[:, :width], wq[...]) + nt(grads_out[:, width : 2 * width], wk[...])
    part = part + nt(grads_out[:, 2 * width :], wv[...])
    for i, r in enumerate(earlier):
        part_out[i * S : (i + 1) * S, :] = r[...]
    part_out[len(earlier) * S :, :] = part.astype(B16)
    unit, _ = norm_parts(tokens[g * S : (g + 1) * S, :].astype(F32))
    total = gains[0][1:2, :] + jnp.sum(part * unit, axis=0, keepdims=True)
    for r in gains[1:]:
        total = total + r[...]
    gain_out[...] = total


def leave_kernel(tokens, gain, part_one, part_two, *refs):
    middle_grad, grad_out = refs[:-1], refs[-1]
    for g in range(len(middle_grad)):
        rows = slice(g * S, (g + 1) * S)
        unit, rate = norm_parts(tokens[rows, :].astype(F32))
        grad = part_one[rows, :].astype(F32) + part_two[rows, :].astype(F32)
        grad_out[rows, :] = middle_grad[g][...] + norm_back(grad, unit, rate, gain[...])


def result_kernel(bias, part_one, part_two, *refs):
    middle, out = refs[:-1], refs[-1]
    for g in range(len(middle)):
        rows = slice(g * S, (g + 1) * S)
        total = part_one[rows, :].astype(F32) + part_two[rows, :].astype(F32)
        out[rows, :] = (middle[g][...] + total + bias[...]).astype(B16)


def latent_leave_kernel(me, latents, part_one, part_two, gain, mid_grad, grad_out, gain_out):
    own = latents.shape[0]
    unit, rate = norm_parts(latents[...].astype(F32))
    total = part_one[...].astype(F32) + part_two[...].astype(F32)
    grad_out[...] = mid_grad[...] + norm_back(total[:own], unit, rate, gain[...])
    share, model = gain_out.shape[1], gain.shape[1]
    row = lax.broadcasted_iota(jnp.int32, (share, model), 0)
    column = lax.broadcasted_iota(jnp.int32, (share, model), 1)
    kept = jnp.where(column == row + me[0] * share, total[own : own + 1], 0.0)
    gain_out[...] = jnp.broadcast_to(jnp.sum(kept, axis=1, keepdims=True), (share, 8)).T


def split_pairs(values, bit, share, send_out, keep_out, cut, keep_cut=None):
    blocks = values.reshape(values.shape[0] // (2 * share), 2, share, values.shape[1])
    even, odd = blocks[:, 0], blocks[:, 1]
    send_out[:, :, cut] = jnp.where(bit == 0, odd, even).astype(B16)
    keep_cut = cut if keep_cut is None else keep_cut
    keep_out[:, :, keep_cut] = jnp.where(bit == 0, even, odd).astype(B16)


def weight_grad_kernel(groups, share, down_pieces, up_pieces, me, cotangent, *refs):
    active, low, hidden_grad = (refs[i * groups : (i + 1) * groups] for i in range(3))
    outs = refs[3 * groups :]
    down_sends, up_sends = outs[:down_pieces], outs[down_pieces:-2]
    down_keep, up_keep = outs[-2:]
    bit = me[0] % 2
    width = active[0].shape[1]
    flat = [cotangent[g * S : (g + 1) * S, :].T for g in range(groups)]
    low_flat = [r[...].T for r in low]

    def total_of(lefts, rights, cut):
        total = nn(lefts[0], rights[0][:, cut])
        for g in range(1, groups):
            total = total + nn(lefts[g], rights[g][:, cut])
        return total

    chunk = width // down_pieces
    for k in range(down_pieces):
        cut = slice(k * chunk, (k + 1) * chunk)
        total = total_of(flat, active, cut)
        split_pairs(total, bit, share, down_sends[k], down_keep, slice(0, chunk), cut)
    chunk = width // up_pieces
    for k in range(up_pieces):
        cut = slice(k * chunk, (k + 1) * chunk)
        total = total_of(low_flat, hidden_grad, cut)
        split_pairs(total, bit, share, up_sends[k], up_keep, slice(0, chunk), cut)


def attention_grad_kernel(groups, share, me, gain_one, gain_two, *refs):
    saved, grads, middle_low, o, side, side_grads, up_bias, down_bias, gains = (
        refs[i * groups : (i + 1) * groups] for i in range(9)
    )
    *send_outs, keep_out = refs[9 * groups :]
    bit = me[0] % 2
    width = o[0].shape[1]
    model = middle_low[0].shape[1]
    stack = [jnp.concatenate([r[...] for r in rs], axis=0) for rs in (side, side_grads)]
    side_low = stack[0][:, 2 * width :].astype(B16)
    side_k, side_v = stack[1][:, :width].astype(B16), stack[1][:, width:].astype(B16)
    flat = [r[:, 3 * width :].T for r in saved]
    low_flat = [r[...].T for r in middle_low]

    def total_of(lefts, rights, cut):
        total = nn(lefts[0], rights[0][:, cut])
        for g in range(1, groups):
            total = total + nn(lefts[g], rights[g][:, cut])
        return total

    def cut_of(i):
        return slice(i * width, (i + 1) * width)

    totals = (
        total_of(flat, grads, cut_of(0)),
        total_of(flat, grads, cut_of(1)) + tn(side_low, side_k),
        total_of(flat, grads, cut_of(2)) + tn(side_low, side_v),
        total_of(low_flat, o, cut_of(0)),
    )
    for i, total in enumerate(totals):
        split_pairs(total, bit, share, send_outs[i], keep_out, cut_of(0), cut_of(i))

    def column(rows):
        return jnp.broadcast_to(rows, (8, rows.shape[1])).T

    def sum_of(parts):
        total = parts[0]
        for part in parts[1:]:
            total = total + part
        return total

    columns = [
        column(sum_of([r[...] for r in down_bias])),
        column(sum_of([r[0:1, :] for r in gains])),
        column(gain_one[...] + gain_two[...]),
    ]
    bias = column(sum_of([r[...] for r in up_bias]))
    times = bias.shape[0] // model
    bias = bias.reshape(model // share, times, share, 8)
    columns += [bias[:, i].reshape(model, 8) for i in range(times)]
    lane = lax.broadcasted_iota(jnp.int32, (model, 128), 1)
    block = jnp.zeros((model, 128), F32)
    for i, one in enumerate(columns):
        block = jnp.where(lane == i, one[:, 0:1], block)
    cut = slice(width, width + 128)
    split_pairs(block, bit, share, send_outs[3], keep_out, cut, slice(4 * width, 4 * width + 128))


def halve_kernel(shift, pieces, cuts, me, keep, *refs):
    gots, outs = refs[: len(pieces)], refs[len(pieces) :]
    bit = (me[0] // shift) % 2
    for got, (first, last) in zip(gots, pieces):
        for k, (start, end) in enumerate(cuts):
            low, high = max(first, start), min(last, end)
            if low >= high:
                continue
            of_got, of_out = slice(low - first, high - first), slice(low - start, high - start)
            for i in range(keep.shape[0]):
                there, here = (
                    keep[i, pl.ds(at, 1), :, low:high].astype(F32)
                    + got[i, pl.ds(at, 1), :, of_got].astype(F32)
                    for at in (1 - bit, bit)
                )
                outs[2 * k][pl.ds(i, 1), :, of_out] = there.astype(B16)
                outs[2 * k + 1][pl.ds(i, 1), :, of_out] = here


def finish_kernel(cuts, keep, got, *outs):
    total = keep[0] + got[0].astype(F32)
    for out, (start, end, flat) in zip(outs, cuts):
        part = total[:, start:end]
        out[...] = part.T[: out.shape[0]] if flat else part


def latent_back_kernel(
    heads, own, order, block, me, group_image, latents, q, k, v, mid_one, mid_two, gain, wq, wk, wv, wo,
    part_out, wq_out, wk_out, wv_out, wo_out, mixed, q_grad, k_grad, v_grad, images,
):
    mid_low = jnp.concatenate([mid_one[...], mid_two[...]], axis=0)
    o_grad = nt(mid_low, wo[...]).astype(B16)
    unit, _ = norm_parts(latents[...].astype(F32))
    low = (unit * gain[...]).astype(B16)
    everyone = low.shape[0]
    images_row, images_column = image_rows(order, own // L, me[0], group_image)

    def rows_of(start, ref_q, ref_grad, ref_images):
        wide_q = spread_heads(ref_q, heads)
        wide_grad = spread_heads(ref_grad, heads)
        scores = nt(wide_q, k[...]) * FACTOR
        member = jnp.concatenate([ref_images] * heads, axis=0) == images_row
        scores = jnp.where(member, scores, NEGATIVE)
        weights = jnp.exp(scores - jnp.max(scores, axis=-1, keepdims=True))
        probs = weights / jnp.sum(weights, axis=-1, keepdims=True)
        probs_low = probs.astype(B16)
        prob_grad = nt(wide_grad, v[...])
        delta = jnp.sum(prob_grad * probs, axis=-1, keepdims=True)
        score_grad = (probs * (prob_grad - delta)).astype(B16)
        mixed[pl.ds(start, block), :] = fold_heads(nn(probs_low, v[...]), heads).astype(B16)
        q_grad[pl.ds(start, block), :] = (
            fold_heads(nn(score_grad, k[...]), heads) * FACTOR
        ).astype(B16)
        return tn(score_grad, wide_q), tn(probs_low, wide_grad)

    if block == everyone:
        k_sum, v_sum = rows_of(0, q[...], o_grad, images_column)
        k_sum, v_sum = k_sum * FACTOR, v_sum
    else:
        v_grad[...] = o_grad
        images[...] = jnp.broadcast_to(images_column, images.shape)

        def step(i, held):
            start = pl.multiple_of(i * block, block)
            here = pl.ds(start, block)
            one, two = rows_of(start, q[here, :], v_grad[here, :], images[here, :][:, :1])
            return held[0] + one, held[1] + two

        zero = jnp.zeros(k.shape, F32)
        k_sum, v_sum = lax.fori_loop(0, everyone // block, step, (zero, zero))
        k_sum = k_sum * FACTOR
    k_grad[...] = k_sum.astype(B16)
    v_grad[...] = v_sum.astype(B16)
    part = nt(q_grad[...], wq[...]) + nt(k_grad[...], wk[...]) + nt(v_grad[...], wv[...])
    gain_part = jnp.sum(part * unit, axis=0, keepdims=True)
    part_out[...] = jnp.concatenate(
        [part[:own], jnp.broadcast_to(gain_part, (16, part.shape[1]))], axis=0
    ).astype(B16)
    share = wq_out.shape[0]
    model = low.shape[1]
    row = lax.broadcasted_iota(jnp.int32, (share, model), 0)
    column = lax.broadcasted_iota(jnp.int32, (share, model), 1)
    pick = (column == row + me[0] * share).astype(B16)
    columns = nt(pick, low).astype(B16)
    wq_out[...] = nn(columns, q_grad[...])
    wk_out[...] = nn(columns, k_grad[...])
    wv_out[...] = nn(columns, v_grad[...])
    wo_out[...] = nn(nt(pick, mid_low).astype(B16), mixed[...])


MIB = 1024 * 1024
OUT = "out"


class Order:
    def __init__(self, pinned):
        self.pinned, self.last = pinned, None

    def call(self, kernel, name, outs, ins, scratch=(), limit=16, behind=()):
        scalars = [isinstance(a, tuple) for a in ins]
        arrays = [a[1] if isinstance(a, tuple) else a for a in ins]
        earlier = tuple(behind) + (() if self.last is None else (self.last,))
        if earlier:
            least = min(range(len(arrays)), key=lambda i: arrays[i].size)
            arrays[least] = after(arrays[least], *earlier)
        if self.pinned:
            arrays = [
                a if scalar else pltpu.with_memory_space_constraint(a, pltpu.VMEM)
                for a, scalar in zip(arrays, scalars)
            ]

        def result(shape, dtype, kind=None):
            if self.pinned and kind != OUT:
                return pltpu.VMEM(shape, dtype)
            return jax.ShapeDtypeStruct(shape, dtype)

        def whole(shape):
            return pl.BlockSpec(tuple(shape), lambda: (0,) * len(shape))

        results = pl.pallas_call(
            kernel,
            out_shape=[result(*out) for out in outs],
            in_specs=[
                pl.BlockSpec(memory_space=pltpu.SMEM) if scalar else whole(a.shape)
                for a, scalar in zip(arrays, scalars)
            ],
            out_specs=[whole(out[0]) for out in outs],
            scratch_shapes=list(scratch),
            compiler_params=pltpu.CompilerParams(vmem_limit_bytes=limit * MIB),
            cost_estimate=pl.CostEstimate(flops=0, bytes_accessed=0, transcendentals=0),
            name=name,
        )(*arrays)
        self.last = min(results, key=lambda a: a.size)
        return results

    def load(self, *arrays, behind=()):
        if not self.pinned:
            return arrays
        sources = list(arrays)
        earlier = tuple(behind) + (() if self.last is None else (self.last,))
        if earlier:
            sources[0] = after(sources[0], *earlier)
        results = pl.pallas_call(
            load_kernel,
            out_shape=[pltpu.VMEM(a.shape, a.dtype) for a in arrays],
            in_specs=[pl.BlockSpec(memory_space=pltpu.HBM)] * len(arrays),
            out_specs=[pl.BlockSpec(memory_space=pltpu.VMEM)] * len(arrays),
            scratch_shapes=[pltpu.SemaphoreType.DMA((len(arrays),))],
            compiler_params=pltpu.CompilerParams(vmem_limit_bytes=MIB),
            cost_estimate=pl.CostEstimate(flops=0, bytes_accessed=0, transcendentals=0),
            name="load",
        )(*[pltpu.with_memory_space_constraint(a, pltpu.HBM) for a in sources])
        self.last = min(results, key=lambda a: a.size)
        return results


def after(value, *earlier):
    return lax.optimization_barrier((value, earlier))[0]


def swap_tp(values, name):
    with jax.named_scope("swap_" + name):
        return lax.ppermute(values, "tp", [(0, 1), (1, 0)])


def flip(values, bits, name):
    size = lax.axis_size("dp")
    with jax.named_scope("flip_" + name):
        return lax.ppermute(values, "dp", [(i, i ^ bits) for i in range(size)])


def gather_steps(size):
    width, steps = 2, []
    while width * 4 < size:
        steps.append([width])
        width *= 2
    if width < size:
        steps.append([width * k for k in range(1, size // width)])
    steps.reverse()
    return steps + [[1]]


def gather_order(size):
    order = [0]
    for step in gather_steps(size):
        order = order + [i ^ bits for bits in [0] + step for i in order][len(order) :]
    return order


def scatter_sum(grads):
    size = lax.axis_size("dp")
    me = lax.axis_index("dp")
    width = 1
    while width * 4 < size:
        bit = (me // width) % 2
        pairs = grads.reshape((grads.shape[0] // 2, 2) + grads.shape[1:])
        send = lax.dynamic_index_in_dim(pairs, 1 - bit, 1, keepdims=False)
        keep = lax.dynamic_index_in_dim(pairs, bit, 1, keepdims=False)
        got = flip(send.astype(B16), width, "sums")
        grads = keep.astype(F32) + got.astype(F32)
        width *= 2
    place = me // width
    total = lax.dynamic_index_in_dim(grads, place, 0, keepdims=False)
    for k in range(1, size // width):
        send = lax.dynamic_index_in_dim(grads, place ^ k, 0, keepdims=False)
        total = total + flip(send.astype(B16), width * k, "sums").astype(F32)
    return total


class Scatter:
    def __init__(self, order, me, width, keep, send, name):
        self.order, self.me, self.width, self.name = order, me, width, name
        sends = send if isinstance(send, list) else [send]
        self.keep, self.gots, self.pieces, at = keep, [flip(a, width, name) for a in sends], [], 0
        for a in sends:
            self.pieces.append((at, at + a.shape[2]))
            at += a.shape[2]

    def halve(self, cuts, behind=()):
        n, share, _ = self.keep.shape
        four = (n // 2, 2) + self.keep.shape[1:]
        shapes = [(n // 2, share, end - start) for start, end in cuts]
        results = self.order.call(
            partial(halve_kernel, 2 * self.width, self.pieces, cuts),
            "halve",
            [out for shape in shapes for out in ((shape, B16), (shape, F32))],
            [("smem", self.me), self.keep.reshape(four)]
            + [a.reshape((n // 2, 2) + a.shape[1:]) for a in self.gots],
            behind=behind,
        )
        return results[::2], results[1::2]

    def next(self, send, keep, name, *ties):
        send = after(send, *ties) if ties else send
        return Scatter(self.order, self.me, 2 * self.width, keep, send, name)

    def whole(self):
        return [(0, self.keep.shape[2])]

    def finish(self, cuts):
        share = self.keep.shape[1]
        shapes = [(8, share) if flat else (share, e - s) for s, e, flat in cuts]
        return self.order.call(
            partial(finish_kernel, cuts),
            "finish",
            [(shape, F32, OUT) for shape in shapes],
            [self.keep, self.gots[0]],
        )


def local(
    tokens,
    latents,
    latent_query,
    latent_key,
    latent_value,
    latent_output,
    query_weight,
    key_weight,
    value_weight,
    output_weight,
    up_weight,
    up_bias,
    down_weight,
    down_bias,
    latent_gain,
    attention_gain,
    feed_gain,
    group_image,
    token_cotangent,
    latent_cotangent,
):
    size = lax.axis_size("dp")
    me = lax.axis_index("dp")
    me_row = me.reshape(1)
    place = lax.axis_index("tp").reshape(1)
    width = latent_query.shape[1]
    heads = width // E
    rows, model = tokens.shape
    hidden_units = up_weight.shape[1]
    groups = rows // S
    own = latents.shape[0]
    everyone = own * size
    share = model // size
    small = everyone <= 512
    aligned = share % 16 == 0 and size >= 8
    each = range(groups)
    latent_gain_row = latent_gain.reshape(1, model)
    attention_gain_row = attention_gain.reshape(1, model)
    feed_gain_row = feed_gain.reshape(1, model)
    up_bias_row = up_bias.reshape(1, hidden_units)
    down_bias_row = down_bias.reshape(1, model)
    chain = Order(small)
    call = chain.call
    latent_limit = 16 if small else 56

    def join(parts):
        if not small:
            return jnp.concatenate(parts, axis=0)
        shape = (sum(p.shape[0] for p in parts), model)
        return call(join_kernel, "join", [(shape, B16)], parts)[0]

    output_weight_two = swap_tp(output_weight, "output_weight")
    gathered = gather_steps(size)
    scalars = (me_row, place)
    gain_rows = (latent_gain_row, attention_gain_row, feed_gain_row, up_bias_row, down_bias_row)
    gathering = latents
    (
        tokens,
        query_weight,
        key_weight,
        value_weight,
        latents,
        latent_cotangent,
        output_weight,
        *latent_weights,
    ) = chain.load(
        tokens,
        query_weight,
        key_weight,
        value_weight,
        latents,
        latent_cotangent,
        output_weight,
        latent_query,
        latent_key,
        latent_value,
        latent_output,
        behind=scalars + gain_rows,
    )
    held = gathering
    held_steps = []
    for step in gathered[:-1]:
        held = join([held] + [flip(held, b, "latents") for b in step])
        held_steps.append(held)
    turns = tuple(gather_order(size))
    saved = []
    for g in each:
        saved += call(
            partial(enter_kernel, g),
            "enter",
            [((S, 3 * width + model), B16)],
            [tokens, attention_gain_row, query_weight, key_weight, value_weight],
            behind=held_steps[:1] if g == groups - 1 else (),
        )
    latents_one, latents_two = held, flip(after(held, saved[0]), 1, "latents")
    latents_all, lat_q, lat_k, lat_v, latent_part = call(
        partial(latent_kernel, heads, own, turns),
        "latent",
        [((everyone, model), B16)] + [((everyone, width), B16)] * 3 + [((own, model), B16)],
        [
            ("smem", me_row),
            ("smem", group_image),
            latents_one,
            latents_two,
            latent_gain_row,
            *latent_weights,
        ],
        limit=latent_limit,
    )
    latent_part_two = swap_tp(latent_part, "latent_part")
    up_weight, down_weight, token_cotangent = chain.load(up_weight, down_weight, token_cotangent)
    o, probs, side, mids, mid_lows = zip(
        *(
            call(
                partial(attend_kernel, g, heads),
                "attend",
                [
                    ((S, width), B16),
                    ((heads * L + 8, S), F32),
                    ((L, 2 * width + model), F32),
                    ((own, model), F32),
                    ((own, model), B16, OUT),
                ],
                [
                    saved[g],
                    latents,
                    latent_part,
                    latent_part_two,
                    attention_gain_row,
                    key_weight,
                    value_weight,
                ],
            )
            for g in each
        )
    )
    mid, mixed_latents = mids[0], mid_lows[0]
    o_two = [swap_tp(a, "o") for a in o]
    fed = []
    cuts_of = [1 if g == groups - 1 else 2 for g in each]
    for g in each:
        last = g == groups - 1
        fed.append(
            call(
                partial(feed_kernel, g, hidden_units // 3, g if last else 0),
                "feed",
                [((S // cuts_of[g], model), B16)] * cuts_of[g]
                + [
                    ((S, hidden_units), B16),
                    ((S, hidden_units), B16),
                    ((S, model), B16),
                    ((S, model), F32),
                    ((rows if last else S, model), B16),
                    ((1, hidden_units), F32),
                    ((1, model), F32),
                ],
                [
                    ("smem", place),
                    tokens,
                    o[g],
                    o_two[g],
                    output_weight,
                    output_weight_two,
                    token_cotangent,
                    feed_gain_row,
                    up_weight,
                    up_bias_row,
                    down_weight,
                ]
                + ([f[-3] for f in fed] if last else []),
            )
        )
    feed_part = [f[:-7] for f in fed]
    active, hidden_grad, feed_low, middle, down_parts, up_bias_sum, down_bias_sum = zip(
        *(f[-7:] for f in fed)
    )
    down_part = down_parts[-1]
    feed_part_two = [[swap_tp(p, "feed_part") for p in parts] for parts in feed_part]

    def turn(g, earlier):
        last = g == groups - 1
        return call(
            partial(turn_kernel, g, heads, cuts_of[g]),
            "turn",
            [
                ((S, width), B16),
                ((8, S), F32),
                ((heads * L, S), B16),
                ((own if last else L, model), B16 if last else F32),
                ((L, 2 * width), F32),
                ((8, model), F32),
                ((S, model), F32),
                ((S, model), B16),
            ],
            [
                token_cotangent,
                middle[g],
                feed_gain_row,
                output_weight,
                key_weight,
                value_weight,
                o[g],
                saved[g],
                probs[g],
                side[g],
                mid,
            ]
            + list(feed_part[g])
            + feed_part_two[g]
            + earlier,
        )

    if aligned:
        down_pieces, up_pieces = 4, 2
        half = (size // 2, share, hidden_units)
        down_piece = (size // 2, share, hidden_units // down_pieces)
        up_piece = (size // 2, share, hidden_units // up_pieces)
        *sends, down_keep, up_keep = call(
            partial(weight_grad_kernel, groups, share, down_pieces, up_pieces),
            "weight_grad",
            [(down_piece, B16)] * down_pieces + [(up_piece, B16)] * up_pieces + [(half, B16)] * 2,
            [("smem", me_row), token_cotangent] + list(active + feed_low + hidden_grad),
        )
    turned = []
    for g in each:
        turned.append(turn(g, [t[3] for t in turned]))
        if aligned and g == 0:
            down_sends = [after(a, turned[0][1]) for a in sends[:down_pieces]]
            down_sum = Scatter(chain, me_row, 1, down_keep, down_sends, "down_core")
            (send,), (keep,) = down_sum.halve(down_sum.whole())
            down_sum = down_sum.next(send, keep, "down_y")
    (
        o_grad,
        delta,
        side_score_grad,
        side_parts,
        side_grads,
        gains,
        middle_grad,
        middle_low,
    ) = zip(*turned)
    side_part = side_parts[-1]
    side_part_two = swap_tp(side_part, "side_part")
    if aligned:
        up_sends = [after(a, delta[-1]) for a in sends[down_pieces:]]
        up_sum = Scatter(chain, me_row, 1, up_keep, up_sends, "up_core")
    back = []
    for g in each:
        last = g == groups - 1
        back.append(
            call(
                partial(attend_back_kernel, g, heads),
                "attend_back",
                [((rows if last else S, model), B16), ((S, 3 * width), B16), ((1, model), F32)],
                [
                    tokens,
                    saved[g],
                    o_grad[g],
                    probs[g],
                    delta[g],
                    side_score_grad[g],
                    side[g],
                    query_weight,
                    key_weight,
                    value_weight,
                    gains[g],
                ]
                + [b[2] for b in back[-1:]]
                + ([b[0] for b in back] if last else []),
            )
        )
        if g == 0:
            if aligned:
                up_sends, up_keeps = up_sum.halve(up_sum.whole())
            mid_low, middle_latent_grad = call(
                side_kernel,
                "side",
                [((own, model), B16), ((own, model), F32)],
                [side_part, side_part_two, mid, latent_cotangent, attention_gain_row],
            )
    if aligned:
        (send,), (keep,) = down_sum.halve(down_sum.whole())
        up_sum = up_sum.next(up_sends[0], up_keeps[0], "up_y", down_sum.gots[0])
        down_sum = down_sum.next(send, keep, "down_z")
    held = mid_low
    held_steps = []
    for step in gathered[:-1]:
        held = join([held] + [flip(held, b, "mid") for b in step])
        held_steps.append(held)
    mid_low_one, mid_low_two = held, flip(held, 1, "mid")
    token_parts, grads, _ = zip(*back)
    token_part = token_parts[-1]
    gain_sum = back[-1][2]
    gain_two = swap_tp(gain_sum, "gain")
    token_part_two = swap_tp(after(token_part, gain_two), "token_part")
    if aligned:
        columns = 4 * width + 128
        arrays = (saved, grads, middle_low, o, side, side_grads, up_bias_sum, down_bias_sum, gains)
        *rest_sends, rest_keep = call(
            partial(attention_grad_kernel, groups, share),
            "attention_grad",
            [((size // 2, share, n), B16) for n in (width, width, width, width + 128, columns)],
            [("smem", me_row), gain_sum, gain_two] + [a for of_groups in arrays for a in of_groups],
        )
        rest_sum = Scatter(chain, me_row, 1, rest_keep, rest_sends, "rest_core")
    else:

        def flat(arrays, start, end):
            return jnp.concatenate([a[:, start:end] for a in arrays], axis=0).astype(B16)

        token_low = flat(saved, 3 * width, 3 * width + model)
        side_low = flat(side, 2 * width, 2 * width + model)
        products = (
            tn(token_cotangent, flat(active, 0, hidden_units)),
            tn(flat(feed_low, 0, model), flat(hidden_grad, 0, hidden_units)),
            tn(token_low, flat(grads, 0, width)),
            tn(token_low, flat(grads, width, 2 * width)) + tn(side_low, flat(side_grads, 0, width)),
            tn(token_low, flat(grads, 2 * width, 3 * width))
            + tn(side_low, flat(side_grads, width, 2 * width)),
            tn(flat(middle_low, 0, model), flat(o, 0, width)),
        )
        vectors = [sum(down_bias_sum), sum(gains)[:1], gain_sum + gain_two]
        vectors.append(sum(up_bias_sum).reshape(size, -1, share).swapaxes(0, 1).reshape(-1, model))
        vectors = jnp.concatenate(vectors, axis=0)
        total = jnp.concatenate([a.astype(B16) for a in products + (vectors.T,)], axis=1)
        total = scatter_sum(total.reshape(size, share, -1))
    block = min(everyone, max(16, 65536 // everyone))
    latent_sum, latent_query_done, latent_key_done, latent_value_done, latent_output_done = call(
        partial(latent_back_kernel, heads, own, turns, block),
        "latent_back",
        [((own + 16, model), B16)] + [((share, width), F32, OUT)] * 4,
        [
            ("smem", me_row),
            ("smem", group_image),
            latents_all,
            lat_q,
            lat_k,
            lat_v,
            mid_low_one,
            mid_low_two,
            latent_gain_row,
            *latent_weights,
        ],
        scratch=[pltpu.VMEM((everyone, width), B16)] * 4 + [pltpu.VMEM((everyone, 128), F32)],
        limit=latent_limit,
    )
    latent_sum_two = swap_tp(latent_sum, "latent_sum")
    down_part_two = swap_tp(after(down_part, latent_sum), "down_part")
    if aligned:
        cuts = [(0, 2 * width), (2 * width, columns)]
        rest_sends, rest_keeps = rest_sum.halve(cuts)
        (send,), (keep,) = down_sum.halve(down_sum.whole())
        down_sum = down_sum.next(send, keep, "down_zz")
        (send,), (keep,) = up_sum.halve(up_sum.whole())
        first = rest_sum.next(rest_sends[0], rest_keeps[0], "first_y", up_sum.gots[0])
        up_sum = up_sum.next(send, keep, "up_z")
    (token_grad,) = call(
        leave_kernel,
        "leave",
        [((rows, model), F32, OUT)],
        [tokens, attention_gain_row, token_part, token_part_two] + list(middle_grad),
    )
    latent_grad, latent_gain_sum = call(
        latent_leave_kernel,
        "latent_leave",
        [((own, model), F32, OUT), ((8, share), F32, OUT)],
        [("smem", me_row), latents, latent_sum, latent_sum_two, latent_gain_row, middle_latent_grad],
    )
    if aligned:
        (down_done,) = down_sum.finish([(0, hidden_units, False)])
        (send,), (keep,) = up_sum.halve(up_sum.whole())
        up_sum = up_sum.next(send, keep, "up_zz")
        (send,), (keep,) = first.halve(first.whole())
        second = rest_sum.next(rest_sends[1], rest_keeps[1], "second_y", first.gots[0])
        first = first.next(send, keep, "first_z")
    (mixed_tokens,) = call(
        result_kernel,
        "result",
        [((rows, model), B16, OUT)],
        [down_bias_row, down_part, down_part_two] + list(middle),
    )
    if aligned:
        (up_done,) = up_sum.finish([(0, hidden_units, False)])
        (send,), (keep,) = first.halve(first.whole())
        first = first.next(send, keep, "first_zz")
        (send,), (keep,) = second.halve(second.whole())
        second = second.next(send, keep, "second_z")
        query_done, key_done = first.finish([(0, width, False), (width, 2 * width, False)])
        (send,), (keep,) = second.halve(second.whole())
        second = second.next(send, keep, "second_zz")
        cuts = [(0, width, False), (width, 2 * width, False), (2 * width, 2 * width + 128, True)]
        value_done, output_done, vectors = second.finish(cuts)
    else:
        ends = [hidden_units, 2 * hidden_units] + [2 * hidden_units + i * width for i in range(1, 5)]
        down_done, up_done, query_done, key_done, value_done, output_done, vectors = jnp.split(
            total, ends, axis=1
        )
        vectors = vectors.T
    return (
        mixed_tokens,
        mixed_latents,
        token_grad,
        latent_grad,
        latent_query_done,
        latent_key_done,
        latent_value_done,
        latent_output_done.T,
        query_done,
        key_done,
        value_done,
        output_done.T,
        up_done,
        vectors[3 : 3 + hidden_units // model].reshape(-1),
        down_done.T,
        vectors[0],
        latent_gain_sum[0],
        vectors[2],
        vectors[1],
    )


def solution(mesh):
    placed = (
        P("dp", None),
        P("dp", None),
        P(None, "tp"),
        P(None, "tp"),
        P(None, "tp"),
        P("tp", None),
        P(None, "tp"),
        P(None, "tp"),
        P(None, "tp"),
        P("tp", None),
        P(None, "tp"),
        P("tp"),
        P("tp", None),
        P(),
        P(),
        P(),
        P(),
        P(),
        P("dp", None),
        P("dp", None),
    )
    return jax.shard_map(
        local,
        mesh=mesh,
        in_specs=placed,
        out_specs=(
            P("dp", None),
            P("dp", None),
            P("dp", None),
            P("dp", None),
            P("dp", "tp"),
            P("dp", "tp"),
            P("dp", "tp"),
            P("tp", "dp"),
            P("dp", "tp"),
            P("dp", "tp"),
            P("dp", "tp"),
            P("tp", "dp"),
            P("dp", "tp"),
            P(("tp", "dp")),
            P("tp", "dp"),
            P("dp"),
            P("dp"),
            P("dp"),
            P("dp"),
        ),
        check_vma=False,
    )
```

```python
from functools import partial

import jax
import jax.numpy as jnp
from jax import lax
from jax.experimental import pallas as pl
from jax.experimental.pallas import tpu as pltpu
from jax.sharding import PartitionSpec as P

E = 64
S = 256
L = 8
EPSILON = 1e-05
NEGATIVE = -1000000000.0
FACTOR = E ** (-0.5)
LOG2E = 1.4426950408889634
F32 = jnp.float32
B16 = jnp.bfloat16


def nn(left, right):
    return lax.dot_general(left, right, (((1,), (0,)), ((), ())), preferred_element_type=F32)


def nt(left, right):
    return lax.dot_general(left, right, (((1,), (1,)), ((), ())), preferred_element_type=F32)


def tn(left, right):
    return lax.dot_general(left, right, (((0,), (0,)), ((), ())), preferred_element_type=F32)


def norm_parts(values):
    average = jnp.mean(values, axis=-1, keepdims=True)
    centred = values - average
    spread = jnp.mean(centred * centred, axis=-1, keepdims=True)
    rate = lax.rsqrt(spread + EPSILON)
    return centred * rate, rate


def norm_back(grad, unit, rate, gain):
    scaled = grad * gain
    first = jnp.mean(scaled, axis=-1, keepdims=True)
    second = jnp.mean(scaled * unit, axis=-1, keepdims=True)
    return rate * (scaled - first - unit * second)


def gelu_both(values):
    square = values * values
    wave = jnp.tanh(0.7978845608028654 * values * (1.0 + 0.044715 * square))
    slope = 0.7978845608028654 * (1.0 + 0.134145 * square)
    half = 0.5 * (1.0 + wave)
    return values * half, half + 0.5 * values * (1.0 - wave * wave) * slope


def head_mask(heads, rows, width):
    row = lax.broadcasted_iota(jnp.int32, (heads * rows, width), 0)
    column = lax.broadcasted_iota(jnp.int32, (heads * rows, width), 1)
    return (row // rows) == (column // E)


def spread_heads(values, heads):
    rows, width = values.shape
    stacked = jnp.concatenate([values] * heads, axis=0)
    return jnp.where(head_mask(heads, rows, width), stacked, jnp.zeros_like(stacked))


def fold_heads(values, heads):
    rows, width = values.shape[0] // heads, values.shape[1]
    kept = jnp.where(head_mask(heads, rows, width), values, jnp.zeros_like(values))
    total = kept[:rows]
    for h in range(1, heads):
        total = total + kept[h * rows : (h + 1) * rows]
    return total


def half_mask(width):
    return lax.broadcasted_iota(jnp.int32, (1, width), 1) < E


def head_only(values, second):
    mask = half_mask(values.shape[1])
    zero = jnp.zeros_like(values)
    return jnp.where(mask, zero, values) if second else jnp.where(mask, values, zero)


def load_kernel(*refs):
    count = (len(refs) - 1) // 2
    ready = refs[-1]
    copies = [
        pltpu.make_async_copy(refs[i], refs[count + i], ready.at[i]) for i in range(count)
    ]
    for copy in copies:
        copy.start()
    for copy in copies:
        copy.wait()


def join_kernel(*refs):
    at = 0
    for r in refs[:-1]:
        refs[-1][at : at + r.shape[0], :] = r[...]
        at += r.shape[0]


def enter_kernel(g, tokens, gain, wq, wk, wv, saved_out):
    unit, _ = norm_parts(tokens[g * S : (g + 1) * S, :].astype(F32))
    low = (unit * gain[...]).astype(B16)
    width = wq.shape[1]
    saved_out[:, :width] = nn(low, wq[...]).astype(B16)
    saved_out[:, width : 2 * width] = nn(low, wk[...]).astype(B16)
    saved_out[:, 2 * width : 3 * width] = nn(low, wv[...]).astype(B16)
    saved_out[:, 3 * width :] = low


def image_rows(order, groups, me, group_image):
    count = len(order) * groups * L
    lane = lax.broadcasted_iota(jnp.int32, (8, count), 1) // L
    images = jnp.zeros((8, count), F32)
    for j, bits in enumerate(order):
        for g in range(groups):
            image = group_image[(me ^ bits) * groups + g].astype(F32)
            images = jnp.where(lane == j * groups + g, image, images)
    return images[:1], images.T[:, :1]


def latent_kernel(
    heads, own, order, me, group_image, one, two, gain, wq, wk, wv, wo, latents_out, q_out, k_out, v_out, part_out
):
    latents = jnp.concatenate([one[...], two[...]], axis=0)
    latents_out[...] = latents
    unit, _ = norm_parts(latents.astype(F32))
    low = (unit * gain[...]).astype(B16)
    q = nn(low, wq[...]).astype(B16)
    k = nn(low, wk[...]).astype(B16)
    v = nn(low, wv[...]).astype(B16)
    q_out[...] = q
    k_out[...] = k
    v_out[...] = v
    scores = nt(spread_heads(q[:own], heads), k) * FACTOR
    images, column = image_rows(order, own // L, me[0], group_image)
    member = jnp.concatenate([column[:own]] * heads, axis=0) == images
    scores = jnp.where(member, scores, NEGATIVE)
    weights = jnp.exp(scores - jnp.max(scores, axis=-1, keepdims=True))
    probs = weights / jnp.sum(weights, axis=-1, keepdims=True)
    mixed = fold_heads(nn(probs.astype(B16), v), heads).astype(B16)
    part_out[...] = nn(mixed, wo[...]).astype(B16)


def pair_of(saved, pair, width):
    start = pair * 2 * E
    return [saved[:, i * width + start : i * width + start + 2 * E] for i in range(3)]


def attend_kernel(
    g, heads, saved, latents, part_one, part_two, gain, wk, wv,
    o_out, probs_out, side_out, mid_out, mid_low_out,
):
    mid = latents[...].astype(F32) + (part_one[...].astype(F32) + part_two[...].astype(F32))
    mid_out[...] = mid
    mid_low_out[...] = mid.astype(B16)
    unit, _ = norm_parts(mid[g * L : (g + 1) * L])
    side_low = (unit * gain[...]).astype(B16)
    side_k = nn(side_low, wk[...]).astype(B16).astype(F32)
    side_v = nn(side_low, wv[...]).astype(B16).astype(F32)
    width = side_k.shape[1]
    side_out[:, :width] = side_k
    side_out[:, width : 2 * width] = side_v
    side_out[:, 2 * width :] = side_low.astype(F32)
    side_v = spread_heads(side_v, heads).astype(B16)
    side_scores = nt(spread_heads(side_k, heads).astype(B16), saved[:, :width])
    scale = FACTOR * LOG2E
    outs, side_probs, lses = [], [], []
    for pair in range(heads // 2):
        q_pair, k_pair, v_pair = pair_of(saved, pair, width)
        for second in (0, 1):
            h = 2 * pair + second
            scores = nt(head_only(k_pair, second), q_pair)
            side = side_scores[h * L : (h + 1) * L]
            top = jnp.maximum(
                jnp.max(scores, axis=0, keepdims=True), jnp.max(side, axis=0, keepdims=True)
            )
            weights = jnp.exp2((scores - top) * scale)
            side = jnp.exp2((side - top) * scale)
            total = jnp.sum(weights, axis=0, keepdims=True) + jnp.sum(side, axis=0, keepdims=True)
            inverse = 1.0 / total
            side_probs.append(side * inverse)
            lses.append(top * scale + jnp.log2(total))
            outs.append(tn((weights * inverse).astype(B16), v_pair))
    side_probs = jnp.concatenate(side_probs, axis=0)
    probs_out[: heads * L, :] = side_probs
    probs_out[heads * L :, :] = jnp.concatenate(
        lses + [jnp.zeros_like(lses[0])] * (8 - heads), axis=0
    )
    side_o = tn(side_probs.astype(B16), side_v)
    first = half_mask(2 * E)
    token_o = jnp.concatenate(
        [jnp.where(first, outs[2 * i], outs[2 * i + 1]) for i in range(heads // 2)], axis=1
    )
    o_out[...] = (token_o + side_o).astype(B16)


def feed_kernel(
    g, chunk, place, tokens, o, o_two, wo, wo_two, cotangent, gain, up, up_bias, down, *rest
):
    part_outs, outs = rest[:-7], rest[-7:]
    active_out, hidden_grad_out, low_out, middle_out, down_part_out, up_bias_out, down_bias_out = outs
    rows = slice(g * S, (g + 1) * S)
    first = place[0] == 0
    o_first = jnp.where(first, o[...], o_two[...])
    o_second = jnp.where(first, o_two[...], o[...])
    wo_first = jnp.where(first, wo[...], wo_two[...])
    wo_second = jnp.where(first, wo_two[...], wo[...])
    middle = tokens[rows, :].astype(F32) + (nn(o_first, wo_first) + nn(o_second, wo_second))
    middle_out[...] = middle
    unit, _ = norm_parts(middle)
    low = (unit * gain[...]).astype(B16)
    low_out[...] = low
    outer = cotangent[rows, :]
    down_bias_out[...] = jnp.sum(outer.astype(F32), axis=0, keepdims=True)
    part, down_part = None, None
    for start in range(0, up.shape[1], chunk):
        cut = slice(start, start + chunk)
        hidden = nn(low, up[:, cut]) + up_bias[:, cut]
        active, slope = gelu_both(hidden)
        active = active.astype(B16)
        active_out[:, cut] = active
        grad = (slope * nt(outer, down[cut, :])).astype(B16)
        hidden_grad_out[:, cut] = grad
        up_bias_out[:, cut] = jnp.sum(grad.astype(F32), axis=0, keepdims=True)
        one = nt(grad, up[:, cut])
        two = nn(active, down[cut, :])
        part = one if part is None else part + one
        down_part = two if down_part is None else down_part + two
    at = 0
    for out in part_outs:
        out[...] = part[at : at + out.shape[0]].astype(B16)
        at += out.shape[0]
    down_part_out[...] = down_part.astype(B16)


def turn_kernel(
    g, heads, cuts, last, cotangent, middle, gain, wo, wk, wv, o, saved, probs, side, mid, *rest
):
    parts, rest = rest[: 2 * cuts], rest[2 * cuts :]
    earlier, outs = rest[:-8], rest[-8:]
    o_grad_out, delta_out, side_score_grad_out, part_out, grads_out, gain_out = outs[:6]
    middle_grad_out, middle_low_out = outs[6:]
    unit, rate = norm_parts(middle[...])
    sides = [jnp.concatenate([r[...] for r in rs], axis=0) for rs in (parts[:cuts], parts[cuts:])]
    grad = sides[0].astype(F32) + sides[1].astype(F32)
    gain_out[0:1, :] = jnp.sum(grad * unit, axis=0, keepdims=True)
    outer = cotangent[g * S : (g + 1) * S, :].astype(F32)
    middle_grad = outer + norm_back(grad, unit, rate, gain[...])
    middle_grad_out[...] = middle_grad
    middle_low = middle_grad.astype(B16)
    middle_low_out[...] = middle_low
    o_grad = nt(middle_low, wo[...]).astype(B16)
    o_grad_out[...] = o_grad
    width = o_grad.shape[1]
    rows8 = lax.broadcasted_iota(jnp.int32, (8, width), 0)
    columns8 = lax.broadcasted_iota(jnp.int32, (8, width), 1) // E
    pick = (rows8 == columns8).astype(B16)
    weighted = o_grad.astype(F32) * o[...].astype(F32)
    high = weighted.astype(B16)
    low = (weighted - high.astype(F32)).astype(B16)
    delta = nt(pick, high) + nt(pick, low)
    delta_out[...] = delta
    side_v = spread_heads(side[:, width : 2 * width], heads).astype(B16)
    side_prob_grad = nt(side_v, o_grad)
    side_probs = probs[: heads * L, :]
    wide = jnp.concatenate(
        [jnp.broadcast_to(delta[h : h + 1], (L, delta.shape[1])) for h in range(heads)], axis=0
    )
    score_grad = (side_probs * (side_prob_grad - wide)).astype(B16)
    side_score_grad_out[...] = score_grad
    k_grad = (fold_heads(nn(score_grad, saved[:, :width]), heads) * FACTOR).astype(B16)
    v_grad = fold_heads(nn(side_probs.astype(B16), o_grad), heads).astype(B16)
    grads_out[:, :width] = k_grad.astype(F32)
    grads_out[:, width:] = v_grad.astype(F32)
    part = nt(k_grad, wk[...]) + nt(v_grad, wv[...])
    side_unit, _ = norm_parts(mid[g * L : (g + 1) * L, :])
    gain_out[1:2, :] = jnp.sum(part * side_unit, axis=0, keepdims=True)
    gain_out[2:, :] = jnp.zeros_like(gain_out[2:, :])
    if last:
        part = jnp.concatenate([r[...] for r in earlier] + [part], axis=0)
    part_out[...] = part.astype(part_out.dtype)


def side_kernel(part_one, part_two, mid, cotangent, gain, low_out, grad_out):
    unit, rate = norm_parts(mid[...])
    part = part_one[...].astype(F32) + part_two[...].astype(F32)
    grad = cotangent[...].astype(F32) + norm_back(part, unit, rate, gain[...])
    grad_out[...] = grad
    low_out[...] = grad.astype(B16)


def attend_back_kernel(
    g, heads, tokens, saved, o_grad, probs, delta, side_score_grad, side, wq, wk, wv, *rest
):
    part_out, grads_out, gain_out = rest[-3:]
    gains, earlier = rest[: min(g, 1) + 1], rest[min(g, 1) + 1 : -3]
    scale = FACTOR * LOG2E
    first = half_mask(2 * E)
    width = o_grad.shape[1]
    side_k = spread_heads(side[:, :width], heads).astype(B16)
    side_q_grad = tn(side_score_grad[...], side_k)
    at = heads * L
    for pair in range(heads // 2):
        start = pair * 2 * E
        cut = slice(start, start + 2 * E)
        q_pair, k_pair, v_pair = pair_of(saved, pair, width)
        grad_pair = o_grad[:, cut]
        q_grads, k_grads, v_grads = [], [], []
        for second in (0, 1):
            h = 2 * pair + second
            scores = nt(head_only(k_pair, second), q_pair)
            weights = jnp.exp2(scores * scale - probs[at + h : at + h + 1, :])
            prob_grad = nt(head_only(v_pair, second), grad_pair)
            score_grad = (weights * (prob_grad - delta[h : h + 1, :])).astype(B16)
            v_grads.append(nn(weights.astype(B16), grad_pair))
            k_grads.append(nn(score_grad, q_pair))
            q_grads.append(tn(score_grad, k_pair))
        q_pair_grad = jnp.where(first, q_grads[0], q_grads[1]) + side_q_grad[:, cut]
        k_pair_grad = jnp.where(first, k_grads[0], k_grads[1])
        v_pair_grad = jnp.where(first, v_grads[0], v_grads[1])
        grads_out[:, start : start + 2 * E] = (q_pair_grad * FACTOR).astype(B16)
        grads_out[:, width + start : width + start + 2 * E] = (k_pair_grad * FACTOR).astype(B16)
        grads_out[:, 2 * width + start : 2 * width + start + 2 * E] = v_pair_grad.astype(B16)
    part = nt(grads_out[:, :width], wq[...]) + nt(grads_out[:, width : 2 * width], wk[...])
    part = part + nt(grads_out[:, 2 * width :], wv[...])
    for i, r in enumerate(earlier):
        part_out[i * S : (i + 1) * S, :] = r[...]
    part_out[len(earlier) * S :, :] = part.astype(B16)
    unit, _ = norm_parts(tokens[g * S : (g + 1) * S, :].astype(F32))
    total = gains[0][1:2, :] + jnp.sum(part * unit, axis=0, keepdims=True)
    for r in gains[1:]:
        total = total + r[...]
    gain_out[...] = total


def leave_kernel(tokens, gain, part_one, part_two, *refs):
    middle_grad, grad_out = refs[:-1], refs[-1]
    for g in range(len(middle_grad)):
        rows = slice(g * S, (g + 1) * S)
        unit, rate = norm_parts(tokens[rows, :].astype(F32))
        grad = part_one[rows, :].astype(F32) + part_two[rows, :].astype(F32)
        grad_out[rows, :] = middle_grad[g][...] + norm_back(grad, unit, rate, gain[...])


def result_kernel(middle, part_one, part_two, bias, *refs):
    earlier, out = refs[:-1], refs[-1]
    at = 0
    for r in earlier:
        out[at : at + S, :] = r[...]
        at += S
    total = part_one[...].astype(F32) + part_two[...].astype(F32)
    out[at:, :] = (middle[...] + total + bias[...]).astype(B16)


def latent_leave_kernel(me, latents, part_one, part_two, gain, mid_grad, grad_out, gain_out):
    own = latents.shape[0]
    unit, rate = norm_parts(latents[...].astype(F32))
    start = part_one.shape[0] - own - 16
    total = part_one[start:, :].astype(F32) + part_two[start:, :].astype(F32)
    grad_out[...] = mid_grad[...] + norm_back(total[:own], unit, rate, gain[...])
    share, model = gain_out.shape[1], gain.shape[1]
    row = lax.broadcasted_iota(jnp.int32, (share, model), 0)
    column = lax.broadcasted_iota(jnp.int32, (share, model), 1)
    kept = jnp.where(column == row + me[0] * share, total[own : own + 1], 0.0)
    gain_out[...] = jnp.broadcast_to(jnp.sum(kept, axis=1, keepdims=True), (share, 8)).T


def split_pairs(values, bit, share, send_out, keep_out):
    blocks = values.reshape(values.shape[0] // (2 * share), 2, share, values.shape[1])
    even, odd = blocks[:, 0], blocks[:, 1]
    send_out[...] = jnp.where(bit == 0, odd, even).astype(B16)
    keep_out[...] = jnp.where(bit == 0, even, odd).astype(B16)


def weight_grad_kernel(groups, share, pieces, me, cotangent, *refs):
    active, low, hidden_grad = (refs[i * groups : (i + 1) * groups] for i in range(3))
    outs = refs[3 * groups :]
    bit = me[0] % 2
    width = active[0].shape[1]
    at = 0
    for count, lefts, rights in (
        (pieces[0], [cotangent[g * S : (g + 1) * S, :].T for g in range(groups)], active),
        (pieces[1], [r[...].T for r in low], hidden_grad),
    ):
        chunk = width // count
        for k in range(count):
            cut = slice(k * chunk, (k + 1) * chunk)
            total = nn(lefts[0], rights[0][:, cut])
            for g in range(1, groups):
                total = total + nn(lefts[g], rights[g][:, cut])
            split_pairs(total, bit, share, outs[at], outs[at + 1])
            at += 2


def attention_grad_kernel(groups, share, me, *refs):
    saved, grads, middle_low, o, side, side_grads = (
        refs[i * groups : (i + 1) * groups] for i in range(6)
    )
    outs = refs[6 * groups :]
    bit = me[0] % 2
    width = o[0].shape[1]
    stack = [jnp.concatenate([r[...] for r in rs], axis=0) for rs in (side, side_grads)]
    side_low = stack[0][:, 2 * width :].astype(B16)
    side_k, side_v = stack[1][:, :width].astype(B16), stack[1][:, width:].astype(B16)
    flat = [r[:, 3 * width :].T for r in saved]
    low_flat = [r[...].T for r in middle_low]

    def total_of(lefts, rights, cut):
        total = nn(lefts[0], rights[0][:, cut])
        for g in range(1, groups):
            total = total + nn(lefts[g], rights[g][:, cut])
        return total

    def cut_of(i):
        return slice(i * width, (i + 1) * width)

    totals = (
        total_of(flat, grads, cut_of(0)),
        total_of(flat, grads, cut_of(1)) + tn(side_low, side_k),
        total_of(flat, grads, cut_of(2)) + tn(side_low, side_v),
        total_of(low_flat, o, cut_of(0)),
    )
    for i, total in enumerate(totals):
        split_pairs(total, bit, share, outs[2 * i], outs[2 * i + 1])


def sum_of(parts):
    total = parts[0]
    for part in parts[1:]:
        total = total + part
    return total


def vector_kernel(groups, share, me, one, two, *refs):
    up_bias, down_bias, gains = (refs[i * groups : (i + 1) * groups] for i in range(3))
    send_out, keep_out = refs[3 * groups :]
    model = one.shape[1]
    gain = one[...] + two[...]

    def column(rows):
        return jnp.broadcast_to(rows, (8, rows.shape[1])).T

    columns = [
        column(sum_of([r[...] for r in down_bias])),
        column(sum_of([r[0:1, :] for r in gains])),
        column(gain),
    ]
    bias = column(sum_of([r[...] for r in up_bias]))
    times = bias.shape[0] // model
    bias = bias.reshape(model // share, times, share, 8)
    columns += [bias[:, i].reshape(model, 8) for i in range(times)]
    lane = lax.broadcasted_iota(jnp.int32, (model, 128), 1)
    block = jnp.zeros((model, 128), F32)
    for i, one in enumerate(columns):
        block = jnp.where(lane == i, one[:, 0:1], block)
    split_pairs(block, me[0] % 2, share, send_out, keep_out)


def halve_kernel(shift, pieces, cuts, me, *refs):
    count = len(pieces)
    keeps, gots, outs = refs[:count], refs[count : 2 * count], refs[2 * count :]
    bit = (me[0] // shift) % 2
    for keep, got, (first, last) in zip(keeps, gots, pieces):
        for k, (start, end) in enumerate(cuts):
            low, high = max(first, start), min(last, end)
            if low >= high:
                continue
            of_piece, of_out = slice(low - first, high - first), slice(low - start, high - start)
            for i in range(keep.shape[0]):
                there, here = (
                    keep[i, pl.ds(at, 1), :, of_piece].astype(F32)
                    + got[i, pl.ds(at, 1), :, of_piece].astype(F32)
                    for at in (1 - bit, bit)
                )
                outs[2 * k][pl.ds(i, 1), :, of_out] = there.astype(B16)
                outs[2 * k + 1][pl.ds(i, 1), :, of_out] = here


def finish_kernel(cuts, keep, got, *outs):
    total = keep[0] + got[0].astype(F32)
    for out, (start, end, flat) in zip(outs, cuts):
        part = total[:, start:end]
        out[...] = part.T[: out.shape[0]] if flat else part


def latent_back_kernel(
    heads, own, order, block, me, group_image, token_part, latents, q, k, v, mid_one, mid_two, gain, wq, wk, wv, wo,
    part_out, wq_out, wk_out, wv_out, wo_out, mixed, q_grad, k_grad, v_grad, images,
):
    mid_low = jnp.concatenate([mid_one[...], mid_two[...]], axis=0)
    o_grad = nt(mid_low, wo[...]).astype(B16)
    unit, _ = norm_parts(latents[...].astype(F32))
    low = (unit * gain[...]).astype(B16)
    everyone = low.shape[0]
    images_row, images_column = image_rows(order, own // L, me[0], group_image)

    def rows_of(start, ref_q, ref_grad, ref_images):
        wide_q = spread_heads(ref_q, heads)
        wide_grad = spread_heads(ref_grad, heads)
        scores = nt(wide_q, k[...]) * FACTOR
        member = jnp.concatenate([ref_images] * heads, axis=0) == images_row
        scores = jnp.where(member, scores, NEGATIVE)
        weights = jnp.exp(scores - jnp.max(scores, axis=-1, keepdims=True))
        probs = weights / jnp.sum(weights, axis=-1, keepdims=True)
        probs_low = probs.astype(B16)
        prob_grad = nt(wide_grad, v[...])
        delta = jnp.sum(prob_grad * probs, axis=-1, keepdims=True)
        score_grad = (probs * (prob_grad - delta)).astype(B16)
        mixed[pl.ds(start, block), :] = fold_heads(nn(probs_low, v[...]), heads).astype(B16)
        q_grad[pl.ds(start, block), :] = (
            fold_heads(nn(score_grad, k[...]), heads) * FACTOR
        ).astype(B16)
        return tn(score_grad, wide_q), tn(probs_low, wide_grad)

    if block == everyone:
        k_sum, v_sum = rows_of(0, q[...], o_grad, images_column)
        k_sum, v_sum = k_sum * FACTOR, v_sum
    else:
        v_grad[...] = o_grad
        images[...] = jnp.broadcast_to(images_column, images.shape)

        def step(i, held):
            start = pl.multiple_of(i * block, block)
            here = pl.ds(start, block)
            one, two = rows_of(start, q[here, :], v_grad[here, :], images[here, :][:, :1])
            return held[0] + one, held[1] + two

        zero = jnp.zeros(k.shape, F32)
        k_sum, v_sum = lax.fori_loop(0, everyone // block, step, (zero, zero))
        k_sum = k_sum * FACTOR
    k_grad[...] = k_sum.astype(B16)
    v_grad[...] = v_sum.astype(B16)
    part = nt(q_grad[...], wq[...]) + nt(k_grad[...], wk[...]) + nt(v_grad[...], wv[...])
    gain_part = jnp.sum(part * unit, axis=0, keepdims=True)
    rows = token_part.shape[0]
    part_out[:rows, :] = token_part[...]
    part_out[rows:, :] = jnp.concatenate(
        [part[:own], jnp.broadcast_to(gain_part, (16, part.shape[1]))], axis=0
    ).astype(B16)
    share = wq_out.shape[0]
    model = low.shape[1]
    row = lax.broadcasted_iota(jnp.int32, (share, model), 0)
    column = lax.broadcasted_iota(jnp.int32, (share, model), 1)
    pick = (column == row + me[0] * share).astype(B16)
    columns = nt(pick, low).astype(B16)
    wq_out[...] = nn(columns, q_grad[...])
    wk_out[...] = nn(columns, k_grad[...])
    wv_out[...] = nn(columns, v_grad[...])
    wo_out[...] = nn(nt(pick, mid_low).astype(B16), mixed[...])


MIB = 1024 * 1024
OUT = "out"


class Order:
    def __init__(self, pinned):
        self.pinned, self.last = pinned, None

    def call(self, kernel, name, outs, ins, scratch=(), limit=16, behind=(), loose=False):
        scalars = [isinstance(a, tuple) for a in ins]
        arrays = [a[1] if isinstance(a, tuple) else a for a in ins]
        earlier = tuple(behind) + (() if self.last is None or loose else (self.last,))
        if earlier:
            least = min(range(len(arrays)), key=lambda i: arrays[i].size)
            arrays[least] = after(arrays[least], *earlier)
        if self.pinned:
            arrays = [
                a if scalar else pltpu.with_memory_space_constraint(a, pltpu.VMEM)
                for a, scalar in zip(arrays, scalars)
            ]

        def result(shape, dtype, kind=None):
            if self.pinned and kind != OUT:
                return pltpu.VMEM(shape, dtype)
            return jax.ShapeDtypeStruct(shape, dtype)

        def whole(shape):
            return pl.BlockSpec(tuple(shape), lambda: (0,) * len(shape))

        results = pl.pallas_call(
            kernel,
            out_shape=[result(*out) for out in outs],
            in_specs=[
                pl.BlockSpec(memory_space=pltpu.SMEM) if scalar else whole(a.shape)
                for a, scalar in zip(arrays, scalars)
            ],
            out_specs=[whole(out[0]) for out in outs],
            scratch_shapes=list(scratch),
            compiler_params=pltpu.CompilerParams(vmem_limit_bytes=limit * MIB),
            cost_estimate=pl.CostEstimate(flops=0, bytes_accessed=0, transcendentals=0),
            name=name,
        )(*arrays)
        if not loose:
            self.last = min(results, key=lambda a: a.size)
        return results

    def load(self, *arrays, behind=()):
        if not self.pinned:
            return arrays
        sources = list(arrays)
        earlier = tuple(behind) + (() if self.last is None else (self.last,))
        if earlier:
            sources[0] = after(sources[0], *earlier)
        results = pl.pallas_call(
            load_kernel,
            out_shape=[pltpu.VMEM(a.shape, a.dtype) for a in arrays],
            in_specs=[pl.BlockSpec(memory_space=pltpu.HBM)] * len(arrays),
            out_specs=[pl.BlockSpec(memory_space=pltpu.VMEM)] * len(arrays),
            scratch_shapes=[pltpu.SemaphoreType.DMA((len(arrays),))],
            compiler_params=pltpu.CompilerParams(vmem_limit_bytes=MIB),
            cost_estimate=pl.CostEstimate(flops=0, bytes_accessed=0, transcendentals=0),
            name="load",
        )(*[pltpu.with_memory_space_constraint(a, pltpu.HBM) for a in sources])
        self.last = min(results, key=lambda a: a.size)
        return results


def after(value, *earlier):
    return lax.optimization_barrier((value, earlier))[0]


def swap_tp(values, name):
    with jax.named_scope("swap_" + name):
        return lax.ppermute(values, "tp", [(0, 1), (1, 0)])


def flip(values, bits, name):
    size = lax.axis_size("dp")
    with jax.named_scope("flip_" + name):
        return lax.ppermute(values, "dp", [(i, i ^ bits) for i in range(size)])


def gather_steps(size):
    width, steps = 2, []
    while width * 4 < size:
        steps.append([width])
        width *= 2
    if width < size:
        steps.append([width * k for k in range(1, size // width)])
    steps.reverse()
    return steps + [[1]]


def one_by_one(steps):
    result = []
    for step in steps:
        result += [[b] for b in step if b & (b - 1) == 0]
    return result


def gather_order(size):
    order = [0]
    for step in gather_steps(size):
        order = order + [i ^ bits for bits in [0] + step for i in order][len(order) :]
    return order


def scatter_sum(grads):
    size = lax.axis_size("dp")
    me = lax.axis_index("dp")
    width = 1
    while width * 4 < size:
        bit = (me // width) % 2
        pairs = grads.reshape((grads.shape[0] // 2, 2) + grads.shape[1:])
        send = lax.dynamic_index_in_dim(pairs, 1 - bit, 1, keepdims=False)
        keep = lax.dynamic_index_in_dim(pairs, bit, 1, keepdims=False)
        got = flip(send.astype(B16), width, "sums")
        grads = keep.astype(F32) + got.astype(F32)
        width *= 2
    place = me // width
    total = lax.dynamic_index_in_dim(grads, place, 0, keepdims=False)
    for k in range(1, size // width):
        send = lax.dynamic_index_in_dim(grads, place ^ k, 0, keepdims=False)
        total = total + flip(send.astype(B16), width * k, "sums").astype(F32)
    return total


class Scatter:
    def __init__(self, order, me, width, keeps, sends, name):
        self.order, self.me, self.width, self.keeps = order, me, width, list(keeps)
        self.gots = [flip(a, width, name) for a in sends]
        self.pieces, self.columns = [], 0
        for a in self.keeps:
            self.pieces.append((self.columns, self.columns + a.shape[2]))
            self.columns += a.shape[2]

    def halve(self, cuts=None, behind=()):
        cuts = [(0, self.columns)] if cuts is None else cuts
        n, share, _ = self.keeps[0].shape
        shapes = [(n // 2, share, end - start) for start, end in cuts]
        results = self.order.call(
            partial(halve_kernel, 2 * self.width, self.pieces, cuts),
            "halve",
            [out for shape in shapes for out in ((shape, B16), (shape, F32))],
            [("smem", self.me)]
            + [a.reshape((n // 2, 2) + a.shape[1:]) for a in self.keeps + self.gots],
            behind=behind,
        )
        return results[::2], results[1::2]

    def next(self, name, *ties):
        (send,), (keep,) = self.halve()
        send = after(send, *ties) if ties else send
        return Scatter(self.order, self.me, 2 * self.width, [keep], [send], name)

    def finish(self, cuts):
        share = self.keeps[0].shape[1]
        shapes = [(8, share) if flat else (share, e - s) for s, e, flat in cuts]
        return self.order.call(
            partial(finish_kernel, cuts),
            "finish",
            [(shape, F32, OUT) for shape in shapes],
            self.keeps + self.gots,
        )


ORDER = (
    "load_small",
    "gather_0",
    "load_first",
    "gather_1",
    "enter_0",
    "enter_1",
    "latent",
    "load_feed",
    "attend_0",
    "attend_1",
    "feed_0",
    "feed_1",
    "weight_grad",
    "turn_0",
    "down_y",
    "turn_1",
    "back_0",
    "result_0",
    "side",
    "back_1",
    "gather_mid_0",
    "attention_grad",
    "gather_mid_1",
    "vectors",
    "gather_mid_2",
    "up_y",
    "down_z",
    "first_y",
    "second_y",
    "latent_back",
    "down_zz",
    "up_z",
    "first_z",
    "up_zz",
    "down_done",
    "first_zz",
    "up_done",
    "second_z",
    "result_1",
    "latent_leave",
    "leave",
    "second_zz",
    "first_done",
    "second_done",
)
SUMS = (
    "weight_grad",
    "down_y",
    "attention_grad",
    "vectors",
    "up_y",
    "down_z",
    "first_y",
    "second_y",
    "down_zz",
    "up_z",
    "first_z",
    "up_zz",
    "down_done",
    "first_zz",
    "up_done",
    "second_z",
    "second_zz",
    "first_done",
    "second_done",
)
PIECES = (4, 2)
TIE_UP = True
TIE_DOWN_0 = "turn"
TIE_DOWN_1 = "gain"
MID_DIRECT = False


def local(
    tokens,
    latents,
    latent_query,
    latent_key,
    latent_value,
    latent_output,
    query_weight,
    key_weight,
    value_weight,
    output_weight,
    up_weight,
    up_bias,
    down_weight,
    down_bias,
    latent_gain,
    attention_gain,
    feed_gain,
    group_image,
    token_cotangent,
    latent_cotangent,
):
    size = lax.axis_size("dp")
    me = lax.axis_index("dp")
    me_row = me.reshape(1)
    place = lax.axis_index("tp").reshape(1)
    width = latent_query.shape[1]
    heads = width // E
    rows, model = tokens.shape
    hidden_units = up_weight.shape[1]
    groups = rows // S
    own = latents.shape[0]
    everyone = own * size
    share = model // size
    small = everyone <= 512
    aligned = share % 16 == 0 and size >= 8
    each = range(groups)
    latent_gain_row = latent_gain.reshape(1, model)
    attention_gain_row = attention_gain.reshape(1, model)
    feed_gain_row = feed_gain.reshape(1, model)
    up_bias_row = up_bias.reshape(1, hidden_units)
    down_bias_row = down_bias.reshape(1, model)
    scalars = (me_row, place)
    gain_rows = (latent_gain_row, attention_gain_row, feed_gain_row, up_bias_row, down_bias_row)
    chain = Order(small)
    call = chain.call
    latent_limit = 16 if small else 56
    gathered = gather_steps(size)
    turns = tuple(gather_order(size))

    def join(parts):
        if not small:
            return jnp.concatenate(parts, axis=0)
        shape = (sum(p.shape[0] for p in parts), model)
        return call(join_kernel, "join", [(shape, B16)], parts)[0]

    at = {}
    output_weight_two = swap_tp(output_weight, "output_weight")

    def load_small():
        at["latents_held"] = latents
        at["latents"], at["latent_cotangent"] = chain.load(
            latents, latent_cotangent, behind=scalars + gain_rows
        )

    def gather(name, steps, first):
        held = at[name]
        others = [flip(held, bits, name) for bits in steps]
        at[name] = join([at["latents"] if first else held] + others)

    def load_all():
        at["tokens"], *weights = chain.load(
            tokens,
            query_weight,
            key_weight,
            value_weight,
            output_weight,
            latent_query,
            latent_key,
            latent_value,
            latent_output,
        )
        at["group_weights"], at["output_weight"], at["latent_weights"] = (
            weights[:3],
            weights[3],
            weights[4:],
        )

    def enter(g):
        (at["saved", g],) = call(
            partial(enter_kernel, g),
            "enter",
            [((S, 3 * width + model), B16)],
            [at["tokens"], attention_gain_row, *at["group_weights"]],
        )

    def latent():
        held = at["latents_held"]
        at["latents_all"], *at["latent_qkv"], at["latent_part"] = call(
            partial(latent_kernel, heads, own, turns),
            "latent",
            [((everyone, model), B16)] + [((everyone, width), B16)] * 3 + [((own, model), B16)],
            [
                ("smem", me_row),
                ("smem", group_image),
                held,
                flip(held, 1, "latents_held"),
                latent_gain_row,
                *at["latent_weights"],
            ],
            limit=latent_limit,
        )
        at["latent_part_two"] = swap_tp(at["latent_part"], "latent_part")

    def load_feed():
        at["up_weight"], at["down_weight"], at["cotangent"] = chain.load(
            up_weight, down_weight, token_cotangent
        )

    def attend(g):
        at["o", g], at["probs", g], at["side", g], mid, mid_low = call(
            partial(attend_kernel, g, heads),
            "attend",
            [
                ((S, width), B16),
                ((heads * L + 8, S), F32),
                ((L, 2 * width + model), F32),
                ((own, model), F32),
                ((own, model), B16, OUT),
            ],
            [
                at["saved", g],
                at["latents"],
                at["latent_part"],
                at["latent_part_two"],
                attention_gain_row,
                *at["group_weights"][1:],
            ],
        )
        if g == 0:
            at["mid"], at["mixed_latents"] = mid, mid_low
        at["o_two", g] = swap_tp(at["o", g], "o")

    def feed(g):
        count = 1 if g == groups - 1 else 2
        results = call(
            partial(feed_kernel, g, hidden_units // 3),
            "feed",
            [((S // count, model), B16)] * count
            + [
                ((S, hidden_units), B16),
                ((S, hidden_units), B16),
                ((S, model), B16),
                ((S, model), F32),
                ((S, model), B16),
                ((1, hidden_units), F32),
                ((1, model), F32),
            ],
            [
                ("smem", place),
                at["tokens"],
                at["o", g],
                at["o_two", g],
                at["output_weight"],
                output_weight_two,
                at["cotangent"],
                feed_gain_row,
                at["up_weight"],
                up_bias_row,
                at["down_weight"],
            ],
        )
        at["feed_part", g] = results[:count]
        names = ("active", "hidden_grad", "feed_low", "middle", "down_part", "up_bias", "down_bias")
        for name, value in zip(names, results[count:]):
            at[name, g] = value
        at["feed_part_two", g] = [swap_tp(p, "feed_part") for p in results[:count]]

    def weight_grad():
        outs = []
        for count in PIECES:
            outs += [((size // 2, share, hidden_units // count), B16)] * (2 * count)
        halves = call(
            partial(weight_grad_kernel, groups, share, PIECES),
            "weight_grad",
            outs,
            [("smem", me_row), at["cotangent"]]
            + [at[name, g] for name in ("active", "feed_low", "hidden_grad") for g in each],
        )
        at["down_halves"], at["up_halves"] = halves[: 2 * PIECES[0]], halves[2 * PIECES[0] :]

    def turn(g):
        last = g == groups - 1
        names = (
            "o_grad",
            "delta",
            "side_score_grad",
            "side_part",
            "side_grads",
            "gains",
            "middle_grad",
            "middle_low",
        )
        results = call(
            partial(turn_kernel, g, heads, len(at["feed_part", g]), last),
            "turn",
            [
                ((S, width), B16),
                ((8, S), F32),
                ((heads * L, S), B16),
                ((own if last else L, model), B16 if last else F32),
                ((L, 2 * width), F32),
                ((8, model), F32),
                ((S, model), F32),
                ((S, model), B16),
            ],
            [
                at["cotangent"],
                at["middle", g],
                feed_gain_row,
                at["output_weight"],
                *at["group_weights"][1:],
                at["o", g],
                at["saved", g],
                at["probs", g],
                at["side", g],
                at["mid"],
                *at["feed_part", g],
                *at["feed_part_two", g],
                *[at["side_part", i] for i in range(g)],
            ],
        )
        for name, value in zip(names, results):
            at[name, g] = value
        if last:
            at["side_part_two"] = swap_tp(at["side_part", g], "side_part")
            if aligned:
                sends = [after(a, at["delta", g]) for a in at["up_halves"][::2]]
                at["up"] = Scatter(chain, me_row, 1, at["up_halves"][1::2], sends, "up_core")
        elif aligned and g == 0:
            sends = [after(a, at["delta", g]) for a in at["down_halves"][::2]]
            at["down"] = Scatter(chain, me_row, 1, at["down_halves"][1::2], sends, "down_core")
        if not last:
            tie = at["delta", 0] if TIE_DOWN_0 == "turn" else at["middle", groups - 1]
            at["down_part_two", g] = swap_tp(after(at["down_part", g], tie), "down_part")

    def back(g):
        last = g == groups - 1
        at["token_part", g], at["grads", g], at["gain"] = call(
            partial(attend_back_kernel, g, heads),
            "attend_back",
            [((rows if last else S, model), B16), ((S, 3 * width), B16), ((1, model), F32)],
            [
                at["tokens"],
                at["saved", g],
                at["o_grad", g],
                at["probs", g],
                at["delta", g],
                at["side_score_grad", g],
                at["side", g],
                *at["group_weights"],
                at["gains", g],
                *([at["gain"]] if g else []),
                *([at["token_part", i] for i in range(g)] if last else []),
            ],
        )
        if last:
            at["gain_two"] = swap_tp(at["gain"], "gain")
            tie = {"gain": "gain_two", "back": "gain", "side": "side_part_two"}[TIE_DOWN_1]
            at["down_part_two", g] = swap_tp(after(at["down_part", g], at[tie]), "down_part")

    def result(g):
        shape, kind = ((rows, model), (OUT,)) if g == groups - 1 else ((S, model), ())
        (at["result", g],) = call(
            result_kernel,
            "result",
            [(shape, B16) + kind],
            [
                at["middle", g],
                at["down_part", g],
                at["down_part_two", g],
                down_bias_row,
                *[at["result", i] for i in range(g)],
            ],
        )

    def side():
        at["mid_held"], at["middle_latent_grad"] = call(
            side_kernel,
            "side",
            [((own, model), B16), ((own, model), F32)],
            [
                at["side_part", groups - 1],
                at["side_part_two"],
                at["mid"],
                at["latent_cotangent"],
                attention_gain_row,
            ],
        )

    def attention_grad():
        names = ("saved", "grads", "middle_low", "o", "side", "side_grads")
        halves = call(
            partial(attention_grad_kernel, groups, share),
            "attention_grad",
            [((size // 2, share, width), B16)] * 8,
            [("smem", me_row)] + [at[name, g] for name in names for g in each],
        )
        at["first"] = Scatter(chain, me_row, 1, halves[1:4:2], halves[:4:2], "first_core")
        at["second_halves"] = halves[4:]

    def vectors():
        names = ("up_bias", "down_bias", "gains")
        at["vector_halves"] = call(
            partial(vector_kernel, groups, share),
            "vectors",
            [((size // 2, share, 128), B16)] * 2,
            [("smem", me_row), at["gain"], at["gain_two"]]
            + [at[name, g] for name in names for g in each],
        )

    def second_y():
        halves = at["second_halves"] + at["vector_halves"]
        at["second"] = Scatter(chain, me_row, 1, halves[1::2], halves[::2], "second_core")
        advance("second", "second_y")

    def advance(which, name, *ties):
        at[which] = at[which].next(name, *ties)

    def latent_back():
        held = at["mid_held"]
        block = min(everyone, max(16, 65536 // everyone))
        at["all_part"], *at["latent_grads"] = call(
            partial(latent_back_kernel, heads, own, turns, block),
            "latent_back",
            [((rows + own + 16, model), B16)] + [((share, width), F32, OUT)] * 4,
            [
                ("smem", me_row),
                ("smem", group_image),
                at["token_part", groups - 1],
                at["latents_all"],
                *at["latent_qkv"],
                held,
                flip(held, 1, "mid_held"),
                latent_gain_row,
                *at["latent_weights"],
            ],
            scratch=[pltpu.VMEM((everyone, width), B16)] * 4 + [pltpu.VMEM((everyone, 128), F32)],
            limit=latent_limit,
        )
        at["all_part_two"] = swap_tp(at["all_part"], "all_part")

    def latent_leave():
        at["latent_grad"], at["latent_gain"] = call(
            latent_leave_kernel,
            "latent_leave",
            [((own, model), F32, OUT), ((8, share), F32, OUT)],
            [
                ("smem", me_row),
                at["latents"],
                at["all_part"],
                at["all_part_two"],
                latent_gain_row,
                at["middle_latent_grad"],
            ],
        )

    def leave():
        (at["token_grad"],) = call(
            leave_kernel,
            "leave",
            [((rows, model), F32, OUT)],
            [at["tokens"], attention_gain_row, at["all_part"], at["all_part_two"]]
            + [at["middle_grad", g] for g in each],
        )

    def done(which, *cuts):
        at[which, "done"] = at[which].finish(cuts)

    steps = {
        "load_small": load_small,
        "load_first": load_all,
        "latent": latent,
        "load_feed": load_feed,
        "weight_grad": weight_grad,
        "side": side,
        "attention_grad": attention_grad,
        "vectors": vectors,
        "second_y": second_y,
        "latent_back": latent_back,
        "latent_leave": latent_leave,
        "leave": leave,
        "down_done": partial(done, "down", (0, hidden_units, False)),
        "up_done": partial(done, "up", (0, hidden_units, False)),
        "first_done": partial(done, "first", (0, width, False), (width, 2 * width, False)),
        "second_done": partial(
            done,
            "second",
            (0, width, False),
            (width, 2 * width, False),
            (2 * width, 2 * width + 128, True),
        ),
    }
    for name, which in (
        ("down_y", "down"),
        ("down_z", "down"),
        ("down_zz", "down"),
        ("up_z", "up"),
        ("up_zz", "up"),
        ("first_y", "first"),
        ("first_z", "first"),
        ("first_zz", "first"),
        ("second_z", "second"),
        ("second_zz", "second"),
    ):
        steps[name] = partial(advance, which, name)
    steps["up_y"] = lambda: advance("up", "up_y", *(at["down"].gots if TIE_UP else ()))
    for g in each:
        for name, step in (
            ("enter", enter),
            ("attend", attend),
            ("feed", feed),
            ("turn", turn),
            ("back", back),
            ("result", result),
        ):
            steps[f"{name}_{g}"] = partial(step, g)
    for i, bits in enumerate(gathered[:-1]):
        steps[f"gather_{i}"] = partial(gather, "latents_held", bits, i == 0)
    mid_steps = gathered[:-1] if MID_DIRECT else one_by_one(gathered[:-1])
    for i, bits in enumerate(mid_steps):
        steps[f"gather_mid_{i}"] = partial(gather, "mid_held", bits, False)
    order = [name for name in ORDER if name in steps and (aligned or name not in SUMS)]
    for name in steps:
        if name not in order and (aligned or name not in SUMS):
            kind, _, number = name.rpartition("_")
            order.insert(order.index(f"{kind}_{int(number) - 1}") + 1, name)
    for name in order:
        steps[name]()
    if aligned:
        (down_done,), (up_done,) = at["down", "done"], at["up", "done"]
        query_done, key_done = at["first", "done"]
        value_done, output_done, vectors_done = at["second", "done"]
    else:

        def flat(name, start, end):
            return jnp.concatenate([at[name, g][:, start:end] for g in each], axis=0).astype(B16)

        token_low = flat("saved", 3 * width, 3 * width + model)
        side_low = flat("side", 2 * width, 2 * width + model)
        products = (
            tn(token_cotangent, flat("active", 0, hidden_units)),
            tn(flat("feed_low", 0, model), flat("hidden_grad", 0, hidden_units)),
            tn(token_low, flat("grads", 0, width)),
            tn(token_low, flat("grads", width, 2 * width))
            + tn(side_low, flat("side_grads", 0, width)),
            tn(token_low, flat("grads", 2 * width, 3 * width))
            + tn(side_low, flat("side_grads", width, 2 * width)),
            tn(flat("middle_low", 0, model), flat("o", 0, width)),
        )
        up_bias_rows = sum(at["up_bias", g] for g in each).reshape(size, -1, share)
        rows_of = [
            sum(at["down_bias", g] for g in each),
            sum(at["gains", g] for g in each)[:1],
            at["gain"] + at["gain_two"],
            up_bias_rows.swapaxes(0, 1).reshape(-1, model),
        ]
        rows_of = jnp.concatenate(rows_of, axis=0)
        total = jnp.concatenate([a.astype(B16) for a in products + (rows_of.T,)], axis=1)
        total = scatter_sum(total.reshape(size, share, -1))
        ends = [hidden_units, 2 * hidden_units] + [2 * hidden_units + i * width for i in range(1, 5)]
        down_done, up_done, query_done, key_done, value_done, output_done, vectors_done = jnp.split(
            total, ends, axis=1
        )
        vectors_done = vectors_done.T
    latent_query_done, latent_key_done, latent_value_done, latent_output_done = at["latent_grads"]
    return (
        at["result", groups - 1],
        at["mixed_latents"],
        at["token_grad"],
        at["latent_grad"],
        latent_query_done,
        latent_key_done,
        latent_value_done,
        latent_output_done.T,
        query_done,
        key_done,
        value_done,
        output_done.T,
        up_done,
        vectors_done[3 : 3 + hidden_units // model].reshape(-1),
        down_done.T,
        vectors_done[0],
        at["latent_gain"][0],
        vectors_done[2],
        vectors_done[1],
    )


def solution(mesh):
    placed = (
        P("dp", None),
        P("dp", None),
        P(None, "tp"),
        P(None, "tp"),
        P(None, "tp"),
        P("tp", None),
        P(None, "tp"),
        P(None, "tp"),
        P(None, "tp"),
        P("tp", None),
        P(None, "tp"),
        P("tp"),
        P("tp", None),
        P(),
        P(),
        P(),
        P(),
        P(),
        P("dp", None),
        P("dp", None),
    )
    return jax.shard_map(
        local,
        mesh=mesh,
        in_specs=placed,
        out_specs=(
            P("dp", None),
            P("dp", None),
            P("dp", None),
            P("dp", None),
            P("dp", "tp"),
            P("dp", "tp"),
            P("dp", "tp"),
            P("tp", "dp"),
            P("dp", "tp"),
            P("dp", "tp"),
            P("dp", "tp"),
            P("tp", "dp"),
            P("dp", "tp"),
            P(("tp", "dp")),
            P("tp", "dp"),
            P("dp"),
            P("dp"),
            P("dp"),
            P("dp"),
        ),
        check_vma=False,
    )
```

```python
from functools import partial

import jax
import jax.numpy as jnp
from jax import lax
from jax.experimental import pallas as pl
from jax.experimental.pallas import tpu as pltpu
from jax.sharding import PartitionSpec as P

E = 64
S = 256
L = 8
EPSILON = 1e-05
NEGATIVE = -1000000000.0
FACTOR = E ** (-0.5)
LOG2E = 1.4426950408889634
F32 = jnp.float32
B16 = jnp.bfloat16


def nn(left, right):
    return lax.dot_general(left, right, (((1,), (0,)), ((), ())), preferred_element_type=F32)


def nt(left, right):
    return lax.dot_general(left, right, (((1,), (1,)), ((), ())), preferred_element_type=F32)


def tn(left, right):
    return lax.dot_general(left, right, (((0,), (0,)), ((), ())), preferred_element_type=F32)


def norm_parts(values):
    average = jnp.mean(values, axis=-1, keepdims=True)
    centred = values - average
    spread = jnp.mean(centred * centred, axis=-1, keepdims=True)
    rate = lax.rsqrt(spread + EPSILON)
    return centred * rate, rate


def norm_back(grad, unit, rate, gain):
    scaled = grad * gain
    first = jnp.mean(scaled, axis=-1, keepdims=True)
    second = jnp.mean(scaled * unit, axis=-1, keepdims=True)
    return rate * (scaled - first - unit * second)


def gelu_both(values):
    square = values * values
    wave = jnp.tanh(0.7978845608028654 * values * (1.0 + 0.044715 * square))
    slope = 0.7978845608028654 * (1.0 + 0.134145 * square)
    half = 0.5 * (1.0 + wave)
    return values * half, half + 0.5 * values * (1.0 - wave * wave) * slope


def head_mask(heads, rows, width):
    row = lax.broadcasted_iota(jnp.int32, (heads * rows, width), 0)
    column = lax.broadcasted_iota(jnp.int32, (heads * rows, width), 1)
    return (row // rows) == (column // E)


def spread_heads(values, heads):
    rows, width = values.shape
    stacked = jnp.concatenate([values] * heads, axis=0)
    return jnp.where(head_mask(heads, rows, width), stacked, jnp.zeros_like(stacked))


def fold_heads(values, heads):
    rows, width = values.shape[0] // heads, values.shape[1]
    kept = jnp.where(head_mask(heads, rows, width), values, jnp.zeros_like(values))
    total = kept[:rows]
    for h in range(1, heads):
        total = total + kept[h * rows : (h + 1) * rows]
    return total


def half_mask(width):
    return lax.broadcasted_iota(jnp.int32, (1, width), 1) < E


def head_only(values, second):
    mask = half_mask(values.shape[1])
    zero = jnp.zeros_like(values)
    return jnp.where(mask, zero, values) if second else jnp.where(mask, values, zero)


def load_kernel(*refs):
    count = (len(refs) - 1) // 2
    ready = refs[-1]
    copies = [
        pltpu.make_async_copy(refs[i], refs[count + i], ready.at[i]) for i in range(count)
    ]
    for copy in copies:
        copy.start()
    for copy in copies:
        copy.wait()


def join_kernel(*refs):
    at = 0
    for r in refs[:-1]:
        refs[-1][at : at + r.shape[0], :] = r[...]
        at += r.shape[0]


def enter_kernel(g, tokens, gain, wq, wk, wv, saved_out):
    unit, _ = norm_parts(tokens[g * S : (g + 1) * S, :].astype(F32))
    low = (unit * gain[...].reshape(1, -1)).astype(B16)
    width = wq.shape[1]
    saved_out[:, :width] = nn(low, wq[...]).astype(B16)
    saved_out[:, width : 2 * width] = nn(low, wk[...]).astype(B16)
    saved_out[:, 2 * width : 3 * width] = nn(low, wv[...]).astype(B16)
    saved_out[:, 3 * width :] = low


def image_rows(order, groups, me, group_image):
    count = len(order) * groups * L
    lane = lax.broadcasted_iota(jnp.int32, (8, count), 1) // L
    images = jnp.zeros((8, count), F32)
    for j, bits in enumerate(order):
        for g in range(groups):
            image = group_image[(me ^ bits) * groups + g].astype(F32)
            images = jnp.where(lane == j * groups + g, image, images)
    return images[:1], images.T[:, :1]


def latent_kernel(
    heads, own, order, me, group_image, one, two, gain, wq, wk, wv, wo, latents_out, q_out, k_out, v_out, part_out
):
    latents = jnp.concatenate([one[...], two[...]], axis=0)
    latents_out[...] = latents
    unit, _ = norm_parts(latents.astype(F32))
    low = (unit * gain[...].reshape(1, -1)).astype(B16)
    q = nn(low, wq[...]).astype(B16)
    k = nn(low, wk[...]).astype(B16)
    v = nn(low, wv[...]).astype(B16)
    q_out[...] = q
    k_out[...] = k
    v_out[...] = v
    scores = nt(spread_heads(q[:own], heads), k) * FACTOR
    images, column = image_rows(order, own // L, me[0], group_image)
    member = jnp.concatenate([column[:own]] * heads, axis=0) == images
    scores = jnp.where(member, scores, NEGATIVE)
    weights = jnp.exp(scores - jnp.max(scores, axis=-1, keepdims=True))
    probs = weights / jnp.sum(weights, axis=-1, keepdims=True)
    mixed = fold_heads(nn(probs.astype(B16), v), heads).astype(B16)
    part_out[...] = nn(mixed, wo[...]).astype(B16)


def pair_of(saved, pair, width):
    start = pair * 2 * E
    return [saved[:, i * width + start : i * width + start + 2 * E] for i in range(3)]


def attend_kernel(
    g, heads, saved, latents, part_one, part_two, gain, wk, wv,
    o_out, probs_out, side_out, mid_out, mid_low_out,
):
    mid = latents[...].astype(F32) + (part_one[...].astype(F32) + part_two[...].astype(F32))
    mid_out[...] = mid
    mid_low_out[...] = mid.astype(B16)
    unit, _ = norm_parts(mid[g * L : (g + 1) * L])
    side_low = (unit * gain[...].reshape(1, -1)).astype(B16)
    side_k = nn(side_low, wk[...]).astype(B16).astype(F32)
    side_v = nn(side_low, wv[...]).astype(B16).astype(F32)
    width = side_k.shape[1]
    side_out[:, :width] = side_k
    side_out[:, width : 2 * width] = side_v
    side_out[:, 2 * width :] = side_low.astype(F32)
    side_v = spread_heads(side_v, heads).astype(B16)
    side_scores = nt(spread_heads(side_k, heads).astype(B16), saved[:, :width])
    scale = FACTOR * LOG2E
    outs, side_probs, lses = [], [], []
    for pair in range(heads // 2):
        q_pair, k_pair, v_pair = pair_of(saved, pair, width)
        for second in (0, 1):
            h = 2 * pair + second
            scores = nt(head_only(k_pair, second), q_pair)
            side = side_scores[h * L : (h + 1) * L]
            top = jnp.maximum(
                jnp.max(scores, axis=0, keepdims=True), jnp.max(side, axis=0, keepdims=True)
            )
            weights = jnp.exp2((scores - top) * scale)
            side = jnp.exp2((side - top) * scale)
            total = jnp.sum(weights, axis=0, keepdims=True) + jnp.sum(side, axis=0, keepdims=True)
            inverse = 1.0 / total
            side_probs.append(side * inverse)
            lses.append(top * scale + jnp.log2(total))
            outs.append(tn((weights * inverse).astype(B16), v_pair))
    side_probs = jnp.concatenate(side_probs, axis=0)
    probs_out[: heads * L, :] = side_probs
    probs_out[heads * L :, :] = jnp.concatenate(
        lses + [jnp.zeros_like(lses[0])] * (8 - heads), axis=0
    )
    side_o = tn(side_probs.astype(B16), side_v)
    first = half_mask(2 * E)
    token_o = jnp.concatenate(
        [jnp.where(first, outs[2 * i], outs[2 * i + 1]) for i in range(heads // 2)], axis=1
    )
    o_out[...] = (token_o + side_o).astype(B16)


def feed_kernel(
    g, chunk, place, tokens, o, o_two, wo, wo_two, cotangent, gain, up, up_bias, down, *rest
):
    part_outs, outs = rest[:-7], rest[-7:]
    active_out, hidden_grad_out, low_out, middle_out, down_part_out, up_bias_out, down_bias_out = outs
    rows = slice(g * S, (g + 1) * S)
    first = place[0] == 0
    o_first = jnp.where(first, o[...], o_two[...])
    o_second = jnp.where(first, o_two[...], o[...])
    wo_first = jnp.where(first, wo[...], wo_two[...])
    wo_second = jnp.where(first, wo_two[...], wo[...])
    middle = tokens[rows, :].astype(F32) + (nn(o_first, wo_first) + nn(o_second, wo_second))
    middle_out[...] = middle
    unit, _ = norm_parts(middle)
    low = (unit * gain[...].reshape(1, -1)).astype(B16)
    low_out[...] = low
    outer = cotangent[rows, :]
    down_bias_out[...] = jnp.sum(outer.astype(F32), axis=0, keepdims=True)
    part, down_part = None, None
    for start in range(0, up.shape[1], chunk):
        cut = slice(start, start + chunk)
        hidden = nn(low, up[:, cut]) + up_bias[cut].reshape(1, -1)
        active, slope = gelu_both(hidden)
        active = active.astype(B16)
        active_out[:, cut] = active
        grad = (slope * nt(outer, down[cut, :])).astype(B16)
        hidden_grad_out[:, cut] = grad
        up_bias_out[:, cut] = jnp.sum(grad.astype(F32), axis=0, keepdims=True)
        one = nt(grad, up[:, cut])
        two = nn(active, down[cut, :])
        part = one if part is None else part + one
        down_part = two if down_part is None else down_part + two
    at = 0
    for out in part_outs:
        out[...] = part[at : at + out.shape[0]].astype(B16)
        at += out.shape[0]
    down_part_out[...] = down_part.astype(B16)


def turn_kernel(
    g, heads, cuts, last, cotangent, middle, gain, wo, wk, wv, o, saved, probs, side, mid, *rest
):
    parts, rest = rest[: 2 * cuts], rest[2 * cuts :]
    earlier, outs = rest[:-8], rest[-8:]
    o_grad_out, delta_out, side_score_grad_out, part_out, grads_out, gain_out = outs[:6]
    middle_grad_out, middle_low_out = outs[6:]
    unit, rate = norm_parts(middle[...])
    sides = [jnp.concatenate([r[...] for r in rs], axis=0) for rs in (parts[:cuts], parts[cuts:])]
    grad = sides[0].astype(F32) + sides[1].astype(F32)
    gain_out[0:1, :] = jnp.sum(grad * unit, axis=0, keepdims=True)
    outer = cotangent[g * S : (g + 1) * S, :].astype(F32)
    middle_grad = outer + norm_back(grad, unit, rate, gain[...].reshape(1, -1))
    middle_grad_out[...] = middle_grad
    middle_low = middle_grad.astype(B16)
    middle_low_out[...] = middle_low
    o_grad = nt(middle_low, wo[...]).astype(B16)
    o_grad_out[...] = o_grad
    width = o_grad.shape[1]
    rows8 = lax.broadcasted_iota(jnp.int32, (8, width), 0)
    columns8 = lax.broadcasted_iota(jnp.int32, (8, width), 1) // E
    pick = (rows8 == columns8).astype(B16)
    weighted = o_grad.astype(F32) * o[...].astype(F32)
    high = weighted.astype(B16)
    low = (weighted - high.astype(F32)).astype(B16)
    delta = nt(pick, high) + nt(pick, low)
    delta_out[...] = delta
    side_v = spread_heads(side[:, width : 2 * width], heads).astype(B16)
    side_prob_grad = nt(side_v, o_grad)
    side_probs = probs[: heads * L, :]
    wide = jnp.concatenate(
        [jnp.broadcast_to(delta[h : h + 1], (L, delta.shape[1])) for h in range(heads)], axis=0
    )
    score_grad = (side_probs * (side_prob_grad - wide)).astype(B16)
    side_score_grad_out[...] = score_grad
    k_grad = (fold_heads(nn(score_grad, saved[:, :width]), heads) * FACTOR).astype(B16)
    v_grad = fold_heads(nn(side_probs.astype(B16), o_grad), heads).astype(B16)
    grads_out[:, :width] = k_grad.astype(F32)
    grads_out[:, width:] = v_grad.astype(F32)
    part = nt(k_grad, wk[...]) + nt(v_grad, wv[...])
    side_unit, _ = norm_parts(mid[g * L : (g + 1) * L, :])
    gain_out[1:2, :] = jnp.sum(part * side_unit, axis=0, keepdims=True)
    gain_out[2:, :] = jnp.zeros_like(gain_out[2:, :])
    if last:
        part = jnp.concatenate([r[...] for r in earlier] + [part], axis=0)
    part_out[...] = part.astype(part_out.dtype)


def side_kernel(part_one, part_two, mid, cotangent, gain, low_out, grad_out):
    unit, rate = norm_parts(mid[...])
    part = part_one[...].astype(F32) + part_two[...].astype(F32)
    grad = cotangent[...].astype(F32) + norm_back(part, unit, rate, gain[...].reshape(1, -1))
    grad_out[...] = grad
    low_out[...] = grad.astype(B16)


def attend_back_kernel(
    g, heads, tokens, saved, o_grad, probs, delta, side_score_grad, side, wq, wk, wv, *rest
):
    part_out, grads_out, gain_out = rest[-3:]
    gains, earlier = rest[: min(g, 1) + 1], rest[min(g, 1) + 1 : -3]
    scale = FACTOR * LOG2E
    first = half_mask(2 * E)
    width = o_grad.shape[1]
    side_k = spread_heads(side[:, :width], heads).astype(B16)
    side_q_grad = tn(side_score_grad[...], side_k)
    at = heads * L
    for pair in range(heads // 2):
        start = pair * 2 * E
        cut = slice(start, start + 2 * E)
        q_pair, k_pair, v_pair = pair_of(saved, pair, width)
        grad_pair = o_grad[:, cut]
        q_grads, k_grads, v_grads = [], [], []
        for second in (0, 1):
            h = 2 * pair + second
            scores = nt(head_only(k_pair, second), q_pair)
            weights = jnp.exp2(scores * scale - probs[at + h : at + h + 1, :])
            prob_grad = nt(head_only(v_pair, second), grad_pair)
            score_grad = (weights * (prob_grad - delta[h : h + 1, :])).astype(B16)
            v_grads.append(nn(weights.astype(B16), grad_pair))
            k_grads.append(nn(score_grad, q_pair))
            q_grads.append(tn(score_grad, k_pair))
        q_pair_grad = jnp.where(first, q_grads[0], q_grads[1]) + side_q_grad[:, cut]
        k_pair_grad = jnp.where(first, k_grads[0], k_grads[1])
        v_pair_grad = jnp.where(first, v_grads[0], v_grads[1])
        grads_out[:, start : start + 2 * E] = (q_pair_grad * FACTOR).astype(B16)
        grads_out[:, width + start : width + start + 2 * E] = (k_pair_grad * FACTOR).astype(B16)
        grads_out[:, 2 * width + start : 2 * width + start + 2 * E] = v_pair_grad.astype(B16)
    part = nt(grads_out[:, :width], wq[...]) + nt(grads_out[:, width : 2 * width], wk[...])
    part = part + nt(grads_out[:, 2 * width :], wv[...])
    for i, r in enumerate(earlier):
        part_out[i * S : (i + 1) * S, :] = r[...]
    part_out[len(earlier) * S :, :] = part.astype(B16)
    unit, _ = norm_parts(tokens[g * S : (g + 1) * S, :].astype(F32))
    total = gains[0][1:2, :] + jnp.sum(part * unit, axis=0, keepdims=True)
    for r in gains[1:]:
        total = total + r[...]
    gain_out[...] = total


def leave_kernel(tokens, gain, part_one, part_two, *refs):
    middle_grad, grad_out = refs[:-1], refs[-1]
    for g in range(len(middle_grad)):
        rows = slice(g * S, (g + 1) * S)
        unit, rate = norm_parts(tokens[rows, :].astype(F32))
        grad = part_one[rows, :].astype(F32) + part_two[rows, :].astype(F32)
        grad_out[rows, :] = middle_grad[g][...] + norm_back(grad, unit, rate, gain[...].reshape(1, -1))


def result_kernel(middle, part_one, part_two, bias, *refs):
    earlier, out = refs[:-1], refs[-1]
    at = 0
    for r in earlier:
        out[at : at + S, :] = r[...]
        at += S
    total = part_one[...].astype(F32) + part_two[...].astype(F32)
    out[at:, :] = (middle[...] + total + bias[...].reshape(1, -1)).astype(B16)


def latent_leave_kernel(me, latents, part_one, part_two, gain, mid_grad, grad_out, gain_out):
    own = latents.shape[0]
    unit, rate = norm_parts(latents[...].astype(F32))
    start = part_one.shape[0] - own - 16
    total = part_one[start:, :].astype(F32) + part_two[start:, :].astype(F32)
    grad_out[...] = mid_grad[...] + norm_back(total[:own], unit, rate, gain[...].reshape(1, -1))
    share, model = gain_out.shape[1], gain.shape[0]
    row = lax.broadcasted_iota(jnp.int32, (share, model), 0)
    column = lax.broadcasted_iota(jnp.int32, (share, model), 1)
    kept = jnp.where(column == row + me[0] * share, total[own : own + 1], 0.0)
    gain_out[...] = jnp.broadcast_to(jnp.sum(kept, axis=1, keepdims=True), (share, 8)).T


def split_pairs(values, bit, share, send_out, keep_out):
    blocks = values.reshape(values.shape[0] // (2 * share), 2, share, values.shape[1])
    even, odd = blocks[:, 0], blocks[:, 1]
    send_out[...] = jnp.where(bit == 0, odd, even).astype(B16)
    keep_out[...] = jnp.where(bit == 0, even, odd).astype(B16)


def weight_grad_kernel(groups, share, pieces, me, cotangent, *refs):
    active, low, hidden_grad = (refs[i * groups : (i + 1) * groups] for i in range(3))
    outs = refs[3 * groups :]
    bit = me[0] % 2
    width = active[0].shape[1]
    at = 0
    for count, lefts, rights in (
        (pieces[0], [cotangent[g * S : (g + 1) * S, :].T for g in range(groups)], active),
        (pieces[1], [r[...].T for r in low], hidden_grad),
    ):
        chunk = width // count
        for k in range(count):
            cut = slice(k * chunk, (k + 1) * chunk)
            total = nn(lefts[0], rights[0][:, cut])
            for g in range(1, groups):
                total = total + nn(lefts[g], rights[g][:, cut])
            split_pairs(total, bit, share, outs[at], outs[at + 1])
            at += 2


def attention_grad_kernel(groups, share, me, *refs):
    saved, grads, middle_low, o, side, side_grads = (
        refs[i * groups : (i + 1) * groups] for i in range(6)
    )
    outs = refs[6 * groups :]
    bit = me[0] % 2
    width = o[0].shape[1]
    stack = [jnp.concatenate([r[...] for r in rs], axis=0) for rs in (side, side_grads)]
    side_low = stack[0][:, 2 * width :].astype(B16)
    side_k, side_v = stack[1][:, :width].astype(B16), stack[1][:, width:].astype(B16)
    flat = [r[:, 3 * width :].T for r in saved]
    low_flat = [r[...].T for r in middle_low]

    def total_of(lefts, rights, cut):
        total = nn(lefts[0], rights[0][:, cut])
        for g in range(1, groups):
            total = total + nn(lefts[g], rights[g][:, cut])
        return total

    def cut_of(i):
        return slice(i * width, (i + 1) * width)

    totals = (
        total_of(flat, grads, cut_of(0)),
        total_of(flat, grads, cut_of(1)) + tn(side_low, side_k),
        total_of(flat, grads, cut_of(2)) + tn(side_low, side_v),
        total_of(low_flat, o, cut_of(0)),
    )
    for i, total in enumerate(totals):
        split_pairs(total, bit, share, outs[2 * i], outs[2 * i + 1])


def sum_of(parts):
    total = parts[0]
    for part in parts[1:]:
        total = total + part
    return total


def vector_kernel(groups, share, me, one, two, *refs):
    up_bias, down_bias, gains = (refs[i * groups : (i + 1) * groups] for i in range(3))
    send_out, keep_out = refs[3 * groups :]
    model = one.shape[1]
    gain = one[...] + two[...]

    def column(rows):
        return jnp.broadcast_to(rows, (8, rows.shape[1])).T

    columns = [
        column(sum_of([r[...] for r in down_bias])),
        column(sum_of([r[0:1, :] for r in gains])),
        column(gain),
    ]
    bias = column(sum_of([r[...] for r in up_bias]))
    times = bias.shape[0] // model
    bias = bias.reshape(model // share, times, share, 8)
    columns += [bias[:, i].reshape(model, 8) for i in range(times)]
    lane = lax.broadcasted_iota(jnp.int32, (model, 128), 1)
    block = jnp.zeros((model, 128), F32)
    for i, one in enumerate(columns):
        block = jnp.where(lane == i, one[:, 0:1], block)
    split_pairs(block, me[0] % 2, share, send_out, keep_out)


def halve_kernel(shift, pieces, cuts, me, *refs):
    count = len(pieces)
    keeps, gots, outs = refs[:count], refs[count : 2 * count], refs[2 * count :]
    bit = (me[0] // shift) % 2
    for keep, got, (first, last) in zip(keeps, gots, pieces):
        for k, (start, end) in enumerate(cuts):
            low, high = max(first, start), min(last, end)
            if low >= high:
                continue
            of_piece, of_out = slice(low - first, high - first), slice(low - start, high - start)
            for i in range(keep.shape[0]):
                there, here = (
                    keep[i, pl.ds(at, 1), :, of_piece].astype(F32)
                    + got[i, pl.ds(at, 1), :, of_piece].astype(F32)
                    for at in (1 - bit, bit)
                )
                outs[2 * k][pl.ds(i, 1), :, of_out] = there.astype(B16)
                outs[2 * k + 1][pl.ds(i, 1), :, of_out] = here


def finish_kernel(cuts, keep, got, *outs):
    total = keep[0] + got[0].astype(F32)
    for out, (start, end, flat) in zip(outs, cuts):
        part = total[:, start:end]
        out[...] = part.T[: out.shape[0]] if flat else part


def latent_back_kernel(
    heads, own, order, block, me, group_image, token_part, latents, q, k, v, mid_one, mid_two, gain, wq, wk, wv, wo,
    part_out, wq_out, wk_out, wv_out, wo_out, mixed, q_grad, k_grad, v_grad, images,
):
    mid_low = jnp.concatenate([mid_one[...], mid_two[...]], axis=0)
    o_grad = nt(mid_low, wo[...]).astype(B16)
    unit, _ = norm_parts(latents[...].astype(F32))
    low = (unit * gain[...].reshape(1, -1)).astype(B16)
    everyone = low.shape[0]
    images_row, images_column = image_rows(order, own // L, me[0], group_image)

    def rows_of(start, ref_q, ref_grad, ref_images):
        wide_q = spread_heads(ref_q, heads)
        wide_grad = spread_heads(ref_grad, heads)
        scores = nt(wide_q, k[...]) * FACTOR
        member = jnp.concatenate([ref_images] * heads, axis=0) == images_row
        scores = jnp.where(member, scores, NEGATIVE)
        weights = jnp.exp(scores - jnp.max(scores, axis=-1, keepdims=True))
        probs = weights / jnp.sum(weights, axis=-1, keepdims=True)
        probs_low = probs.astype(B16)
        prob_grad = nt(wide_grad, v[...])
        delta = jnp.sum(prob_grad * probs, axis=-1, keepdims=True)
        score_grad = (probs * (prob_grad - delta)).astype(B16)
        mixed[pl.ds(start, block), :] = fold_heads(nn(probs_low, v[...]), heads).astype(B16)
        q_grad[pl.ds(start, block), :] = (
            fold_heads(nn(score_grad, k[...]), heads) * FACTOR
        ).astype(B16)
        return tn(score_grad, wide_q), tn(probs_low, wide_grad)

    if block == everyone:
        k_sum, v_sum = rows_of(0, q[...], o_grad, images_column)
        k_sum, v_sum = k_sum * FACTOR, v_sum
    else:
        v_grad[...] = o_grad
        images[...] = jnp.broadcast_to(images_column, images.shape)

        def step(i, held):
            start = pl.multiple_of(i * block, block)
            here = pl.ds(start, block)
            one, two = rows_of(start, q[here, :], v_grad[here, :], images[here, :][:, :1])
            return held[0] + one, held[1] + two

        zero = jnp.zeros(k.shape, F32)
        k_sum, v_sum = lax.fori_loop(0, everyone // block, step, (zero, zero))
        k_sum = k_sum * FACTOR
    k_grad[...] = k_sum.astype(B16)
    v_grad[...] = v_sum.astype(B16)
    part = nt(q_grad[...], wq[...]) + nt(k_grad[...], wk[...]) + nt(v_grad[...], wv[...])
    gain_part = jnp.sum(part * unit, axis=0, keepdims=True)
    rows = token_part.shape[0]
    part_out[:rows, :] = token_part[...]
    part_out[rows:, :] = jnp.concatenate(
        [part[:own], jnp.broadcast_to(gain_part, (16, part.shape[1]))], axis=0
    ).astype(B16)
    share = wq_out.shape[0]
    model = low.shape[1]
    row = lax.broadcasted_iota(jnp.int32, (share, model), 0)
    column = lax.broadcasted_iota(jnp.int32, (share, model), 1)
    pick = (column == row + me[0] * share).astype(B16)
    columns = nt(pick, low).astype(B16)
    wq_out[...] = nn(columns, q_grad[...])
    wk_out[...] = nn(columns, k_grad[...])
    wv_out[...] = nn(columns, v_grad[...])
    wo_out[...] = nn(nt(pick, mid_low).astype(B16), mixed[...])


MIB = 1024 * 1024
OUT = "out"


class Order:
    def __init__(self, pinned):
        self.pinned, self.last = pinned, None

    def call(self, kernel, name, outs, ins, scratch=(), limit=16, behind=(), loose=False):
        scalars = [isinstance(a, tuple) for a in ins]
        arrays = [a[1] if isinstance(a, tuple) else a for a in ins]
        earlier = tuple(behind) + (() if self.last is None or loose else (self.last,))
        if earlier:
            least = min(range(len(arrays)), key=lambda i: arrays[i].size)
            arrays[least] = after(arrays[least], *earlier)
        if self.pinned:
            arrays = [
                a if scalar else pltpu.with_memory_space_constraint(a, pltpu.VMEM)
                for a, scalar in zip(arrays, scalars)
            ]

        def result(shape, dtype, kind=None):
            if self.pinned and kind != OUT:
                return pltpu.VMEM(shape, dtype)
            return jax.ShapeDtypeStruct(shape, dtype)

        def whole(shape):
            return pl.BlockSpec(tuple(shape), lambda: (0,) * len(shape))

        results = pl.pallas_call(
            kernel,
            out_shape=[result(*out) for out in outs],
            in_specs=[
                pl.BlockSpec(memory_space=pltpu.SMEM) if scalar else whole(a.shape)
                for a, scalar in zip(arrays, scalars)
            ],
            out_specs=[whole(out[0]) for out in outs],
            scratch_shapes=list(scratch),
            compiler_params=pltpu.CompilerParams(vmem_limit_bytes=limit * MIB),
            cost_estimate=pl.CostEstimate(flops=0, bytes_accessed=0, transcendentals=0),
            name=name,
        )(*arrays)
        if not loose:
            self.last = min(results, key=lambda a: a.size)
        return results

    def load(self, *arrays, behind=()):
        if not self.pinned:
            return arrays
        sources = list(arrays)
        earlier = tuple(behind) + (() if self.last is None else (self.last,))
        if earlier:
            sources[0] = after(sources[0], *earlier)
        results = pl.pallas_call(
            load_kernel,
            out_shape=[pltpu.VMEM(a.shape, a.dtype) for a in arrays],
            in_specs=[pl.BlockSpec(memory_space=pltpu.HBM)] * len(arrays),
            out_specs=[pl.BlockSpec(memory_space=pltpu.VMEM)] * len(arrays),
            scratch_shapes=[pltpu.SemaphoreType.DMA((len(arrays),))],
            compiler_params=pltpu.CompilerParams(vmem_limit_bytes=MIB),
            cost_estimate=pl.CostEstimate(flops=0, bytes_accessed=0, transcendentals=0),
            name="load",
        )(*[pltpu.with_memory_space_constraint(a, pltpu.HBM) for a in sources])
        self.last = min(results, key=lambda a: a.size)
        return results


def after(value, *earlier):
    return lax.optimization_barrier((value, earlier))[0]


def swap_tp(values, name):
    with jax.named_scope("swap_" + name):
        return lax.ppermute(values, "tp", [(0, 1), (1, 0)])


def flip(values, bits, name):
    size = lax.axis_size("dp")
    with jax.named_scope("flip_" + name):
        return lax.ppermute(values, "dp", [(i, i ^ bits) for i in range(size)])


def gather_steps(size):
    width, steps = 2, []
    while width * 4 < size:
        steps.append([width])
        width *= 2
    if width < size:
        steps.append([width * k for k in range(1, size // width)])
    steps.reverse()
    return steps + [[1]]


def one_by_one(steps):
    result = []
    for step in steps:
        result += [[b] for b in step if b & (b - 1) == 0]
    return result


def gather_order(size):
    order = [0]
    for step in gather_steps(size):
        order = order + [i ^ bits for bits in [0] + step for i in order][len(order) :]
    return order


def scatter_sum(grads):
    size = lax.axis_size("dp")
    me = lax.axis_index("dp")
    width = 1
    while width * 4 < size:
        bit = (me // width) % 2
        pairs = grads.reshape((grads.shape[0] // 2, 2) + grads.shape[1:])
        send = lax.dynamic_index_in_dim(pairs, 1 - bit, 1, keepdims=False)
        keep = lax.dynamic_index_in_dim(pairs, bit, 1, keepdims=False)
        got = flip(send.astype(B16), width, "sums")
        grads = keep.astype(F32) + got.astype(F32)
        width *= 2
    place = me // width
    total = lax.dynamic_index_in_dim(grads, place, 0, keepdims=False)
    for k in range(1, size // width):
        send = lax.dynamic_index_in_dim(grads, place ^ k, 0, keepdims=False)
        total = total + flip(send.astype(B16), width * k, "sums").astype(F32)
    return total


class Scatter:
    def __init__(self, order, me, width, keeps, sends, name):
        self.order, self.me, self.width, self.keeps = order, me, width, list(keeps)
        self.gots = [flip(a, width, name) for a in sends]
        self.pieces, self.columns = [], 0
        for a in self.keeps:
            self.pieces.append((self.columns, self.columns + a.shape[2]))
            self.columns += a.shape[2]

    def halve(self, cuts=None, behind=()):
        cuts = [(0, self.columns)] if cuts is None else cuts
        n, share, _ = self.keeps[0].shape
        shapes = [(n // 2, share, end - start) for start, end in cuts]
        results = self.order.call(
            partial(halve_kernel, 2 * self.width, self.pieces, cuts),
            "halve",
            [out for shape in shapes for out in ((shape, B16), (shape, F32))],
            [("smem", self.me)]
            + [a.reshape((n // 2, 2) + a.shape[1:]) for a in self.keeps + self.gots],
            behind=behind,
        )
        return results[::2], results[1::2]

    def next(self, name, *ties):
        (send,), (keep,) = self.halve()
        send = after(send, *ties) if ties else send
        return Scatter(self.order, self.me, 2 * self.width, [keep], [send], name)

    def finish(self, cuts):
        share = self.keeps[0].shape[1]
        shapes = [(8, share) if flat else (share, e - s) for s, e, flat in cuts]
        return self.order.call(
            partial(finish_kernel, cuts),
            "finish",
            [(shape, F32, OUT) for shape in shapes],
            self.keeps + self.gots,
        )


ORDER = (
    "load_small",
    "gather_0",
    "load_first",
    "enter_0",
    "gather_1",
    "enter_1",
    "latent",
    "load_feed",
    "attend_0",
    "attend_1",
    "feed_0",
    "feed_1",
    "weight_grad",
    "turn_0",
    "down_y",
    "turn_1",
    "back_0",
    "result_0",
    "side",
    "back_1",
    "gather_mid_0",
    "attention_grad",
    "gather_mid_1",
    "vectors",
    "gather_mid_2",
    "up_y",
    "down_z",
    "first_y",
    "second_y",
    "latent_back",
    "down_zz",
    "up_z",
    "first_z",
    "up_zz",
    "down_done",
    "first_zz",
    "up_done",
    "second_z",
    "result_1",
    "latent_leave",
    "leave",
    "second_zz",
    "first_done",
    "second_done",
)
SUMS = (
    "weight_grad",
    "down_y",
    "attention_grad",
    "vectors",
    "up_y",
    "down_z",
    "first_y",
    "second_y",
    "down_zz",
    "up_z",
    "first_z",
    "up_zz",
    "down_done",
    "first_zz",
    "up_done",
    "second_z",
    "second_zz",
    "first_done",
    "second_done",
)
PIECES = (4, 2)
TIE_UP = True
TIE_DOWN_0 = "turn"
TIE_DOWN_1 = "gain"
MID_DIRECT = False


def local(
    tokens,
    latents,
    latent_query,
    latent_key,
    latent_value,
    latent_output,
    query_weight,
    key_weight,
    value_weight,
    output_weight,
    up_weight,
    up_bias,
    down_weight,
    down_bias,
    latent_gain,
    attention_gain,
    feed_gain,
    group_image,
    token_cotangent,
    latent_cotangent,
):
    size = lax.axis_size("dp")
    me = lax.axis_index("dp")
    me_row = me.reshape(1)
    place = lax.axis_index("tp").reshape(1)
    width = latent_query.shape[1]
    heads = width // E
    rows, model = tokens.shape
    hidden_units = up_weight.shape[1]
    groups = rows // S
    own = latents.shape[0]
    everyone = own * size
    share = model // size
    small = everyone <= 512
    aligned = share % 16 == 0 and size >= 8
    each = range(groups)
    scalars = (me_row, place)
    chain = Order(small)
    call = chain.call
    latent_limit = 16 if small else 56
    gathered = gather_steps(size)
    turns = tuple(gather_order(size))

    def join(parts):
        if not small:
            return jnp.concatenate(parts, axis=0)
        shape = (sum(p.shape[0] for p in parts), model)
        return call(join_kernel, "join", [(shape, B16)], parts)[0]

    at = {}
    output_weight_two = swap_tp(output_weight, "output_weight")

    def load_small():
        at["latents_held"] = latents
        names = ("latents", "latent_cotangent", "latent_gain", "attention_gain", "feed_gain")
        values = chain.load(
            latents,
            latent_cotangent,
            latent_gain,
            attention_gain,
            feed_gain,
            up_bias,
            down_bias,
            behind=scalars,
        )
        for name, value in zip(names + ("up_bias_row", "down_bias_row"), values):
            at[name] = value

    def gather(name, steps, first):
        held = at[name]
        others = [flip(held, bits, name) for bits in steps]
        at[name] = join([at["latents"] if first else held] + others)

    def load_all():
        at["tokens"], *weights = chain.load(
            tokens,
            query_weight,
            key_weight,
            value_weight,
            output_weight,
            latent_query,
            latent_key,
            latent_value,
            latent_output,
        )
        at["group_weights"], at["output_weight"], at["latent_weights"] = (
            weights[:3],
            weights[3],
            weights[4:],
        )

    def enter(g):
        (at["saved", g],) = call(
            partial(enter_kernel, g),
            "enter",
            [((S, 3 * width + model), B16)],
            [at["tokens"], at["attention_gain"], *at["group_weights"]],
        )

    def latent():
        held = at["latents_held"]
        at["latents_all"], *at["latent_qkv"], at["latent_part"] = call(
            partial(latent_kernel, heads, own, turns),
            "latent",
            [((everyone, model), B16)] + [((everyone, width), B16)] * 3 + [((own, model), B16)],
            [
                ("smem", me_row),
                ("smem", group_image),
                held,
                flip(held, 1, "latents_held"),
                at["latent_gain"],
                *at["latent_weights"],
            ],
            limit=latent_limit,
        )
        at["latent_part_two"] = swap_tp(at["latent_part"], "latent_part")

    def load_feed():
        at["up_weight"], at["down_weight"], at["cotangent"] = chain.load(
            up_weight, down_weight, token_cotangent
        )

    def attend(g):
        at["o", g], at["probs", g], at["side", g], mid, mid_low = call(
            partial(attend_kernel, g, heads),
            "attend",
            [
                ((S, width), B16),
                ((heads * L + 8, S), F32),
                ((L, 2 * width + model), F32),
                ((own, model), F32),
                ((own, model), B16, OUT),
            ],
            [
                at["saved", g],
                at["latents"],
                at["latent_part"],
                at["latent_part_two"],
                at["attention_gain"],
                *at["group_weights"][1:],
            ],
        )
        if g == 0:
            at["mid"], at["mixed_latents"] = mid, mid_low
        at["o_two", g] = swap_tp(at["o", g], "o")

    def feed(g):
        count = 1 if g == groups - 1 else 2
        results = call(
            partial(feed_kernel, g, hidden_units // 3),
            "feed",
            [((S // count, model), B16)] * count
            + [
                ((S, hidden_units), B16),
                ((S, hidden_units), B16),
                ((S, model), B16),
                ((S, model), F32),
                ((S, model), B16),
                ((1, hidden_units), F32),
                ((1, model), F32),
            ],
            [
                ("smem", place),
                at["tokens"],
                at["o", g],
                at["o_two", g],
                at["output_weight"],
                output_weight_two,
                at["cotangent"],
                at["feed_gain"],
                at["up_weight"],
                at["up_bias_row"],
                at["down_weight"],
            ],
        )
        at["feed_part", g] = results[:count]
        names = ("active", "hidden_grad", "feed_low", "middle", "down_part", "up_bias", "down_bias")
        for name, value in zip(names, results[count:]):
            at[name, g] = value
        at["feed_part_two", g] = [swap_tp(p, "feed_part") for p in results[:count]]

    def weight_grad():
        outs = []
        for count in PIECES:
            outs += [((size // 2, share, hidden_units // count), B16)] * (2 * count)
        halves = call(
            partial(weight_grad_kernel, groups, share, PIECES),
            "weight_grad",
            outs,
            [("smem", me_row), at["cotangent"]]
            + [at[name, g] for name in ("active", "feed_low", "hidden_grad") for g in each],
        )
        at["down_halves"], at["up_halves"] = halves[: 2 * PIECES[0]], halves[2 * PIECES[0] :]

    def turn(g):
        last = g == groups - 1
        names = (
            "o_grad",
            "delta",
            "side_score_grad",
            "side_part",
            "side_grads",
            "gains",
            "middle_grad",
            "middle_low",
        )
        results = call(
            partial(turn_kernel, g, heads, len(at["feed_part", g]), last),
            "turn",
            [
                ((S, width), B16),
                ((8, S), F32),
                ((heads * L, S), B16),
                ((own if last else L, model), B16 if last else F32),
                ((L, 2 * width), F32),
                ((8, model), F32),
                ((S, model), F32),
                ((S, model), B16),
            ],
            [
                at["cotangent"],
                at["middle", g],
                at["feed_gain"],
                at["output_weight"],
                *at["group_weights"][1:],
                at["o", g],
                at["saved", g],
                at["probs", g],
                at["side", g],
                at["mid"],
                *at["feed_part", g],
                *at["feed_part_two", g],
                *[at["side_part", i] for i in range(g)],
            ],
        )
        for name, value in zip(names, results):
            at[name, g] = value
        if last:
            at["side_part_two"] = swap_tp(at["side_part", g], "side_part")
            if aligned:
                sends = [after(a, at["delta", g]) for a in at["up_halves"][::2]]
                at["up"] = Scatter(chain, me_row, 1, at["up_halves"][1::2], sends, "up_core")
        elif aligned and g == 0:
            sends = [after(a, at["delta", g]) for a in at["down_halves"][::2]]
            at["down"] = Scatter(chain, me_row, 1, at["down_halves"][1::2], sends, "down_core")
        if not last:
            tie = at["delta", 0] if TIE_DOWN_0 == "turn" else at["middle", groups - 1]
            at["down_part_two", g] = swap_tp(after(at["down_part", g], tie), "down_part")

    def back(g):
        last = g == groups - 1
        at["token_part", g], at["grads", g], at["gain"] = call(
            partial(attend_back_kernel, g, heads),
            "attend_back",
            [((rows if last else S, model), B16), ((S, 3 * width), B16), ((1, model), F32)],
            [
                at["tokens"],
                at["saved", g],
                at["o_grad", g],
                at["probs", g],
                at["delta", g],
                at["side_score_grad", g],
                at["side", g],
                *at["group_weights"],
                at["gains", g],
                *([at["gain"]] if g else []),
                *([at["token_part", i] for i in range(g)] if last else []),
            ],
        )
        if last:
            at["gain_two"] = swap_tp(at["gain"], "gain")
            tie = {"gain": "gain_two", "back": "gain", "side": "side_part_two"}[TIE_DOWN_1]
            at["down_part_two", g] = swap_tp(after(at["down_part", g], at[tie]), "down_part")

    def result(g):
        shape, kind = ((rows, model), (OUT,)) if g == groups - 1 else ((S, model), ())
        (at["result", g],) = call(
            result_kernel,
            "result",
            [(shape, B16) + kind],
            [
                at["middle", g],
                at["down_part", g],
                at["down_part_two", g],
                at["down_bias_row"],
                *[at["result", i] for i in range(g)],
            ],
        )

    def side():
        at["mid_held"], at["middle_latent_grad"] = call(
            side_kernel,
            "side",
            [((own, model), B16), ((own, model), F32)],
            [
                at["side_part", groups - 1],
                at["side_part_two"],
                at["mid"],
                at["latent_cotangent"],
                at["attention_gain"],
            ],
        )

    def attention_grad():
        names = ("saved", "grads", "middle_low", "o", "side", "side_grads")
        halves = call(
            partial(attention_grad_kernel, groups, share),
            "attention_grad",
            [((size // 2, share, width), B16)] * 8,
            [("smem", me_row)] + [at[name, g] for name in names for g in each],
        )
        at["first"] = Scatter(chain, me_row, 1, halves[1:4:2], halves[:4:2], "first_core")
        at["second_halves"] = halves[4:]

    def vectors():
        names = ("up_bias", "down_bias", "gains")
        at["vector_halves"] = call(
            partial(vector_kernel, groups, share),
            "vectors",
            [((size // 2, share, 128), B16)] * 2,
            [("smem", me_row), at["gain"], at["gain_two"]]
            + [at[name, g] for name in names for g in each],
        )

    def second_y():
        halves = at["second_halves"] + at["vector_halves"]
        at["second"] = Scatter(chain, me_row, 1, halves[1::2], halves[::2], "second_core")
        advance("second", "second_y")

    def advance(which, name, *ties):
        at[which] = at[which].next(name, *ties)

    def latent_back():
        held = at["mid_held"]
        block = min(everyone, max(16, 65536 // everyone))
        at["all_part"], *at["latent_grads"] = call(
            partial(latent_back_kernel, heads, own, turns, block),
            "latent_back",
            [((rows + own + 16, model), B16)] + [((share, width), F32, OUT)] * 4,
            [
                ("smem", me_row),
                ("smem", group_image),
                at["token_part", groups - 1],
                at["latents_all"],
                *at["latent_qkv"],
                held,
                flip(held, 1, "mid_held"),
                at["latent_gain"],
                *at["latent_weights"],
            ],
            scratch=[pltpu.VMEM((everyone, width), B16)] * 4 + [pltpu.VMEM((everyone, 128), F32)],
            limit=latent_limit,
        )
        at["all_part_two"] = swap_tp(at["all_part"], "all_part")

    def latent_leave():
        at["latent_grad"], at["latent_gain_sum"] = call(
            latent_leave_kernel,
            "latent_leave",
            [((own, model), F32, OUT), ((8, share), F32, OUT)],
            [
                ("smem", me_row),
                at["latents"],
                at["all_part"],
                at["all_part_two"],
                at["latent_gain"],
                at["middle_latent_grad"],
            ],
        )

    def leave():
        (at["token_grad"],) = call(
            leave_kernel,
            "leave",
            [((rows, model), F32, OUT)],
            [at["tokens"], at["attention_gain"], at["all_part"], at["all_part_two"]]
            + [at["middle_grad", g] for g in each],
        )

    def done(which, *cuts):
        at[which, "done"] = at[which].finish(cuts)

    steps = {
        "load_small": load_small,
        "load_first": load_all,
        "latent": latent,
        "load_feed": load_feed,
        "weight_grad": weight_grad,
        "side": side,
        "attention_grad": attention_grad,
        "vectors": vectors,
        "second_y": second_y,
        "latent_back": latent_back,
        "latent_leave": latent_leave,
        "leave": leave,
        "down_done": partial(done, "down", (0, hidden_units, False)),
        "up_done": partial(done, "up", (0, hidden_units, False)),
        "first_done": partial(done, "first", (0, width, False), (width, 2 * width, False)),
        "second_done": partial(
            done,
            "second",
            (0, width, False),
            (width, 2 * width, False),
            (2 * width, 2 * width + 128, True),
        ),
    }
    for name, which in (
        ("down_y", "down"),
        ("down_z", "down"),
        ("down_zz", "down"),
        ("up_z", "up"),
        ("up_zz", "up"),
        ("first_y", "first"),
        ("first_z", "first"),
        ("first_zz", "first"),
        ("second_z", "second"),
        ("second_zz", "second"),
    ):
        steps[name] = partial(advance, which, name)
    steps["up_y"] = lambda: advance("up", "up_y", *(at["down"].gots if TIE_UP else ()))
    for g in each:
        for name, step in (
            ("enter", enter),
            ("attend", attend),
            ("feed", feed),
            ("turn", turn),
            ("back", back),
            ("result", result),
        ):
            steps[f"{name}_{g}"] = partial(step, g)
    for i, bits in enumerate(gathered[:-1]):
        steps[f"gather_{i}"] = partial(gather, "latents_held", bits, i == 0)
    mid_steps = gathered[:-1] if MID_DIRECT else one_by_one(gathered[:-1])
    for i, bits in enumerate(mid_steps):
        steps[f"gather_mid_{i}"] = partial(gather, "mid_held", bits, False)
    order = [name for name in ORDER if name in steps and (aligned or name not in SUMS)]
    for name in steps:
        if name not in order and (aligned or name not in SUMS):
            kind, _, number = name.rpartition("_")
            order.insert(order.index(f"{kind}_{int(number) - 1}") + 1, name)
    for name in order:
        steps[name]()
    if aligned:
        (down_done,), (up_done,) = at["down", "done"], at["up", "done"]
        query_done, key_done = at["first", "done"]
        value_done, output_done, vectors_done = at["second", "done"]
    else:

        def flat(name, start, end):
            return jnp.concatenate([at[name, g][:, start:end] for g in each], axis=0).astype(B16)

        token_low = flat("saved", 3 * width, 3 * width + model)
        side_low = flat("side", 2 * width, 2 * width + model)
        products = (
            tn(token_cotangent, flat("active", 0, hidden_units)),
            tn(flat("feed_low", 0, model), flat("hidden_grad", 0, hidden_units)),
            tn(token_low, flat("grads", 0, width)),
            tn(token_low, flat("grads", width, 2 * width))
            + tn(side_low, flat("side_grads", 0, width)),
            tn(token_low, flat("grads", 2 * width, 3 * width))
            + tn(side_low, flat("side_grads", width, 2 * width)),
            tn(flat("middle_low", 0, model), flat("o", 0, width)),
        )
        bias_rows = sum(at["up_bias", g] for g in each).reshape(size, -1, share)
        rows_of = [
            sum(at["down_bias", g] for g in each),
            sum(at["gains", g] for g in each)[:1],
            at["gain"] + at["gain_two"],
            bias_rows.swapaxes(0, 1).reshape(-1, model),
        ]
        rows_of = jnp.concatenate(rows_of, axis=0)
        total = jnp.concatenate([a.astype(B16) for a in products + (rows_of.T,)], axis=1)
        total = scatter_sum(total.reshape(size, share, -1))
        ends = [hidden_units, 2 * hidden_units] + [2 * hidden_units + i * width for i in range(1, 5)]
        down_done, up_done, query_done, key_done, value_done, output_done, vectors_done = jnp.split(
            total, ends, axis=1
        )
        vectors_done = vectors_done.T
    latent_query_done, latent_key_done, latent_value_done, latent_output_done = at["latent_grads"]
    return (
        at["result", groups - 1],
        at["mixed_latents"],
        at["token_grad"],
        at["latent_grad"],
        latent_query_done,
        latent_key_done,
        latent_value_done,
        latent_output_done.T,
        query_done,
        key_done,
        value_done,
        output_done.T,
        up_done,
        vectors_done[3 : 3 + hidden_units // model].reshape(-1),
        down_done.T,
        vectors_done[0],
        at["latent_gain_sum"][0],
        vectors_done[2],
        vectors_done[1],
    )


def solution(mesh):
    placed = (
        P("dp", None),
        P("dp", None),
        P(None, "tp"),
        P(None, "tp"),
        P(None, "tp"),
        P("tp", None),
        P(None, "tp"),
        P(None, "tp"),
        P(None, "tp"),
        P("tp", None),
        P(None, "tp"),
        P("tp"),
        P("tp", None),
        P(),
        P(),
        P(),
        P(),
        P(),
        P("dp", None),
        P("dp", None),
    )
    return jax.shard_map(
        local,
        mesh=mesh,
        in_specs=placed,
        out_specs=(
            P("dp", None),
            P("dp", None),
            P("dp", None),
            P("dp", None),
            P("dp", "tp"),
            P("dp", "tp"),
            P("dp", "tp"),
            P("tp", "dp"),
            P("dp", "tp"),
            P("dp", "tp"),
            P("dp", "tp"),
            P("tp", "dp"),
            P("dp", "tp"),
            P(("tp", "dp")),
            P("tp", "dp"),
            P("dp"),
            P("dp"),
            P("dp"),
            P("dp"),
        ),
        check_vma=False,
    )
```

```python
from functools import partial

import jax
import jax.numpy as jnp
from jax import lax
from jax.experimental import pallas as pl
from jax.experimental.pallas import tpu as pltpu
from jax.sharding import PartitionSpec as P

E = 64
S = 256
L = 8
EPSILON = 1e-05
NEGATIVE = -1000000000.0
FACTOR = E ** (-0.5)
LOG2E = 1.4426950408889634
F32 = jnp.float32
B16 = jnp.bfloat16


def nn(left, right):
    return lax.dot_general(left, right, (((1,), (0,)), ((), ())), preferred_element_type=F32)


def nt(left, right):
    return lax.dot_general(left, right, (((1,), (1,)), ((), ())), preferred_element_type=F32)


def tn(left, right):
    return lax.dot_general(left, right, (((0,), (0,)), ((), ())), preferred_element_type=F32)


def norm_parts(values):
    average = jnp.mean(values, axis=-1, keepdims=True)
    centred = values - average
    spread = jnp.mean(centred * centred, axis=-1, keepdims=True)
    rate = lax.rsqrt(spread + EPSILON)
    return centred * rate, rate


def norm_back(grad, unit, rate, gain):
    scaled = grad * gain
    first = jnp.mean(scaled, axis=-1, keepdims=True)
    second = jnp.mean(scaled * unit, axis=-1, keepdims=True)
    return rate * (scaled - first - unit * second)


def gelu_both(values):
    square = values * values
    wave = jnp.tanh(0.7978845608028654 * values * (1.0 + 0.044715 * square))
    slope = 0.7978845608028654 * (1.0 + 0.134145 * square)
    half = 0.5 * (1.0 + wave)
    return values * half, half + 0.5 * values * (1.0 - wave * wave) * slope


def head_mask(heads, rows, width):
    row = lax.broadcasted_iota(jnp.int32, (heads * rows, width), 0)
    column = lax.broadcasted_iota(jnp.int32, (heads * rows, width), 1)
    return (row // rows) == (column // E)


def spread_heads(values, heads):
    rows, width = values.shape
    stacked = jnp.concatenate([values] * heads, axis=0)
    return jnp.where(head_mask(heads, rows, width), stacked, jnp.zeros_like(stacked))


def fold_heads(values, heads):
    rows, width = values.shape[0] // heads, values.shape[1]
    kept = jnp.where(head_mask(heads, rows, width), values, jnp.zeros_like(values))
    total = kept[:rows]
    for h in range(1, heads):
        total = total + kept[h * rows : (h + 1) * rows]
    return total


def half_mask(width):
    return lax.broadcasted_iota(jnp.int32, (1, width), 1) < E


def head_only(values, second):
    mask = half_mask(values.shape[1])
    zero = jnp.zeros_like(values)
    return jnp.where(mask, zero, values) if second else jnp.where(mask, values, zero)


def load_kernel(*refs):
    count = (len(refs) - 1) // 2
    ready = refs[-1]
    copies = [
        pltpu.make_async_copy(refs[i], refs[count + i], ready.at[i]) for i in range(count)
    ]
    for copy in copies:
        copy.start()
    for copy in copies:
        copy.wait()


def join_kernel(*refs):
    at = 0
    for r in refs[:-1]:
        refs[-1][at : at + r.shape[0], :] = r[...]
        at += r.shape[0]


def enter_kernel(g, tokens, gain, wq, wk, wv, saved_out):
    unit, _ = norm_parts(tokens[g * S : (g + 1) * S, :].astype(F32))
    low = (unit * gain[...].reshape(1, -1)).astype(B16)
    width = wq.shape[1]
    saved_out[:, :width] = nn(low, wq[...]).astype(B16)
    saved_out[:, width : 2 * width] = nn(low, wk[...]).astype(B16)
    saved_out[:, 2 * width : 3 * width] = nn(low, wv[...]).astype(B16)
    saved_out[:, 3 * width :] = low


def image_rows(order, groups, me, group_image):
    count = len(order) * groups * L
    lane = lax.broadcasted_iota(jnp.int32, (8, count), 1) // L
    images = jnp.zeros((8, count), F32)
    for j, bits in enumerate(order):
        for g in range(groups):
            image = group_image[(me ^ bits) * groups + g].astype(F32)
            images = jnp.where(lane == j * groups + g, image, images)
    return images[:1], images.T[:, :1]


def latent_kernel(
    heads, own, order, me, group_image, one, two, gain, wq, wk, wv, wo, latents_out, q_out, k_out, v_out, part_out
):
    latents = jnp.concatenate([one[...], two[...]], axis=0)
    latents_out[...] = latents
    unit, _ = norm_parts(latents.astype(F32))
    low = (unit * gain[...].reshape(1, -1)).astype(B16)
    q = nn(low, wq[...]).astype(B16)
    k = nn(low, wk[...]).astype(B16)
    v = nn(low, wv[...]).astype(B16)
    q_out[...] = q
    k_out[...] = k
    v_out[...] = v
    scores = nt(spread_heads(q[:own], heads), k) * FACTOR
    images, column = image_rows(order, own // L, me[0], group_image)
    member = jnp.concatenate([column[:own]] * heads, axis=0) == images
    scores = jnp.where(member, scores, NEGATIVE)
    weights = jnp.exp(scores - jnp.max(scores, axis=-1, keepdims=True))
    probs = weights / jnp.sum(weights, axis=-1, keepdims=True)
    mixed = fold_heads(nn(probs.astype(B16), v), heads).astype(B16)
    part_out[...] = nn(mixed, wo[...]).astype(B16)


def pair_of(saved, pair, width):
    start = pair * 2 * E
    return [saved[:, i * width + start : i * width + start + 2 * E] for i in range(3)]


def attend_kernel(
    g, heads, saved, latents, part_one, part_two, gain, wk, wv,
    o_out, probs_out, side_out, mid_out, mid_low_out,
):
    mid = latents[...].astype(F32) + (part_one[...].astype(F32) + part_two[...].astype(F32))
    mid_out[...] = mid
    mid_low_out[...] = mid.astype(B16)
    unit, _ = norm_parts(mid[g * L : (g + 1) * L])
    side_low = (unit * gain[...].reshape(1, -1)).astype(B16)
    side_k = nn(side_low, wk[...]).astype(B16).astype(F32)
    side_v = nn(side_low, wv[...]).astype(B16).astype(F32)
    width = side_k.shape[1]
    side_out[:, :width] = side_k
    side_out[:, width : 2 * width] = side_v
    side_out[:, 2 * width :] = side_low.astype(F32)
    side_v = spread_heads(side_v, heads).astype(B16)
    side_scores = nt(spread_heads(side_k, heads).astype(B16), saved[:, :width])
    scale = FACTOR * LOG2E
    outs, side_probs, lses = [], [], []
    for pair in range(heads // 2):
        q_pair, k_pair, v_pair = pair_of(saved, pair, width)
        for second in (0, 1):
            h = 2 * pair + second
            scores = nt(head_only(k_pair, second), q_pair)
            side = side_scores[h * L : (h + 1) * L]
            top = jnp.maximum(
                jnp.max(scores, axis=0, keepdims=True), jnp.max(side, axis=0, keepdims=True)
            )
            weights = jnp.exp2((scores - top) * scale)
            side = jnp.exp2((side - top) * scale)
            total = jnp.sum(weights, axis=0, keepdims=True) + jnp.sum(side, axis=0, keepdims=True)
            inverse = 1.0 / total
            side_probs.append(side * inverse)
            lses.append(top * scale + jnp.log2(total))
            outs.append(tn((weights * inverse).astype(B16), v_pair))
    side_probs = jnp.concatenate(side_probs, axis=0)
    probs_out[: heads * L, :] = side_probs
    probs_out[heads * L :, :] = jnp.concatenate(
        lses + [jnp.zeros_like(lses[0])] * (8 - heads), axis=0
    )
    side_o = tn(side_probs.astype(B16), side_v)
    first = half_mask(2 * E)
    token_o = jnp.concatenate(
        [jnp.where(first, outs[2 * i], outs[2 * i + 1]) for i in range(heads // 2)], axis=1
    )
    o_out[...] = (token_o + side_o).astype(B16)


def feed_kernel(
    g, chunk, place, tokens, o, o_two, wo, wo_two, cotangent, gain, up, up_bias, down, *rest
):
    part_outs, outs = rest[:-7], rest[-7:]
    active_out, hidden_grad_out, low_out, middle_out, down_part_out, up_bias_out, down_bias_out = outs
    rows = slice(g * S, (g + 1) * S)
    first = place[0] == 0
    o_first = jnp.where(first, o[...], o_two[...])
    o_second = jnp.where(first, o_two[...], o[...])
    wo_first = jnp.where(first, wo[...], wo_two[...])
    wo_second = jnp.where(first, wo_two[...], wo[...])
    middle = tokens[rows, :].astype(F32) + (nn(o_first, wo_first) + nn(o_second, wo_second))
    middle_out[...] = middle
    unit, _ = norm_parts(middle)
    low = (unit * gain[...].reshape(1, -1)).astype(B16)
    low_out[...] = low
    outer = cotangent[rows, :]
    down_bias_out[...] = jnp.sum(outer.astype(F32), axis=0, keepdims=True)
    part, down_part = None, None
    for start in range(0, up.shape[1], chunk):
        cut = slice(start, start + chunk)
        hidden = nn(low, up[:, cut]) + up_bias[cut].reshape(1, -1)
        active, slope = gelu_both(hidden)
        active = active.astype(B16)
        active_out[:, cut] = active
        grad = (slope * nt(outer, down[cut, :])).astype(B16)
        hidden_grad_out[:, cut] = grad
        up_bias_out[:, cut] = jnp.sum(grad.astype(F32), axis=0, keepdims=True)
        one = nt(grad, up[:, cut])
        two = nn(active, down[cut, :])
        part = one if part is None else part + one
        down_part = two if down_part is None else down_part + two
    at = 0
    for out in part_outs:
        out[...] = part[at : at + out.shape[0]].astype(B16)
        at += out.shape[0]
    down_part_out[...] = down_part.astype(B16)


def turn_kernel(
    g, heads, cuts, last, cotangent, middle, gain, wo, wk, wv, o, saved, probs, side, mid, *rest
):
    parts, rest = rest[: 2 * cuts], rest[2 * cuts :]
    earlier, outs = rest[:-8], rest[-8:]
    o_grad_out, delta_out, side_score_grad_out, part_out, grads_out, gain_out = outs[:6]
    middle_grad_out, middle_low_out = outs[6:]
    unit, rate = norm_parts(middle[...])
    sides = [jnp.concatenate([r[...] for r in rs], axis=0) for rs in (parts[:cuts], parts[cuts:])]
    grad = sides[0].astype(F32) + sides[1].astype(F32)
    gain_out[0:1, :] = jnp.sum(grad * unit, axis=0, keepdims=True)
    outer = cotangent[g * S : (g + 1) * S, :].astype(F32)
    middle_grad = outer + norm_back(grad, unit, rate, gain[...].reshape(1, -1))
    middle_grad_out[...] = middle_grad
    middle_low = middle_grad.astype(B16)
    middle_low_out[...] = middle_low
    o_grad = nt(middle_low, wo[...]).astype(B16)
    o_grad_out[...] = o_grad
    width = o_grad.shape[1]
    rows8 = lax.broadcasted_iota(jnp.int32, (8, width), 0)
    columns8 = lax.broadcasted_iota(jnp.int32, (8, width), 1) // E
    pick = (rows8 == columns8).astype(B16)
    weighted = o_grad.astype(F32) * o[...].astype(F32)
    high = weighted.astype(B16)
    low = (weighted - high.astype(F32)).astype(B16)
    delta = nt(pick, high) + nt(pick, low)
    delta_out[...] = delta
    side_v = spread_heads(side[:, width : 2 * width], heads).astype(B16)
    side_prob_grad = nt(side_v, o_grad)
    side_probs = probs[: heads * L, :]
    wide = jnp.concatenate(
        [jnp.broadcast_to(delta[h : h + 1], (L, delta.shape[1])) for h in range(heads)], axis=0
    )
    score_grad = (side_probs * (side_prob_grad - wide)).astype(B16)
    side_score_grad_out[...] = score_grad
    k_grad = (fold_heads(nn(score_grad, saved[:, :width]), heads) * FACTOR).astype(B16)
    v_grad = fold_heads(nn(side_probs.astype(B16), o_grad), heads).astype(B16)
    grads_out[:, :width] = k_grad.astype(F32)
    grads_out[:, width:] = v_grad.astype(F32)
    part = nt(k_grad, wk[...]) + nt(v_grad, wv[...])
    side_unit, _ = norm_parts(mid[g * L : (g + 1) * L, :])
    gain_out[1:2, :] = jnp.sum(part * side_unit, axis=0, keepdims=True)
    gain_out[2:, :] = jnp.zeros_like(gain_out[2:, :])
    if last:
        part = jnp.concatenate([r[...] for r in earlier] + [part], axis=0)
    part_out[...] = part.astype(part_out.dtype)


def side_kernel(part_one, part_two, mid, cotangent, gain, low_out, grad_out):
    unit, rate = norm_parts(mid[...])
    part = part_one[...].astype(F32) + part_two[...].astype(F32)
    grad = cotangent[...].astype(F32) + norm_back(part, unit, rate, gain[...].reshape(1, -1))
    grad_out[...] = grad
    low_out[...] = grad.astype(B16)


def attend_back_kernel(
    g, heads, tokens, saved, o_grad, probs, delta, side_score_grad, side, wq, wk, wv, *rest
):
    part_out, grads_out, gain_out = rest[-3:]
    gains, earlier = rest[: min(g, 1) + 1], rest[min(g, 1) + 1 : -3]
    scale = FACTOR * LOG2E
    first = half_mask(2 * E)
    width = o_grad.shape[1]
    side_k = spread_heads(side[:, :width], heads).astype(B16)
    side_q_grad = tn(side_score_grad[...], side_k)
    at = heads * L
    for pair in range(heads // 2):
        start = pair * 2 * E
        cut = slice(start, start + 2 * E)
        q_pair, k_pair, v_pair = pair_of(saved, pair, width)
        grad_pair = o_grad[:, cut]
        k_flat = k_pair.T
        q_grads, k_grads, v_grads = [], [], []
        for second in (0, 1):
            h = 2 * pair + second
            scores = nt(head_only(k_pair, second), q_pair)
            weights = jnp.exp2(scores * scale - probs[at + h : at + h + 1, :])
            prob_grad = nt(head_only(v_pair, second), grad_pair)
            score_grad = (weights * (prob_grad - delta[h : h + 1, :])).astype(B16)
            v_grads.append(nn(weights.astype(B16), grad_pair))
            k_grads.append(nn(score_grad, q_pair))
            q_grads.append(nn(k_flat[second * E : (second + 1) * E], score_grad))
        q_pair_grad = jnp.concatenate(q_grads, axis=0).T + side_q_grad[:, cut]
        k_pair_grad = jnp.where(first, k_grads[0], k_grads[1])
        v_pair_grad = jnp.where(first, v_grads[0], v_grads[1])
        grads_out[:, start : start + 2 * E] = (q_pair_grad * FACTOR).astype(B16)
        grads_out[:, width + start : width + start + 2 * E] = (k_pair_grad * FACTOR).astype(B16)
        grads_out[:, 2 * width + start : 2 * width + start + 2 * E] = v_pair_grad.astype(B16)
    part = nt(grads_out[:, :width], wq[...]) + nt(grads_out[:, width : 2 * width], wk[...])
    part = part + nt(grads_out[:, 2 * width :], wv[...])
    for i, r in enumerate(earlier):
        part_out[i * S : (i + 1) * S, :] = r[...]
    part_out[len(earlier) * S :, :] = part.astype(B16)
    unit, _ = norm_parts(tokens[g * S : (g + 1) * S, :].astype(F32))
    total = gains[0][1:2, :] + jnp.sum(part * unit, axis=0, keepdims=True)
    for r in gains[1:]:
        total = total + r[...]
    gain_out[...] = total


def leave_kernel(tokens, gain, part_one, part_two, *refs):
    middle_grad, grad_out = refs[:-1], refs[-1]
    for g in range(len(middle_grad)):
        rows = slice(g * S, (g + 1) * S)
        unit, rate = norm_parts(tokens[rows, :].astype(F32))
        grad = part_one[rows, :].astype(F32) + part_two[rows, :].astype(F32)
        grad_out[rows, :] = middle_grad[g][...] + norm_back(grad, unit, rate, gain[...].reshape(1, -1))


def result_kernel(middle, part_one, part_two, bias, *refs):
    earlier, out = refs[:-1], refs[-1]
    at = 0
    for r in earlier:
        out[at : at + S, :] = r[...]
        at += S
    total = part_one[...].astype(F32) + part_two[...].astype(F32)
    out[at:, :] = (middle[...] + total + bias[...].reshape(1, -1)).astype(B16)


def latent_leave_kernel(me, latents, part_one, part_two, gain, mid_grad, grad_out, gain_out):
    own = latents.shape[0]
    unit, rate = norm_parts(latents[...].astype(F32))
    start = part_one.shape[0] - own - 16
    total = part_one[start:, :].astype(F32) + part_two[start:, :].astype(F32)
    grad_out[...] = mid_grad[...] + norm_back(total[:own], unit, rate, gain[...].reshape(1, -1))
    share, model = gain_out.shape[0], gain.shape[0]
    row = lax.broadcasted_iota(jnp.int32, (share, model), 0)
    column = lax.broadcasted_iota(jnp.int32, (share, model), 1)
    kept = jnp.where(column == row + me[0] * share, total[own : own + 1], 0.0)
    sums = jnp.broadcast_to(jnp.sum(kept, axis=1, keepdims=True), (share, 8))
    gain_out[...] = sums.T[:1].reshape(share)


def split_pairs(values, bit, share, send_out, keep_out):
    blocks = values.reshape(values.shape[0] // (2 * share), 2, share, values.shape[1])
    even, odd = blocks[:, 0], blocks[:, 1]
    send_out[...] = jnp.where(bit == 0, odd, even).astype(B16)
    keep_out[...] = jnp.where(bit == 0, even, odd).astype(B16)


def weight_grad_kernel(groups, share, pieces, me, cotangent, *refs):
    active, low, hidden_grad = (refs[i * groups : (i + 1) * groups] for i in range(3))
    outs = refs[3 * groups :]
    bit = me[0] % 2
    width = active[0].shape[1]
    at = 0
    for count, lefts, rights in (
        (pieces[0], [cotangent[g * S : (g + 1) * S, :].T for g in range(groups)], active),
        (pieces[1], [r[...].T for r in low], hidden_grad),
    ):
        chunk = width // count
        for k in range(count):
            cut = slice(k * chunk, (k + 1) * chunk)
            total = nn(lefts[0], rights[0][:, cut])
            for g in range(1, groups):
                total = total + nn(lefts[g], rights[g][:, cut])
            split_pairs(total, bit, share, outs[at], outs[at + 1])
            at += 2


def attention_grad_kernel(groups, share, me, *refs):
    saved, grads, middle_low, o, side, side_grads = (
        refs[i * groups : (i + 1) * groups] for i in range(6)
    )
    outs = refs[6 * groups :]
    bit = me[0] % 2
    width = o[0].shape[1]
    stack = [jnp.concatenate([r[...] for r in rs], axis=0) for rs in (side, side_grads)]
    side_low = stack[0][:, 2 * width :].astype(B16)
    side_k, side_v = stack[1][:, :width].astype(B16), stack[1][:, width:].astype(B16)
    flat = [r[:, 3 * width :].T for r in saved]
    low_flat = [r[...].T for r in middle_low]

    def total_of(lefts, rights, cut):
        total = nn(lefts[0], rights[0][:, cut])
        for g in range(1, groups):
            total = total + nn(lefts[g], rights[g][:, cut])
        return total

    def cut_of(i):
        return slice(i * width, (i + 1) * width)

    totals = (
        total_of(flat, grads, cut_of(0)),
        total_of(flat, grads, cut_of(1)) + tn(side_low, side_k),
        total_of(flat, grads, cut_of(2)) + tn(side_low, side_v),
        total_of(low_flat, o, cut_of(0)),
    )
    for i, total in enumerate(totals):
        split_pairs(total, bit, share, outs[2 * i], outs[2 * i + 1])


def sum_of(parts):
    total = parts[0]
    for part in parts[1:]:
        total = total + part
    return total


def vector_kernel(groups, share, me, one, two, *refs):
    up_bias, down_bias, gains = (refs[i * groups : (i + 1) * groups] for i in range(3))
    send_out, keep_out = refs[3 * groups :]
    model = one.shape[1]
    gain = one[...] + two[...]

    def column(rows):
        return jnp.broadcast_to(rows, (8, rows.shape[1])).T

    columns = [
        column(sum_of([r[...] for r in down_bias])),
        column(sum_of([r[0:1, :] for r in gains])),
        column(gain),
    ]
    bias = column(sum_of([r[...] for r in up_bias]))
    times = bias.shape[0] // model
    bias = bias.reshape(model // share, times, share, 8)
    columns += [bias[:, i].reshape(model, 8) for i in range(times)]
    lane = lax.broadcasted_iota(jnp.int32, (model, 128), 1)
    block = jnp.zeros((model, 128), F32)
    for i, one in enumerate(columns):
        block = jnp.where(lane == i, one[:, 0:1], block)
    split_pairs(block, me[0] % 2, share, send_out, keep_out)


def halve_kernel(shift, pieces, cuts, me, *refs):
    count = len(pieces)
    keeps, gots, outs = refs[:count], refs[count : 2 * count], refs[2 * count :]
    bit = (me[0] // shift) % 2
    for keep, got, (first, last) in zip(keeps, gots, pieces):
        for k, (start, end) in enumerate(cuts):
            low, high = max(first, start), min(last, end)
            if low >= high:
                continue
            of_piece, of_out = slice(low - first, high - first), slice(low - start, high - start)
            for i in range(keep.shape[0]):
                there, here = (
                    keep[i, pl.ds(at, 1), :, of_piece].astype(F32)
                    + got[i, pl.ds(at, 1), :, of_piece].astype(F32)
                    for at in (1 - bit, bit)
                )
                outs[2 * k][pl.ds(i, 1), :, of_out] = there.astype(B16)
                outs[2 * k + 1][pl.ds(i, 1), :, of_out] = here


def finish_kernel(cuts, keep, got, *outs):
    total = keep[0] + got[0].astype(F32)
    for out, (start, end, flat) in zip(outs, cuts):
        part = total[:, start:end]
        if flat:
            rows = part.T
            share = rows.shape[1]
            for i in range(out.shape[0] // share):
                out[i * share : (i + 1) * share] = rows[i : i + 1, :].reshape(share)
        else:
            out[...] = part


def latent_back_kernel(
    heads, own, order, block, me, group_image, token_part, latents, q, k, v, mid_one, mid_two, gain, wq, wk, wv, wo,
    part_out, wq_out, wk_out, wv_out, wo_out, mixed, q_grad, k_grad, v_grad, images,
):
    mid_low = jnp.concatenate([mid_one[...], mid_two[...]], axis=0)
    o_grad = nt(mid_low, wo[...]).astype(B16)
    unit, _ = norm_parts(latents[...].astype(F32))
    low = (unit * gain[...].reshape(1, -1)).astype(B16)
    everyone = low.shape[0]
    images_row, images_column = image_rows(order, own // L, me[0], group_image)

    def rows_of(start, ref_q, ref_grad, ref_images):
        wide_q = spread_heads(ref_q, heads)
        wide_grad = spread_heads(ref_grad, heads)
        scores = nt(wide_q, k[...]) * FACTOR
        member = jnp.concatenate([ref_images] * heads, axis=0) == images_row
        scores = jnp.where(member, scores, NEGATIVE)
        weights = jnp.exp(scores - jnp.max(scores, axis=-1, keepdims=True))
        probs = weights / jnp.sum(weights, axis=-1, keepdims=True)
        probs_low = probs.astype(B16)
        prob_grad = nt(wide_grad, v[...])
        delta = jnp.sum(prob_grad * probs, axis=-1, keepdims=True)
        score_grad = (probs * (prob_grad - delta)).astype(B16)
        mixed[pl.ds(start, block), :] = fold_heads(nn(probs_low, v[...]), heads).astype(B16)
        q_grad[pl.ds(start, block), :] = (
            fold_heads(nn(score_grad, k[...]), heads) * FACTOR
        ).astype(B16)
        return tn(score_grad, wide_q), tn(probs_low, wide_grad)

    if block == everyone:
        k_sum, v_sum = rows_of(0, q[...], o_grad, images_column)
        k_sum, v_sum = k_sum * FACTOR, v_sum
    else:
        v_grad[...] = o_grad
        images[...] = jnp.broadcast_to(images_column, images.shape)

        def step(i, held):
            start = pl.multiple_of(i * block, block)
            here = pl.ds(start, block)
            one, two = rows_of(start, q[here, :], v_grad[here, :], images[here, :][:, :1])
            return held[0] + one, held[1] + two

        zero = jnp.zeros(k.shape, F32)
        k_sum, v_sum = lax.fori_loop(0, everyone // block, step, (zero, zero))
        k_sum = k_sum * FACTOR
    k_grad[...] = k_sum.astype(B16)
    v_grad[...] = v_sum.astype(B16)
    part = nt(q_grad[...], wq[...]) + nt(k_grad[...], wk[...]) + nt(v_grad[...], wv[...])
    gain_part = jnp.sum(part * unit, axis=0, keepdims=True)
    rows = token_part.shape[0]
    part_out[:rows, :] = token_part[...]
    part_out[rows:, :] = jnp.concatenate(
        [part[:own], jnp.broadcast_to(gain_part, (16, part.shape[1]))], axis=0
    ).astype(B16)
    share = wq_out.shape[0]
    model = low.shape[1]
    row = lax.broadcasted_iota(jnp.int32, (share, model), 0)
    column = lax.broadcasted_iota(jnp.int32, (share, model), 1)
    pick = (column == row + me[0] * share).astype(B16)
    columns = nt(pick, low).astype(B16)
    wq_out[...] = nn(columns, q_grad[...])
    wk_out[...] = nn(columns, k_grad[...])
    wv_out[...] = nn(columns, v_grad[...])
    wo_out[...] = nn(nt(pick, mid_low).astype(B16), mixed[...])


MIB = 1024 * 1024
OUT = "out"


class Order:
    def __init__(self, pinned):
        self.pinned, self.last = pinned, None

    def call(self, kernel, name, outs, ins, scratch=(), limit=16, behind=(), loose=False):
        scalars = [isinstance(a, tuple) for a in ins]
        arrays = [a[1] if isinstance(a, tuple) else a for a in ins]
        earlier = tuple(behind) + (() if self.last is None or loose else (self.last,))
        if earlier:
            least = min(range(len(arrays)), key=lambda i: arrays[i].size)
            arrays[least] = after(arrays[least], *earlier)
        if self.pinned:
            arrays = [
                a if scalar else pltpu.with_memory_space_constraint(a, pltpu.VMEM)
                for a, scalar in zip(arrays, scalars)
            ]

        def result(shape, dtype, kind=None):
            if self.pinned and kind != OUT:
                return pltpu.VMEM(shape, dtype)
            return jax.ShapeDtypeStruct(shape, dtype)

        def whole(shape):
            return pl.BlockSpec(tuple(shape), lambda: (0,) * len(shape))

        results = pl.pallas_call(
            kernel,
            out_shape=[result(*out) for out in outs],
            in_specs=[
                pl.BlockSpec(memory_space=pltpu.SMEM) if scalar else whole(a.shape)
                for a, scalar in zip(arrays, scalars)
            ],
            out_specs=[whole(out[0]) for out in outs],
            scratch_shapes=list(scratch),
            compiler_params=pltpu.CompilerParams(vmem_limit_bytes=limit * MIB),
            cost_estimate=pl.CostEstimate(flops=0, bytes_accessed=0, transcendentals=0),
            name=name,
        )(*arrays)
        if not loose:
            self.last = min(results, key=lambda a: a.size)
        return results

    def load(self, *arrays, behind=()):
        if not self.pinned:
            return arrays
        sources = list(arrays)
        earlier = tuple(behind) + (() if self.last is None else (self.last,))
        if earlier:
            sources[0] = after(sources[0], *earlier)
        results = pl.pallas_call(
            load_kernel,
            out_shape=[pltpu.VMEM(a.shape, a.dtype) for a in arrays],
            in_specs=[pl.BlockSpec(memory_space=pltpu.HBM)] * len(arrays),
            out_specs=[pl.BlockSpec(memory_space=pltpu.VMEM)] * len(arrays),
            scratch_shapes=[pltpu.SemaphoreType.DMA((len(arrays),))],
            compiler_params=pltpu.CompilerParams(vmem_limit_bytes=MIB),
            cost_estimate=pl.CostEstimate(flops=0, bytes_accessed=0, transcendentals=0),
            name="load",
        )(*[pltpu.with_memory_space_constraint(a, pltpu.HBM) for a in sources])
        self.last = min(results, key=lambda a: a.size)
        return results


def after(value, *earlier):
    return lax.optimization_barrier((value, earlier))[0]


def swap_tp(values, name):
    with jax.named_scope("swap_" + name):
        return lax.ppermute(values, "tp", [(0, 1), (1, 0)])


def flip(values, bits, name):
    size = lax.axis_size("dp")
    with jax.named_scope("flip_" + name):
        return lax.ppermute(values, "dp", [(i, i ^ bits) for i in range(size)])


def gather_steps(size):
    width, steps = 2, []
    while width * 4 < size:
        steps.append([width])
        width *= 2
    if width < size:
        steps.append([width * k for k in range(1, size // width)])
    steps.reverse()
    return steps + [[1]]


def one_by_one(steps):
    result = []
    for step in steps:
        result += [[b] for b in step if b & (b - 1) == 0]
    return result


def gather_order(size):
    order = [0]
    for step in gather_steps(size):
        order = order + [i ^ bits for bits in [0] + step for i in order][len(order) :]
    return order


def scatter_sum(grads):
    size = lax.axis_size("dp")
    me = lax.axis_index("dp")
    width = 1
    while width * 4 < size:
        bit = (me // width) % 2
        pairs = grads.reshape((grads.shape[0] // 2, 2) + grads.shape[1:])
        send = lax.dynamic_index_in_dim(pairs, 1 - bit, 1, keepdims=False)
        keep = lax.dynamic_index_in_dim(pairs, bit, 1, keepdims=False)
        got = flip(send.astype(B16), width, "sums")
        grads = keep.astype(F32) + got.astype(F32)
        width *= 2
    place = me // width
    total = lax.dynamic_index_in_dim(grads, place, 0, keepdims=False)
    for k in range(1, size // width):
        send = lax.dynamic_index_in_dim(grads, place ^ k, 0, keepdims=False)
        total = total + flip(send.astype(B16), width * k, "sums").astype(F32)
    return total


class Scatter:
    def __init__(self, order, me, width, keeps, sends, name):
        self.order, self.me, self.width, self.keeps = order, me, width, list(keeps)
        self.gots = [flip(a, width, name) for a in sends]
        self.pieces, self.columns = [], 0
        for a in self.keeps:
            self.pieces.append((self.columns, self.columns + a.shape[2]))
            self.columns += a.shape[2]

    def halve(self, cuts=None, behind=()):
        cuts = [(0, self.columns)] if cuts is None else cuts
        n, share, _ = self.keeps[0].shape
        shapes = [(n // 2, share, end - start) for start, end in cuts]
        results = self.order.call(
            partial(halve_kernel, 2 * self.width, self.pieces, cuts),
            "halve",
            [out for shape in shapes for out in ((shape, B16), (shape, F32))],
            [("smem", self.me)]
            + [a.reshape((n // 2, 2) + a.shape[1:]) for a in self.keeps + self.gots],
            behind=behind,
        )
        return results[::2], results[1::2]

    def next(self, name, *ties):
        (send,), (keep,) = self.halve()
        send = after(send, *ties) if ties else send
        return Scatter(self.order, self.me, 2 * self.width, [keep], [send], name)

    def finish(self, cuts):
        share = self.keeps[0].shape[1]
        shapes = [(flat * share,) if flat else (share, e - s) for s, e, flat in cuts]
        return self.order.call(
            partial(finish_kernel, cuts),
            "finish",
            [(shape, F32, OUT) for shape in shapes],
            self.keeps + self.gots,
        )


ORDER = (
    "load_small",
    "gather_0",
    "load_first",
    "enter_0",
    "gather_1",
    "enter_1",
    "latent",
    "load_feed",
    "attend_0",
    "attend_1",
    "feed_0",
    "feed_1",
    "weight_grad",
    "turn_0",
    "down_y",
    "turn_1",
    "back_0",
    "result_0",
    "side",
    "back_1",
    "gather_mid_0",
    "attention_grad",
    "gather_mid_1",
    "vectors",
    "gather_mid_2",
    "up_y",
    "down_z",
    "first_y",
    "second_y",
    "latent_back",
    "down_zz",
    "up_z",
    "first_z",
    "up_zz",
    "down_done",
    "up_done",
    "first_zz",
    "second_z",
    "leave",
    "result_1",
    "latent_leave",
    "first_done",
    "second_zz",
    "second_done",
)
SUMS = (
    "weight_grad",
    "down_y",
    "attention_grad",
    "vectors",
    "up_y",
    "down_z",
    "first_y",
    "second_y",
    "down_zz",
    "up_z",
    "first_z",
    "up_zz",
    "down_done",
    "first_zz",
    "up_done",
    "second_z",
    "second_zz",
    "first_done",
    "second_done",
)
PIECES = (4, 2)
TIE_UP = True
TIE_DOWN_0 = "feed"
TIE_DOWN_1 = "gain"
MID_DIRECT = False
FEED_CHUNKS = 3


def local(
    tokens,
    latents,
    latent_query,
    latent_key,
    latent_value,
    latent_output,
    query_weight,
    key_weight,
    value_weight,
    output_weight,
    up_weight,
    up_bias,
    down_weight,
    down_bias,
    latent_gain,
    attention_gain,
    feed_gain,
    group_image,
    token_cotangent,
    latent_cotangent,
):
    size = lax.axis_size("dp")
    me = lax.axis_index("dp")
    me_row = me.reshape(1)
    place = lax.axis_index("tp").reshape(1)
    width = latent_query.shape[1]
    heads = width // E
    rows, model = tokens.shape
    hidden_units = up_weight.shape[1]
    groups = rows // S
    own = latents.shape[0]
    everyone = own * size
    share = model // size
    small = everyone <= 512
    aligned = share % 16 == 0 and size >= 8
    each = range(groups)
    scalars = (me_row, place)
    chain = Order(small)
    call = chain.call
    latent_limit = 16 if small else 56
    gathered = gather_steps(size)
    turns = tuple(gather_order(size))

    def join(parts):
        if not small:
            return jnp.concatenate(parts, axis=0)
        shape = (sum(p.shape[0] for p in parts), model)
        return call(join_kernel, "join", [(shape, B16)], parts)[0]

    at = {}
    output_weight_two = swap_tp(output_weight, "output_weight")

    def load_small():
        at["latents_held"] = latents
        names = ("latents", "latent_cotangent", "latent_gain", "attention_gain", "feed_gain")
        values = chain.load(
            latents,
            latent_cotangent,
            latent_gain,
            attention_gain,
            feed_gain,
            up_bias,
            down_bias,
            behind=scalars,
        )
        for name, value in zip(names + ("up_bias_row", "down_bias_row"), values):
            at[name] = value

    def gather(name, steps, first):
        held = at[name]
        others = [flip(held, bits, name) for bits in steps]
        at[name] = join([at["latents"] if first else held] + others)

    def load_all():
        at["tokens"], *weights = chain.load(
            tokens,
            query_weight,
            key_weight,
            value_weight,
            output_weight,
            latent_query,
            latent_key,
            latent_value,
            latent_output,
        )
        at["group_weights"], at["output_weight"], at["latent_weights"] = (
            weights[:3],
            weights[3],
            weights[4:],
        )

    def enter(g):
        (at["saved", g],) = call(
            partial(enter_kernel, g),
            "enter",
            [((S, 3 * width + model), B16)],
            [at["tokens"], at["attention_gain"], *at["group_weights"]],
        )

    def latent():
        held = at["latents_held"]
        at["latents_all"], *at["latent_qkv"], at["latent_part"] = call(
            partial(latent_kernel, heads, own, turns),
            "latent",
            [((everyone, model), B16)] + [((everyone, width), B16)] * 3 + [((own, model), B16)],
            [
                ("smem", me_row),
                ("smem", group_image),
                held,
                flip(held, 1, "latents_held"),
                at["latent_gain"],
                *at["latent_weights"],
            ],
            limit=latent_limit,
        )
        at["latent_part_two"] = swap_tp(at["latent_part"], "latent_part")

    def load_feed():
        at["up_weight"], at["down_weight"], at["cotangent"] = chain.load(
            up_weight, down_weight, token_cotangent
        )

    def attend(g):
        at["o", g], at["probs", g], at["side", g], mid, mid_low = call(
            partial(attend_kernel, g, heads),
            "attend",
            [
                ((S, width), B16),
                ((heads * L + 8, S), F32),
                ((L, 2 * width + model), F32),
                ((own, model), F32),
                ((own, model), B16, OUT),
            ],
            [
                at["saved", g],
                at["latents"],
                at["latent_part"],
                at["latent_part_two"],
                at["attention_gain"],
                *at["group_weights"][1:],
            ],
        )
        if g == 0:
            at["mid"], at["mixed_latents"] = mid, mid_low
        at["o_two", g] = swap_tp(at["o", g], "o")

    def feed(g):
        count = 1 if g == groups - 1 else 2
        results = call(
            partial(feed_kernel, g, hidden_units // FEED_CHUNKS),
            "feed",
            [((S // count, model), B16)] * count
            + [
                ((S, hidden_units), B16),
                ((S, hidden_units), B16),
                ((S, model), B16),
                ((S, model), F32),
                ((S, model), B16),
                ((1, hidden_units), F32),
                ((1, model), F32),
            ],
            [
                ("smem", place),
                at["tokens"],
                at["o", g],
                at["o_two", g],
                at["output_weight"],
                output_weight_two,
                at["cotangent"],
                at["feed_gain"],
                at["up_weight"],
                at["up_bias_row"],
                at["down_weight"],
            ],
        )
        at["feed_part", g] = results[:count]
        names = ("active", "hidden_grad", "feed_low", "middle", "down_part", "up_bias", "down_bias")
        for name, value in zip(names, results[count:]):
            at[name, g] = value
        at["feed_part_two", g] = [swap_tp(p, "feed_part") for p in results[:count]]

    def weight_grad():
        outs = []
        for count in PIECES:
            outs += [((size // 2, share, hidden_units // count), B16)] * (2 * count)
        halves = call(
            partial(weight_grad_kernel, groups, share, PIECES),
            "weight_grad",
            outs,
            [("smem", me_row), at["cotangent"]]
            + [at[name, g] for name in ("active", "feed_low", "hidden_grad") for g in each],
        )
        at["down_halves"], at["up_halves"] = halves[: 2 * PIECES[0]], halves[2 * PIECES[0] :]

    def turn(g):
        last = g == groups - 1
        names = (
            "o_grad",
            "delta",
            "side_score_grad",
            "side_part",
            "side_grads",
            "gains",
            "middle_grad",
            "middle_low",
        )
        results = call(
            partial(turn_kernel, g, heads, len(at["feed_part", g]), last),
            "turn",
            [
                ((S, width), B16),
                ((8, S), F32),
                ((heads * L, S), B16),
                ((own if last else L, model), B16 if last else F32),
                ((L, 2 * width), F32),
                ((8, model), F32),
                ((S, model), F32),
                ((S, model), B16),
            ],
            [
                at["cotangent"],
                at["middle", g],
                at["feed_gain"],
                at["output_weight"],
                *at["group_weights"][1:],
                at["o", g],
                at["saved", g],
                at["probs", g],
                at["side", g],
                at["mid"],
                *at["feed_part", g],
                *at["feed_part_two", g],
                *[at["side_part", i] for i in range(g)],
            ],
        )
        for name, value in zip(names, results):
            at[name, g] = value
        if last:
            at["side_part_two"] = swap_tp(at["side_part", g], "side_part")
            if aligned:
                sends = [after(a, at["delta", g]) for a in at["up_halves"][::2]]
                at["up"] = Scatter(chain, me_row, 1, at["up_halves"][1::2], sends, "up_core")
        elif aligned and g == 0:
            sends = [after(a, at["delta", g]) for a in at["down_halves"][::2]]
            at["down"] = Scatter(chain, me_row, 1, at["down_halves"][1::2], sends, "down_core")
        if not last:
            tie = at["delta", 0] if TIE_DOWN_0 == "turn" else at["middle", groups - 1]
            at["down_part_two", g] = swap_tp(after(at["down_part", g], tie), "down_part")

    def back(g):
        last = g == groups - 1
        at["token_part", g], at["grads", g], at["gain"] = call(
            partial(attend_back_kernel, g, heads),
            "attend_back",
            [((rows if last else S, model), B16), ((S, 3 * width), B16), ((1, model), F32)],
            [
                at["tokens"],
                at["saved", g],
                at["o_grad", g],
                at["probs", g],
                at["delta", g],
                at["side_score_grad", g],
                at["side", g],
                *at["group_weights"],
                at["gains", g],
                *([at["gain"]] if g else []),
                *([at["token_part", i] for i in range(g)] if last else []),
            ],
        )
        if last:
            at["gain_two"] = swap_tp(at["gain"], "gain")
            tie = {"gain": "gain_two", "back": "gain", "side": "side_part_two"}[TIE_DOWN_1]
            at["down_part_two", g] = swap_tp(after(at["down_part", g], at[tie]), "down_part")

    def result(g):
        shape, kind = ((rows, model), (OUT,)) if g == groups - 1 else ((S, model), ())
        (at["result", g],) = call(
            result_kernel,
            "result",
            [(shape, B16) + kind],
            [
                at["middle", g],
                at["down_part", g],
                at["down_part_two", g],
                at["down_bias_row"],
                *[at["result", i] for i in range(g)],
            ],
        )

    def side():
        at["mid_held"], at["middle_latent_grad"] = call(
            side_kernel,
            "side",
            [((own, model), B16), ((own, model), F32)],
            [
                at["side_part", groups - 1],
                at["side_part_two"],
                at["mid"],
                at["latent_cotangent"],
                at["attention_gain"],
            ],
        )

    def attention_grad():
        names = ("saved", "grads", "middle_low", "o", "side", "side_grads")
        halves = call(
            partial(attention_grad_kernel, groups, share),
            "attention_grad",
            [((size // 2, share, width), B16)] * 8,
            [("smem", me_row)] + [at[name, g] for name in names for g in each],
        )
        at["first"] = Scatter(chain, me_row, 1, halves[1:4:2], halves[:4:2], "first_core")
        at["second_halves"] = halves[4:]

    def vectors():
        names = ("up_bias", "down_bias", "gains")
        at["vector_halves"] = call(
            partial(vector_kernel, groups, share),
            "vectors",
            [((size // 2, share, 128), B16)] * 2,
            [("smem", me_row), at["gain"], at["gain_two"]]
            + [at[name, g] for name in names for g in each],
        )

    def second_y():
        halves = at["second_halves"] + at["vector_halves"]
        at["second"] = Scatter(chain, me_row, 1, halves[1::2], halves[::2], "second_core")
        advance("second", "second_y")

    def advance(which, name, *ties):
        at[which] = at[which].next(name, *ties)

    def latent_back():
        held = at["mid_held"]
        block = min(everyone, max(16, 65536 // everyone))
        at["all_part"], *at["latent_grads"] = call(
            partial(latent_back_kernel, heads, own, turns, block),
            "latent_back",
            [((rows + own + 16, model), B16)] + [((share, width), F32, OUT)] * 4,
            [
                ("smem", me_row),
                ("smem", group_image),
                at["token_part", groups - 1],
                at["latents_all"],
                *at["latent_qkv"],
                held,
                flip(held, 1, "mid_held"),
                at["latent_gain"],
                *at["latent_weights"],
            ],
            scratch=[pltpu.VMEM((everyone, width), B16)] * 4 + [pltpu.VMEM((everyone, 128), F32)],
            limit=latent_limit,
        )
        at["all_part_two"] = swap_tp(at["all_part"], "all_part")

    def latent_leave():
        at["latent_grad"], at["latent_gain_sum"] = call(
            latent_leave_kernel,
            "latent_leave",
            [((own, model), F32, OUT), ((share,), F32, OUT)],
            [
                ("smem", me_row),
                at["latents"],
                at["all_part"],
                at["all_part_two"],
                at["latent_gain"],
                at["middle_latent_grad"],
            ],
        )

    def leave():
        (at["token_grad"],) = call(
            leave_kernel,
            "leave",
            [((rows, model), F32, OUT)],
            [at["tokens"], at["attention_gain"], at["all_part"], at["all_part_two"]]
            + [at["middle_grad", g] for g in each],
        )

    def done(which, *cuts):
        at[which, "done"] = at[which].finish(cuts)

    steps = {
        "load_small": load_small,
        "load_first": load_all,
        "latent": latent,
        "load_feed": load_feed,
        "weight_grad": weight_grad,
        "side": side,
        "attention_grad": attention_grad,
        "vectors": vectors,
        "second_y": second_y,
        "latent_back": latent_back,
        "latent_leave": latent_leave,
        "leave": leave,
        "down_done": partial(done, "down", (0, hidden_units, 0)),
        "up_done": partial(done, "up", (0, hidden_units, 0)),
        "first_done": partial(done, "first", (0, width, 0), (width, 2 * width, 0)),
        "second_done": partial(
            done,
            "second",
            (0, width, 0),
            (width, 2 * width, 0),
            (2 * width, 2 * width + 128, 1),
            (2 * width + 1, 2 * width + 128, 1),
            (2 * width + 2, 2 * width + 128, 1),
            (2 * width + 3, 2 * width + 128, hidden_units // model),
        ),
    }
    for name, which in (
        ("down_y", "down"),
        ("down_z", "down"),
        ("down_zz", "down"),
        ("up_z", "up"),
        ("up_zz", "up"),
        ("first_y", "first"),
        ("first_z", "first"),
        ("first_zz", "first"),
        ("second_z", "second"),
        ("second_zz", "second"),
    ):
        steps[name] = partial(advance, which, name)
    steps["up_y"] = lambda: advance("up", "up_y", *(at["down"].gots if TIE_UP else ()))
    for g in each:
        for name, step in (
            ("enter", enter),
            ("attend", attend),
            ("feed", feed),
            ("turn", turn),
            ("back", back),
            ("result", result),
        ):
            steps[f"{name}_{g}"] = partial(step, g)
    for i, bits in enumerate(gathered[:-1]):
        steps[f"gather_{i}"] = partial(gather, "latents_held", bits, i == 0)
    mid_steps = gathered[:-1] if MID_DIRECT else one_by_one(gathered[:-1])
    for i, bits in enumerate(mid_steps):
        steps[f"gather_mid_{i}"] = partial(gather, "mid_held", bits, 0)
    order = [name for name in ORDER if name in steps and (aligned or name not in SUMS)]
    for name in steps:
        if name not in order and (aligned or name not in SUMS):
            kind, _, number = name.rpartition("_")
            order.insert(order.index(f"{kind}_{int(number) - 1}") + 1, name)
    for name in order:
        steps[name]()
    if aligned:
        (down_done,), (up_done,) = at["down", "done"], at["up", "done"]
        query_done, key_done = at["first", "done"]
        value_done, output_done, *vectors_done = at["second", "done"]
    else:

        def flat(name, start, end):
            return jnp.concatenate([at[name, g][:, start:end] for g in each], axis=0).astype(B16)

        token_low = flat("saved", 3 * width, 3 * width + model)
        side_low = flat("side", 2 * width, 2 * width + model)
        products = (
            tn(token_cotangent, flat("active", 0, hidden_units)),
            tn(flat("feed_low", 0, model), flat("hidden_grad", 0, hidden_units)),
            tn(token_low, flat("grads", 0, width)),
            tn(token_low, flat("grads", width, 2 * width))
            + tn(side_low, flat("side_grads", 0, width)),
            tn(token_low, flat("grads", 2 * width, 3 * width))
            + tn(side_low, flat("side_grads", width, 2 * width)),
            tn(flat("middle_low", 0, model), flat("o", 0, width)),
        )
        bias_rows = sum(at["up_bias", g] for g in each).reshape(size, -1, share)
        rows_of = [
            sum(at["down_bias", g] for g in each),
            sum(at["gains", g] for g in each)[:1],
            at["gain"] + at["gain_two"],
            bias_rows.swapaxes(0, 1).reshape(-1, model),
        ]
        rows_of = jnp.concatenate(rows_of, axis=0)
        total = jnp.concatenate([a.astype(B16) for a in products + (rows_of.T,)], axis=1)
        total = scatter_sum(total.reshape(size, share, -1))
        ends = [hidden_units, 2 * hidden_units] + [2 * hidden_units + i * width for i in range(1, 5)]
        down_done, up_done, query_done, key_done, value_done, output_done, vectors_done = jnp.split(
            total, ends, axis=1
        )
        vectors_done = [*vectors_done.T[:3], vectors_done.T[3:].reshape(-1)]
    latent_query_done, latent_key_done, latent_value_done, latent_output_done = at["latent_grads"]
    return (
        at["result", groups - 1],
        at["mixed_latents"],
        at["token_grad"],
        at["latent_grad"],
        latent_query_done,
        latent_key_done,
        latent_value_done,
        latent_output_done.T,
        query_done,
        key_done,
        value_done,
        output_done.T,
        up_done,
        vectors_done[3],
        down_done.T,
        vectors_done[0],
        at["latent_gain_sum"],
        vectors_done[2],
        vectors_done[1],
    )


def solution(mesh):
    placed = (
        P("dp", None),
        P("dp", None),
        P(None, "tp"),
        P(None, "tp"),
        P(None, "tp"),
        P("tp", None),
        P(None, "tp"),
        P(None, "tp"),
        P(None, "tp"),
        P("tp", None),
        P(None, "tp"),
        P("tp"),
        P("tp", None),
        P(),
        P(),
        P(),
        P(),
        P(),
        P("dp", None),
        P("dp", None),
    )
    return jax.shard_map(
        local,
        mesh=mesh,
        in_specs=placed,
        out_specs=(
            P("dp", None),
            P("dp", None),
            P("dp", None),
            P("dp", None),
            P("dp", "tp"),
            P("dp", "tp"),
            P("dp", "tp"),
            P("tp", "dp"),
            P("dp", "tp"),
            P("dp", "tp"),
            P("dp", "tp"),
            P("tp", "dp"),
            P("dp", "tp"),
            P(("tp", "dp")),
            P("tp", "dp"),
            P("dp"),
            P("dp"),
            P("dp"),
            P("dp"),
        ),
        check_vma=False,
    )
```
